32 devices in a mesh: expert: 8 (over z, x), wshard: 4 (over y, core).
Axes of the slice: x: 2, y: 2, z: 4, core: 2. Of those that a mesh axis runs over, the one named last changes fastest.
Arguments:
- images: bfloat16 [256, 197, 512], P(('expert', 'wshard')), may hold values from -6 to 6
- cotangent: bfloat16 [256, 197, 512], P(('expert', 'wshard')), may hold values from -6 to 6
- image_count: int32 [32], P(('expert', 'wshard')), may hold values from 4 to 8, as said below
- routes: int32 [256, 197, 2], P(('expert', 'wshard')), may hold values from 0 to 7, all different within a row
- attn_norm_gain: bfloat16 [512], P('wshard'), may hold values from 0.5 to 1.5
- attn_norm_bias: bfloat16 [512], P('wshard'), may hold values from -1.25 to 1.25
- w_qkv: bfloat16 [512, 1536], P('wshard'), may hold values from -0.25 to 0.25
- b_query: bfloat16 [512], P('wshard'), may hold values from -1.25 to 1.25
- b_value: bfloat16 [512], P('wshard'), may hold values from -1.25 to 1.25
- w_attn_out: bfloat16 [512, 512], P('wshard'), may hold values from -1 to 1
- b_attn_out: bfloat16 [512], P('wshard'), may hold values from -1.25 to 1.25
- moe_norm_gain: bfloat16 [512], P('wshard'), may hold values from 0.5 to 1.5
- moe_norm_bias: bfloat16 [512], P('wshard'), may hold values from -1.25 to 1.25
- w_router: bfloat16 [512, 8], P('wshard'), may hold values from -0.1875 to 0.1875
- expert_in: bfloat16 [8, 512, 2048], P('expert', None, 'wshard'), may hold values from -0.25 to 0.25
- expert_in_bias: bfloat16 [8, 2048], P('expert', 'wshard'), may hold values from -1.75 to 1.75
- expert_out: bfloat16 [8, 2048, 512], P('expert', 'wshard'), may hold values from -2 to 2
- expert_out_bias: bfloat16 [8, 512], P('expert', 'wshard'), may hold values from -6 to 6
Outputs:
- output: bfloat16 [256, 197, 512], P(('expert', 'wshard'))
- grad_images: float32 [256, 197, 512], P(('expert', 'wshard'))
- grad_attn_norm_gain: float32 [512], P('wshard')
- grad_attn_norm_bias: float32 [512], P('wshard')
- grad_w_qkv: float32 [512, 1536], P('wshard')
- grad_b_query: float32 [512], P('wshard')
- grad_b_value: float32 [512], P('wshard')
- grad_w_attn_out: float32 [512, 512], P('wshard')
- grad_b_attn_out: float32 [512], P('wshard')
- grad_moe_norm_gain: float32 [512], P('wshard')
- grad_moe_norm_bias: float32 [512], P('wshard')
- grad_w_router: float32 [512, 8], P('wshard')
- grad_expert_in: float32 [8, 512, 2048], P('expert', None, 'wshard')
- grad_expert_in_bias: float32 [8, 2048], P('expert', 'wshard')
- grad_expert_out: float32 [8, 2048, 512], P('expert', 'wshard')
- grad_expert_out_bias: float32 [8, 512], P('expert', 'wshard')
The draws below stay inside these ranges and needn't reach their ends.
Inputs may be any that keep to these rules, and one draw needn't show every extreme that they name: `image_count`: each device's live images are its first slots; some device has all 8 live and some device has the fewest. `routes`: each token names two different experts; every expert is named by some token.
All inputs are finite; a program needn't handle non-finite values.
Results may differ from the reference program's by a relative error of at most 0.015.
Values may be sent and summed in bfloat16 or wider, within the bound.
A program may use at most 256 MiB of HBM per device.

```python
import jax
import jax.numpy as jnp
from jax import lax

D = 512
HEADS = 8
HEAD_DIM = 64
HID = 2048
SEQ = 197
SLOTS = 8
EXPERTS = 8
IMAGES = 256
CAP = 394


def draw_image_count(key, part):
    key = jax.random.fold_in(key, 17)
    first_key, second_key, third_key = jax.random.split(key, 3)
    device_count = IMAGES // SLOTS
    fewest = max(1, SLOTS // 2)
    counts = jax.random.randint(first_key, (device_count,), fewest, SLOTS + 1)
    full_device = jax.random.randint(second_key, (), 0, device_count)
    sparse_device = (full_device + 1 + jax.random.randint(third_key, (), 0, device_count - 1)) % device_count
    counts = counts.at[full_device].set(SLOTS).at[sparse_device].set(fewest)
    return counts.astype(jnp.int32)


def level_of(rng, dims, cuts, least, high):
    factor_of = 1.0
    for dim, parts in cuts:
        draws = jax.random.uniform(jax.random.fold_in(jax.random.fold_in(rng, 6), dim), (parts,), jnp.float32, least / len(cuts), high / len(cuts))
        factor_of = factor_of * jnp.repeat(jnp.exp(draws), dims[dim] // parts).reshape((-1,) + (1,) * (len(dims) - 1 - dim))
    return factor_of


def picks_of(own_key, rows, number_of, top, lift):
    sequence = jax.random.permutation(jax.random.fold_in(own_key, 1), number_of)
    favour = sequence
    for power in range(3):
        favour = favour * favour // number_of
    favour = favour * lift // number_of
    tickets = jax.random.randint(jax.random.fold_in(own_key, 2), (rows, number_of), 0, 4096) + favour
    fixed_rows = jax.random.permutation(jax.random.fold_in(own_key, 3), rows)[jnp.arange(number_of) % rows]
    tickets = jnp.where(jnp.arange(rows)[:, None] == fixed_rows[None, :], 1 << 14, tickets)
    priority = tickets * number_of + jnp.arange(number_of)
    return lax.top_k(priority.astype(jnp.int32), top)[1].astype(jnp.int32)


def bell_draw(rng, shape, width, bound, pieces=(), kind=jnp.bfloat16):
    values = width * jax.random.normal(rng, shape, jnp.float32)
    if pieces:
        values = values * level_of(rng, shape, pieces, -0.22, 0.18)
    return jnp.clip(values, -bound, bound).astype(kind)


def setup_inputs(seed: int = 0) -> dict:
    key_of = jax.random.split(jax.random.key(seed), 19)
    images = bell_draw(key_of[0], (IMAGES, SEQ, D), 1.0, 6.0, ((0, 32),))
    cotangent = bell_draw(key_of[1], (IMAGES, SEQ, D), 1.0, 6.0, ((0, 32),))
    image_count = draw_image_count(jax.random.fold_in(key_of[18], 71), 0)
    routes = picks_of(key_of[3], IMAGES * SEQ, EXPERTS, 2, 4096).reshape((IMAGES, SEQ, 2))
    attn_norm_gain = jnp.clip(1.0 + 0.1 * jax.random.normal(key_of[4], (D,), jnp.float32), 0.5, 1.5).astype(jnp.bfloat16)
    attn_norm_bias = bell_draw(key_of[5], (D,), 0.2, 1.25, ((0, 4),))
    w_qkv = bell_draw(key_of[6], (D, 3 * D), D ** -0.5, 0.25, ((0, 4),))
    b_query = bell_draw(key_of[7], (D,), 0.2, 1.25, ((0, 4),))
    b_value = bell_draw(key_of[8], (D,), 0.2, 1.25, ((0, 4),))
    w_attn_out = bell_draw(key_of[9], (D, D), (D // 16) ** -0.5, 1.0, ((0, 4),))
    b_attn_out = bell_draw(key_of[10], (D,), 0.2, 1.25, ((0, 4),))
    moe_norm_gain = jnp.clip(1.0 + 0.1 * jax.random.normal(key_of[11], (D,), jnp.float32), 0.5, 1.5).astype(jnp.bfloat16)
    moe_norm_bias = bell_draw(key_of[12], (D,), 0.2, 1.25, ((0, 4),))
    w_router = bell_draw(key_of[13], (D, EXPERTS), (2 * D) ** -0.5, 0.1875, ((0, 4),))
    expert_in = bell_draw(key_of[14], (EXPERTS, D, HID), D ** -0.5, 0.25, ((0, 8), (2, 4)))
    expert_in_bias = bell_draw(key_of[15], (EXPERTS, HID), 0.3, 1.75, ((0, 8), (1, 4)))
    expert_out = bell_draw(key_of[16], (EXPERTS, HID, D), (max(1, HID // 256)) ** -0.5, 2.0, ((0, 8), (1, 4)))
    expert_out_bias = bell_draw(key_of[17], (EXPERTS, D), 1.0, 6.0, ((0, 8), (1, 4)))
    return dict(images=images, cotangent=cotangent, image_count=image_count, routes=routes, attn_norm_gain=attn_norm_gain, attn_norm_bias=attn_norm_bias, w_qkv=w_qkv, b_query=b_query, b_value=b_value, w_attn_out=w_attn_out, b_attn_out=b_attn_out, moe_norm_gain=moe_norm_gain, moe_norm_bias=moe_norm_bias, w_router=w_router, expert_in=expert_in, expert_in_bias=expert_in_bias, expert_out=expert_out, expert_out_bias=expert_out_bias)


@jax.custom_vjp
def reduced_state(v):
    return lax.optimization_barrier(v.astype(jnp.bfloat16)).astype(jnp.float32)

@jax.custom_vjp
def reduced_backward(v):
    return v

def low_keep(v):
    return (reduced_state(v), None)

def low_pass(kept, grad):
    return (grad,)

def back_keep(v):
    return (v, None)

def back_low(kept, grad):
    return (reduced_state(grad),)
reduced_state.defvjp(low_keep, low_pass)
reduced_backward.defvjp(back_keep, back_low)
norm_eps = 1e-06

def layer_norm(values, gain, bias):
    centre = values - lax.optimization_barrier(jnp.mean(values, axis=-1, keepdims=True))
    spread = lax.optimization_barrier(jnp.mean(centre * centre, axis=-1, keepdims=True))
    return centre * lax.rsqrt(spread + norm_eps) * gain + bias

def matrix_product(form, left, right):
    return jnp.einsum(form, left, right, precision=lax.Precision.HIGHEST)

def routing_slots(image_count, routes):
    device_count = image_count.shape[0]
    tok_count = SLOTS * SEQ
    live_images = (jnp.arange(SLOTS, dtype=jnp.int32)[None, :] < image_count[:, None]).astype(jnp.float32)
    live_tokens = jnp.repeat(live_images, SEQ, axis=1)
    pair_expert = routes.reshape(device_count, tok_count * 2)
    pair_live = jnp.repeat(live_tokens, 2, axis=1) > 0.5
    onehot = ((pair_expert[:, :, None] == jnp.arange(EXPERTS, dtype=jnp.int32)[None, None, :]) & pair_live[:, :, None]).astype(jnp.int32)
    earlier = jnp.cumsum(onehot, axis=1) - onehot
    position = lax.optimization_barrier(jnp.sum(earlier * onehot, axis=2))
    keeping = pair_live & (position < CAP)
    slot_index = jnp.where(keeping, pair_expert * CAP + position, EXPERTS * CAP).astype(jnp.int32)
    return (live_tokens, slot_index)

def reference(images, cotangent, image_count, routes, attn_norm_gain, attn_norm_bias, w_qkv, b_query, b_value, w_attn_out, b_attn_out, moe_norm_gain, moe_norm_bias, w_router, expert_in, expert_in_bias, expert_out, expert_out_bias):
    device_count = IMAGES // SLOTS
    tok_count = SLOTS * SEQ
    live_tokens, slot_index = routing_slots(image_count, routes)
    route_pairs = routes.reshape(device_count, tok_count, 2)
    score_scale = HEAD_DIM ** (-0.5)

    def forward(inputs, norm1_gain, norm1_bias, query_key_value_weight, query_bias, value_bias, projection_weight, projection_bias, norm2_gain, norm2_bias, router_weight, inner_weight, inner_bias, outer_weight, outer_bias):

        def attend(image_block):
            hidden_state = reduced_state(layer_norm(image_block, norm1_gain, norm1_bias))
            merged_bias = jnp.concatenate([query_bias, jnp.zeros((D,), jnp.float32), value_bias])
            merged_rows = reduced_state(reduced_backward(matrix_product('vax,xp->vap', hidden_state, query_key_value_weight) + merged_bias))
            queries = merged_rows[..., :D].reshape(SLOTS, SEQ, HEADS, HEAD_DIM)
            key_rows = merged_rows[..., D:2 * D].reshape(SLOTS, SEQ, HEADS, HEAD_DIM)
            value_rows = merged_rows[..., 2 * D:].reshape(SLOTS, SEQ, HEADS, HEAD_DIM)
            scores = reduced_backward(matrix_product('slhc,smhc->shlm', queries, key_rows) * score_scale)
            weights = reduced_state(jax.nn.softmax(scores, axis=-1))
            blended_rows = reduced_state(reduced_backward(matrix_product('shlm,smhc->slhc', weights, value_rows))).reshape(SLOTS, SEQ, D)
            residual_branch = reduced_backward(matrix_product('vax,xp->vap', blended_rows, projection_weight) + projection_bias)
            return image_block + residual_branch
        stacked = inputs.reshape(device_count, SLOTS, SEQ, D)
        attended = lax.map(jax.checkpoint(attend), stacked).reshape(device_count, tok_count, D)
        normed = reduced_state(layer_norm(attended, norm2_gain, norm2_bias))
        logits = reduced_backward(matrix_product('ntd,de->nte', normed, router_weight))
        router_probs = jax.nn.softmax(logits, axis=-1)
        gate_values = jnp.take_along_axis(router_probs, route_pairs, axis=-1)
        pair_rows = jnp.repeat(normed, 2, axis=1)

        def place_rows(slots_here, rows_here):
            return jnp.zeros((EXPERTS * CAP + 1, D), jnp.float32).at[slots_here].set(rows_here)[:-1]
        buffers = jax.vmap(place_rows)(slot_index, pair_rows)
        grouped = buffers.reshape(device_count, EXPERTS, CAP, D).transpose(1, 0, 2, 3).reshape(EXPERTS, device_count * CAP, D)
        grouped = reduced_backward(grouped)

        def expert(packed):
            rows_in, first_weight, first_bias, second_weight, second_bias = packed
            before = reduced_backward(matrix_product('rd,dh->rh', rows_in, first_weight) + first_bias)
            active = reduced_state(jax.nn.gelu(before))
            return reduced_state(reduced_backward(matrix_product('rh,hd->rd', active, second_weight) + second_bias))
        results = lax.map(jax.checkpoint(expert), (grouped, inner_weight, inner_bias, outer_weight, outer_bias))
        returned = results.reshape(EXPERTS, device_count, CAP, D).transpose(1, 0, 2, 3).reshape(device_count, EXPERTS * CAP, D)
        returned = jnp.concatenate([returned, jnp.zeros((device_count, 1, D), jnp.float32)], axis=1)
        picked = jax.vmap(lambda table, where_rows: table[where_rows])(returned, slot_index).reshape(device_count, tok_count, 2, D)
        combined = lax.optimization_barrier(jnp.sum(gate_values[..., None] * picked, axis=2))
        result = (attended + combined) * live_tokens[..., None]
        return result.reshape(IMAGES, SEQ, D)
    float_args = tuple((item.astype(jnp.float32) for item in (attn_norm_gain, attn_norm_bias, w_qkv, b_query, b_value, w_attn_out, b_attn_out, moe_norm_gain, moe_norm_bias, w_router, expert_in, expert_in_bias, expert_out, expert_out_bias)))
    output, pullback = jax.vjp(forward, images.astype(jnp.float32), *float_args)
    grads = pullback(cotangent.astype(jnp.float32))
    return (output.astype(jnp.bfloat16), grads[0], grads[1], grads[2], grads[3], grads[4], grads[5], grads[6], grads[7], grads[8], grads[9], grads[10], grads[11], grads[12], grads[13], grads[14])
```

```python
import functools

import jax
import jax.numpy as jnp
from jax import lax
from jax.experimental import pallas as pl
from jax.experimental.pallas import tpu as pltpu
from jax.sharding import PartitionSpec as P

HEADS = 8


norm_eps = 1e-06


def layer_norm(values, gain, bias):
    centre = values - jnp.mean(values, axis=-1, keepdims=True)
    spread = jnp.mean(centre * centre, axis=-1, keepdims=True)
    return centre * lax.rsqrt(spread + norm_eps) * gain + bias


def take_share(full, shard_index, shard_count):
    piece = full.shape[0] // shard_count
    return lax.dynamic_slice_in_dim(full, shard_index * piece, piece, 0)


def place_rows(slot_index, rows_here, total_slots):
    buffer = (
        jnp.zeros((total_slots + 1, rows_here.shape[1]), rows_here.dtype)
        .at[slot_index]
        .set(rows_here)
    )
    return buffer[:total_slots]


def token_body(
    images,
    cotangent,
    image_count,
    routes,
    attn_norm_gain,
    attn_norm_bias,
    w_qkv,
    b_query,
    b_value,
    w_attn_out,
    b_attn_out,
    moe_norm_gain,
    moe_norm_bias,
    w_router,
    expert_in,
    expert_in_bias,
    expert_out,
    expert_out_bias,
):
    image_slots, seq_len, model_width = images.shape
    tok_count = image_slots * seq_len
    experts = lax.axis_size("expert")
    shard_count = lax.axis_size("wshard")
    shard_index = lax.axis_index("wshard")
    capacity = (2 * tok_count + experts - 1) // experts
    total_slots = experts * capacity
    head_dim = model_width // HEADS
    score_scale = head_dim ** (-0.5)
    gathered = (
        lax.all_gather(attn_norm_gain, "wshard", axis=0, tiled=True),
        lax.all_gather(attn_norm_bias, "wshard", axis=0, tiled=True),
        lax.all_gather(w_qkv, "wshard", axis=0, tiled=True),
        lax.all_gather(b_query, "wshard", axis=0, tiled=True),
        lax.all_gather(b_value, "wshard", axis=0, tiled=True),
        lax.all_gather(w_attn_out, "wshard", axis=0, tiled=True),
        lax.all_gather(b_attn_out, "wshard", axis=0, tiled=True),
        lax.all_gather(moe_norm_gain, "wshard", axis=0, tiled=True),
        lax.all_gather(moe_norm_bias, "wshard", axis=0, tiled=True),
        lax.all_gather(w_router, "wshard", axis=0, tiled=True),
    )
    gain_one = gathered[0].astype(jnp.float32)
    bias_one = gathered[1].astype(jnp.float32)
    query_key_value_weight = gathered[2]
    query_bias = gathered[3].astype(jnp.float32)
    value_bias = gathered[4].astype(jnp.float32)
    projection_weight = gathered[5]
    projection_bias = gathered[6].astype(jnp.float32)
    gain_two = gathered[7].astype(jnp.float32)
    bias_two = gathered[8].astype(jnp.float32)
    router_weight = gathered[9]
    live_tokens = jnp.repeat(
        (jnp.arange(image_slots, dtype=jnp.int32) < image_count[0]).astype(jnp.float32), seq_len
    )
    inputs = images.astype(jnp.float32).reshape(tok_count, model_width)
    normed_one, norm_one_back = jax.vjp(layer_norm, inputs, gain_one, bias_one)
    hidden_state = normed_one.astype(jnp.bfloat16)
    merged_bias = jnp.concatenate([query_bias, jnp.zeros((model_width,), jnp.float32), value_bias])
    merged_rows = (
        jnp.dot(hidden_state, query_key_value_weight, preferred_element_type=jnp.float32)
        + merged_bias
    ).astype(jnp.bfloat16)
    queries = merged_rows[:, :model_width].reshape(image_slots, seq_len, HEADS, head_dim)
    key_rows = merged_rows[:, model_width : 2 * model_width].reshape(
        image_slots, seq_len, HEADS, head_dim
    )
    value_rows = merged_rows[:, 2 * model_width :].reshape(image_slots, seq_len, HEADS, head_dim)
    scores = (
        jnp.einsum("slhc,smhc->shlm", queries, key_rows, preferred_element_type=jnp.float32)
        * score_scale
    )
    log_total = jax.nn.logsumexp(scores, axis=-1, keepdims=True)
    weights = jnp.exp(scores - log_total).astype(jnp.bfloat16)
    blended_rows = (
        jnp.einsum("shlm,smhc->slhc", weights, value_rows, preferred_element_type=jnp.float32)
        .astype(jnp.bfloat16)
        .reshape(tok_count, model_width)
    )
    attended = (
        inputs
        + jnp.dot(blended_rows, projection_weight, preferred_element_type=jnp.float32)
        + projection_bias
    )
    normed_two, norm_two_back = jax.vjp(layer_norm, attended, gain_two, bias_two)
    routed = normed_two.astype(jnp.bfloat16)
    logits = jnp.dot(routed, router_weight, preferred_element_type=jnp.float32)
    router_probs = jax.nn.softmax(logits, axis=-1)
    route_pairs = routes.reshape(tok_count, 2)
    gate_values = jnp.take_along_axis(router_probs, route_pairs, axis=1)
    pair_expert = route_pairs.reshape(2 * tok_count)
    pair_live = jnp.repeat(live_tokens, 2) > 0.5
    onehot = (
        (pair_expert[:, None] == jnp.arange(experts, dtype=jnp.int32)[None, :]) & pair_live[:, None]
    ).astype(jnp.int32)
    earlier = jnp.cumsum(onehot, axis=0) - onehot
    position = jnp.sum(earlier * onehot, axis=1)
    keeping = pair_live & (position < capacity)
    slot_index = jnp.where(keeping, pair_expert * capacity + position, total_slots)
    outgoing = place_rows(slot_index, jnp.repeat(routed, 2, axis=0), total_slots).reshape(
        experts, capacity, model_width
    )
    arrived = lax.all_to_all(outgoing, "expert", split_axis=0, concat_axis=0, tiled=True).reshape(
        total_slots, model_width
    )
    full_in, full_in_bias, full_out, full_out_bias = (
        lax.all_gather(expert_in, "wshard", axis=2, tiled=True),
        lax.all_gather(expert_in_bias, "wshard", axis=1, tiled=True),
        lax.all_gather(expert_out, "wshard", axis=1, tiled=True),
        lax.all_gather(expert_out_bias, "wshard", axis=1, tiled=True),
    )
    full_in = full_in[0]
    full_out = full_out[0]
    before = jnp.dot(arrived, full_in, preferred_element_type=jnp.float32) + full_in_bias[0].astype(
        jnp.float32
    )
    active, gelu_back = jax.vjp(jax.nn.gelu, before)
    active = active.astype(jnp.bfloat16)
    leaving = (
        jnp.dot(active, full_out, preferred_element_type=jnp.float32)
        + full_out_bias[0].astype(jnp.float32)
    ).astype(jnp.bfloat16)
    coming_back = lax.all_to_all(
        leaving.reshape(experts, capacity, model_width),
        "expert",
        split_axis=0,
        concat_axis=0,
        tiled=True,
    )
    padded = jnp.concatenate(
        [coming_back.reshape(total_slots, model_width), jnp.zeros((1, model_width), jnp.bfloat16)],
        axis=0,
    )
    picked = padded[slot_index].reshape(tok_count, 2, model_width).astype(jnp.float32)
    combined = jnp.sum(gate_values[:, :, None] * picked, axis=1)
    output = (
        ((attended + combined) * live_tokens[:, None])
        .astype(jnp.bfloat16)
        .reshape(image_slots, seq_len, model_width)
    )
    grad_out = cotangent.astype(jnp.float32).reshape(tok_count, model_width) * live_tokens[:, None]
    grad_gates = jnp.einsum("td,tkd->tk", grad_out, picked)
    pair_grads = (
        (gate_values[:, :, None] * grad_out[:, None, :])
        .reshape(2 * tok_count, model_width)
        .astype(jnp.bfloat16)
    )
    outgoing_grads = place_rows(slot_index, pair_grads, total_slots).reshape(
        experts, capacity, model_width
    )
    arrived_grads = lax.all_to_all(
        outgoing_grads, "expert", split_axis=0, concat_axis=0, tiled=True
    ).reshape(total_slots, model_width)
    grad_active = jnp.einsum(
        "rd,hd->rh", arrived_grads, full_out, preferred_element_type=jnp.float32
    )
    grad_before = gelu_back(grad_active)[0].astype(jnp.bfloat16)
    grad_full_out = jnp.einsum(
        "rh,rd->hd", active, arrived_grads, preferred_element_type=jnp.float32
    )
    grad_full_out_bias = jnp.sum(arrived_grads.astype(jnp.float32), axis=0)
    grad_full_in = jnp.einsum("rd,rh->dh", arrived, grad_before, preferred_element_type=jnp.float32)
    grad_full_in_bias = jnp.sum(grad_before.astype(jnp.float32), axis=0)
    grad_arrived = jnp.einsum(
        "rh,dh->rd", grad_before, full_in, preferred_element_type=jnp.float32
    ).astype(jnp.bfloat16)
    expert_grads = (
        lax.psum_scatter(grad_full_in[None], "wshard", scatter_dimension=2, tiled=True),
        lax.psum_scatter(grad_full_in_bias[None], "wshard", scatter_dimension=1, tiled=True),
        lax.psum_scatter(grad_full_out[None], "wshard", scatter_dimension=1, tiled=True),
        lax.psum_scatter(grad_full_out_bias[None], "wshard", scatter_dimension=1, tiled=True),
    )
    returned_grads = lax.all_to_all(
        grad_arrived.reshape(experts, capacity, model_width),
        "expert",
        split_axis=0,
        concat_axis=0,
        tiled=True,
    )
    padded_grads = jnp.concatenate(
        [
            returned_grads.reshape(total_slots, model_width),
            jnp.zeros((1, model_width), jnp.bfloat16),
        ],
        axis=0,
    )
    grad_routed = jnp.sum(
        padded_grads[slot_index].reshape(tok_count, 2, model_width).astype(jnp.float32), axis=1
    )
    route_onehot = (
        route_pairs[:, :, None] == jnp.arange(experts, dtype=jnp.int32)[None, None, :]
    ).astype(jnp.float32)
    grad_probs = jnp.einsum("tk,tke->te", grad_gates, route_onehot)
    grad_logits = (
        router_probs * (grad_probs - jnp.sum(router_probs * grad_probs, axis=-1, keepdims=True))
    ).astype(jnp.bfloat16)
    grad_router = jnp.einsum("td,te->de", routed, grad_logits, preferred_element_type=jnp.float32)
    grad_routed = grad_routed + jnp.einsum(
        "te,de->td", grad_logits, router_weight, preferred_element_type=jnp.float32
    )
    grad_attended, grad_gain_two, grad_bias_two = norm_two_back(grad_routed)
    grad_attended = grad_attended + grad_out
    grad_branch = grad_attended.astype(jnp.bfloat16)
    grad_proj = jnp.einsum(
        "td,te->de", blended_rows, grad_branch, preferred_element_type=jnp.float32
    )
    grad_proj_bias = jnp.sum(grad_branch.astype(jnp.float32), axis=0)
    grad_mixed = (
        jnp.einsum("te,de->td", grad_branch, projection_weight, preferred_element_type=jnp.float32)
        .astype(jnp.bfloat16)
        .reshape(image_slots, seq_len, HEADS, head_dim)
    )
    scores_again = (
        jnp.einsum("slhc,smhc->shlm", queries, key_rows, preferred_element_type=jnp.float32)
        * score_scale
    )
    probs_again = jnp.exp(scores_again - log_total)
    grad_weights = jnp.einsum(
        "slhc,smhc->shlm", grad_mixed, value_rows, preferred_element_type=jnp.float32
    )
    grad_values = jnp.einsum(
        "shlm,slhc->smhc", weights, grad_mixed, preferred_element_type=jnp.float32
    )
    grad_scores = (
        probs_again * (grad_weights - jnp.sum(probs_again * grad_weights, axis=-1, keepdims=True))
    ).astype(jnp.bfloat16)
    grad_queries = (
        jnp.einsum("shlm,smhc->slhc", grad_scores, key_rows, preferred_element_type=jnp.float32)
        * score_scale
    )
    grad_keys = (
        jnp.einsum("shlm,slhc->smhc", grad_scores, queries, preferred_element_type=jnp.float32)
        * score_scale
    )
    grad_joint = jnp.concatenate(
        [
            grad_queries.reshape(tok_count, model_width),
            grad_keys.reshape(tok_count, model_width),
            grad_values.reshape(tok_count, model_width),
        ],
        axis=1,
    ).astype(jnp.bfloat16)
    grad_qkv = jnp.einsum("td,te->de", hidden_state, grad_joint, preferred_element_type=jnp.float32)
    grad_query_bias = jnp.sum(grad_joint[:, :model_width].astype(jnp.float32), axis=0)
    grad_value_bias = jnp.sum(grad_joint[:, 2 * model_width :].astype(jnp.float32), axis=0)
    grad_hidden = jnp.einsum(
        "te,de->td", grad_joint, query_key_value_weight, preferred_element_type=jnp.float32
    )
    grad_inputs, grad_gain_one, grad_bias_one = norm_one_back(grad_hidden)
    grad_images = (grad_attended + grad_inputs).reshape(image_slots, seq_len, model_width)
    full_grads = (
        grad_gain_one,
        grad_bias_one,
        grad_qkv,
        grad_query_bias,
        grad_value_bias,
        grad_proj,
        grad_proj_bias,
        grad_gain_two,
        grad_bias_two,
        grad_router,
    )
    total_grads = lax.psum(
        (
            full_grads[0],
            full_grads[1],
            full_grads[2],
            full_grads[3],
            full_grads[4],
            full_grads[5],
            full_grads[6],
            full_grads[7],
            full_grads[8],
            full_grads[9],
        ),
        ("expert", "wshard"),
    )
    final_grads = tuple((take_share(item, shard_index, shard_count) for item in total_grads))
    return (
        output,
        grad_images,
        final_grads[0],
        final_grads[1],
        final_grads[2],
        final_grads[3],
        final_grads[4],
        final_grads[5],
        final_grads[6],
        final_grads[7],
        final_grads[8],
        final_grads[9],
        expert_grads[0],
        expert_grads[1],
        expert_grads[2],
        expert_grads[3],
    )


F32 = jnp.float32
BF16 = jnp.bfloat16
VMEM_LIMIT = 56 * 1024 * 1024
NN = (((1,), (0,)), ((), ()))
NT = (((1,), (1,)), ((), ()))
TN = (((0,), (0,)), ((), ()))
ROUTER_ROW = 8


def mm(a, b, dims=NN):
    return lax.dot_general(a, b, dims, preferred_element_type=F32)


def whole(shape):
    return pl.BlockSpec(shape, lambda *_: (0,) * len(shape))


def part(shape):
    return pl.BlockSpec((1,) + shape, lambda i: (i,) + (0,) * len(shape))


def params(*semantics):
    return pltpu.CompilerParams(
        dimension_semantics=semantics or None, vmem_limit_bytes=VMEM_LIMIT
    )


def cost(flops, nbytes):
    return pl.CostEstimate(flops=int(flops), bytes_accessed=int(nbytes), transcendentals=0)


def norm_parts(values):
    centre = values - jnp.mean(values, axis=-1, keepdims=True)
    rstd = lax.rsqrt(jnp.mean(centre * centre, axis=-1, keepdims=True) + norm_eps)
    return centre * rstd, rstd


def norm_back(grad, unit, rstd, gain):
    scaled = grad * gain
    return rstd * (
        scaled
        - jnp.mean(scaled, axis=-1, keepdims=True)
        - unit * jnp.mean(scaled * unit, axis=-1, keepdims=True)
    )


def padded_rows(ref, scratch):
    seq, rows = ref.shape[1], scratch.shape[0]
    scratch[rows - 16 : rows] = jnp.zeros((16, scratch.shape[1]), scratch.dtype)
    scratch[0:seq] = ref[0].astype(scratch.dtype)
    return scratch[...]


def half_mask(rows, half):
    return (lax.broadcasted_iota(jnp.int32, (rows, 128), 1) // 64) == half


def forward_kernel(
    images, w_qkv, w_out, vec, router, joint_o, weights_o, mixed_o, attended_o, routed_o, probs_o, rows
):
    seq, width = images.shape[1:]
    inputs = padded_rows(images, rows)
    sp = rows.shape[0]
    unit, _ = norm_parts(inputs)
    hidden = (unit * vec[0:1] + vec[1:2]).astype(BF16)
    bias = jnp.concatenate([vec[2:3], jnp.zeros((1, width), F32), vec[3:4]], axis=1)
    joint_o[0] = (mm(hidden, w_qkv[...]) + bias).astype(BF16)
    scale = (width // HEADS) ** (-0.5)
    key_ok = lax.broadcasted_iota(jnp.int32, (sp, sp), 1) < seq
    for pair in range(HEADS // 2):
        cols = pair * 128
        q = joint_o[0, :, cols : cols + 128]
        k = joint_o[0, :, width + cols : width + cols + 128]
        v = joint_o[0, :, 2 * width + cols : 2 * width + cols + 128]
        total = jnp.zeros((sp, 128), F32)
        for half in range(2):
            sel = half_mask(sp, half)
            km = jnp.where(sel, k, 0)
            vm = jnp.where(sel, v, 0)
            scores = mm(q, km, NT) * scale
            scores = jnp.where(key_ok, scores, -1e30)
            top = jnp.max(scores, axis=-1, keepdims=True)
            power = jnp.exp(scores - top)
            weights = (power / jnp.sum(power, axis=-1, keepdims=True)).astype(BF16)
            weights_o[0, pair * 2 + half] = weights
            total = total + mm(weights, vm)
        mixed_o[0, :, cols : cols + 128] = total.astype(BF16)
    attended = inputs + mm(mixed_o[0], w_out[...]) + vec[4:5]
    attended_o[0] = attended
    unit, _ = norm_parts(attended)
    routed = (unit * vec[5:6] + vec[6:7]).astype(BF16)
    routed_o[0] = routed
    logits = mm(routed, router[...], NT)
    experts = HEADS
    logits = jnp.where(
        lax.broadcasted_iota(jnp.int32, (sp, 128), 1) < experts, logits, -1e30
    )
    power = jnp.exp(logits - jnp.max(logits, axis=-1, keepdims=True))
    probs_o[0] = power / jnp.sum(power, axis=-1, keepdims=True)


def attention_forward(images, w_qkv, w_out, vec, router, sp):
    n, seq, width = images.shape
    shapes = [
        jax.ShapeDtypeStruct((n, sp, 3 * width), BF16),
        jax.ShapeDtypeStruct((n, HEADS, sp, sp), BF16),
        jax.ShapeDtypeStruct((n, sp, width), BF16),
        jax.ShapeDtypeStruct((n, sp, width), F32),
        jax.ShapeDtypeStruct((n, sp, width), BF16),
        jax.ShapeDtypeStruct((n, sp, 128), F32),
    ]
    return pl.pallas_call(
        forward_kernel,
        grid=(n,),
        in_specs=[
            part((seq, width)),
            whole(w_qkv.shape),
            whole(w_out.shape),
            whole(vec.shape),
            whole(router.shape),
        ],
        out_specs=[part(s.shape[1:]) for s in shapes],
        out_shape=shapes,
        scratch_shapes=[pltpu.VMEM((sp, width), F32)],
        compiler_params=params("arbitrary"),
        cost_estimate=cost(2 * n * seq * width * width * 10, 30e6),
        name="attention_forward",
    )(images, w_qkv, w_out, vec, router)


def hot_rows(slots, cap_rows):
    places = lax.broadcasted_iota(jnp.int32, (cap_rows, slots.shape[1]), 0)
    return jnp.where(places == slots, 1.0, 0.0).astype(BF16)


def dispatch_rows_kernel(slots, source, placed_o, flat):
    @pl.when(pl.program_id(0) == 0)
    def _():
        n, seq = source.shape[:2]
        sp = flat.shape[0] // n
        for i in range(n):
            flat[(i + 1) * sp - 16 : (i + 1) * sp] = jnp.zeros((16, flat.shape[1]), BF16)
            flat[i * sp : i * sp + seq] = source[i]

    hot = hot_rows(slots[0], placed_o.shape[1])
    placed_o[0] = mm(hot, flat[...]).astype(BF16)


def dispatch_cotangent(slots, source, sp, cap_rows):
    n, seq, width = source.shape
    count = slots.shape[0]
    return pl.pallas_call(
        dispatch_rows_kernel,
        grid=(count,),
        in_specs=[part(slots.shape[1:]), whole(source.shape)],
        out_specs=part((cap_rows, width)),
        out_shape=jax.ShapeDtypeStruct((count, cap_rows, width), BF16),
        scratch_shapes=[pltpu.VMEM((n * sp, width), BF16)],
        compiler_params=params("arbitrary"),
        cost_estimate=cost(2 * count * cap_rows * n * sp * width, 4e6),
        name="dispatch_cotangent",
    )(slots, source)


def dispatch_routed_kernel(first, slots, routed, probs, placed_o, gates_o):
    hot = hot_rows(slots[0], placed_o.shape[1])
    placed_o[0] = mm(hot, routed[...]).astype(BF16)
    high = probs[...].astype(BF16)
    low = (probs[...] - high.astype(F32)).astype(BF16)
    gates = mm(hot, high) + mm(hot, low)
    lane = lax.broadcasted_iota(jnp.int32, gates.shape, 1)
    mine = jnp.where(lane == first + pl.program_id(0), gates, 0.0)
    gates_o[0] = jnp.sum(mine, axis=1, keepdims=True)


def dispatch_routed(first, slots, routed, probs, cap_rows):
    rows, width = routed.shape
    count = slots.shape[0]
    return pl.pallas_call(
        functools.partial(dispatch_routed_kernel, first),
        grid=(count,),
        in_specs=[part(slots.shape[1:]), whole(routed.shape), whole(probs.shape)],
        out_specs=[part((cap_rows, width)), part((cap_rows, 1))],
        out_shape=[
            jax.ShapeDtypeStruct((count, cap_rows, width), BF16),
            jax.ShapeDtypeStruct((count, cap_rows, 1), F32),
        ],
        compiler_params=params("arbitrary"),
        cost_estimate=cost(2 * count * cap_rows * rows * width * 1.5, 4e6),
        name="dispatch_routed",
    )(slots, routed, probs)


ROOT = 0.7978845608028654
CUBE = 0.044715


def expert_kernel(
    rows_l, rows_r, cot_l, cot_r, gate_l, gate_r, w0, w1, w2, w3, bias_out,
    ans_l, ans_r, grow_l, grow_r, gg_l, gg_r, g0, g1, g2, g3,
    x_s, g_s, gate_s, ans_s, grow_s,
):
    cap = rows_l.shape[1]
    width = rows_l.shape[2]
    x_s[0:cap] = rows_l[0]
    x_s[cap : 2 * cap] = rows_r[0]
    g_s[0:cap] = cot_l[0]
    g_s[cap : 2 * cap] = cot_r[0]
    gate_s[0:cap] = gate_l[0]
    gate_s[cap : 2 * cap] = gate_r[0]
    x = x_s[...]
    scaled = (g_s[...].astype(F32) * gate_s[...]).astype(BF16)
    g_bias_out = jnp.sum(scaled.astype(F32), axis=0, keepdims=True)
    for step, (w, grad) in enumerate(((w0, g0), (w1, g1), (w2, g2), (w3, g3))):
        w_in = w[0:width]
        w_out = w[width : 2 * width]
        before = mm(x, w_in) + w[2 * width : 2 * width + 1].astype(F32)
        square = before * before
        inner = before * (ROOT + ROOT * CUBE * square)
        curve = jnp.tanh(inner)
        half = 0.5 * curve + 0.5
        active = (before * half).astype(BF16)
        slope = half + (0.5 * before) * (1.0 - curve * curve) * (
            ROOT + 3.0 * ROOT * CUBE * square
        )
        grad_active = mm(scaled, w_out, NT)
        grad_before = (grad_active * slope).astype(BF16)
        if step == 0:
            ans_s[...] = mm(active, w_out)
            grow_s[...] = mm(grad_before, w_in, NT)
        else:
            ans_s[...] += mm(active, w_out)
            grow_s[...] += mm(grad_before, w_in, NT)
        grad[0:width] = mm(x, grad_before, TN).astype(BF16)
        grad[width : 2 * width] = mm(active, scaled, TN).astype(BF16)
        tail = lax.broadcasted_iota(jnp.int32, (16, width), 0)
        g_bias_in = jnp.sum(grad_before.astype(F32), axis=0, keepdims=True)
        grad[2 * width : 2 * width + 16] = jnp.where(
            tail == 0, g_bias_in, jnp.where(tail == 1, g_bias_out, 0.0)
        ).astype(BF16)
    answer = (ans_s[...] + bias_out[...]).astype(BF16).astype(F32)
    gg = jnp.sum(answer * g_s[...].astype(F32), axis=1, keepdims=True)
    gated = (answer * gate_s[...]).astype(BF16)
    grows = grow_s[...].astype(BF16)
    ans_l[...] = gated[0:cap]
    ans_r[...] = gated[cap : 2 * cap]
    grow_l[...] = grows[0:cap]
    grow_r[...] = grows[cap : 2 * cap]
    gg_l[...] = gg[0:cap]
    gg_r[...] = gg[cap : 2 * cap]


def expert_step(k, rows_l, rows_r, cot_l, cot_r, gate_l, gate_r, pieces, bias_out):
    _, cap, width = rows_l.shape
    pick = lambda shape: pl.BlockSpec((1,) + shape, lambda i: (k, 0, 0))
    rows = pick((cap, width))
    gates = pick((cap, 1))
    wide = jax.ShapeDtypeStruct((cap, width), BF16)
    thin = jax.ShapeDtypeStruct((cap, 1), F32)
    grad = jax.ShapeDtypeStruct(pieces[0].shape, BF16)
    vmem = pl.BlockSpec(memory_space=pltpu.VMEM)
    return pl.pallas_call(
        expert_kernel,
        grid=(1,),
        in_specs=[rows] * 4 + [gates] * 2 + [vmem] * 5,
        out_specs=[vmem] * 10,
        out_shape=[wide] * 4 + [thin] * 2 + [grad] * 4,
        scratch_shapes=[
            pltpu.VMEM((2 * cap, width), BF16),
            pltpu.VMEM((2 * cap, width), BF16),
            pltpu.VMEM((2 * cap, 1), F32),
            pltpu.VMEM((2 * cap, width), F32),
            pltpu.VMEM((2 * cap, width), F32),
        ],
        compiler_params=params(),
        cost_estimate=cost(2 * 2 * cap * width * width * 4 * 6, 12e6),
        name="expert_step",
    )(rows_l, rows_r, cot_l, cot_r, gate_l, gate_r, *pieces, bias_out)


def hot_tokens(slots, r, cap_rows):
    places = lax.broadcasted_iota(jnp.int32, (slots.shape[0], cap_rows), 1)
    return jnp.where(places == slots[:, r : r + 1], 1.0, 0.0).astype(BF16)


def output_kernel(count, slots, attended, *refs):
    answers, output = refs[:-1], refs[-1]
    cap = answers[0].shape[0]
    total = attended[0]
    for r in range(len(answers)):
        total = total + mm(hot_tokens(slots[0], r, cap), answers[r][...])
    live = (pl.program_id(0) < count[0]).astype(F32)
    output[0] = (total * live).astype(BF16)[0 : output.shape[1]]


def combine_output(count, slots, attended, answers, seq):
    n, sp, width = attended.shape
    cap = answers[0].shape[0]
    return pl.pallas_call(
        output_kernel,
        grid=(n,),
        in_specs=[
            pl.BlockSpec(memory_space=pltpu.SMEM),
            part(slots.shape[1:]),
            part((sp, width)),
        ]
        + [whole((cap, width))] * len(answers),
        out_specs=part((seq, width)),
        out_shape=jax.ShapeDtypeStruct((n, seq, width), BF16),
        compiler_params=params("arbitrary"),
        cost_estimate=cost(2 * n * sp * cap * len(answers) * width, 10e6),
        name="combine_output",
    )(count, slots, attended, *answers)


def backward_kernel(
    count, images, cotangent, joint, weights, mixed, attended, routed, probs, slots,
    w_qkv, w_out, vec, router, *refs
):
    grows, ggs = refs[0:8], refs[8:16]
    g_images, g_qkv, g_out, g_vec, rows, cots, g_joint = refs[16:]
    step = pl.program_id(0)
    seq, width = images.shape[1:]
    sp = rows.shape[0]
    cap = grows[0].shape[0]

    @pl.when(step == 0)
    def _():
        g_qkv[...] = jnp.zeros_like(g_qkv)
        g_out[...] = jnp.zeros_like(g_out)
        g_vec[...] = jnp.zeros_like(g_vec)

    live = (step < count[0]).astype(F32)
    inputs = padded_rows(images, rows)
    grad = padded_rows(cotangent, cots) * live
    lane = lax.broadcasted_iota(jnp.int32, (cap, 128), 1)
    g_routed = jnp.zeros((sp, width), F32)
    g_probs = jnp.zeros((sp, 128), F32)
    for r in range(8):
        hot = hot_tokens(slots[0], r, cap)
        g_routed = g_routed + mm(hot, grows[r][...])
        g_probs = g_probs + mm(hot, jnp.where(lane == r, ggs[r][...], 0.0).astype(BF16))
    p = probs[0]
    g_logits = (p * (g_probs - jnp.sum(p * g_probs, axis=-1, keepdims=True))).astype(BF16)
    g_routed = g_routed + mm(g_logits, router[...])
    g_vec[8:16] += mm(g_logits, routed[0], TN)[0:8]
    unit, rstd = norm_parts(attended[0])
    g_vec[5:6] += jnp.sum(g_routed * unit, axis=0, keepdims=True)
    g_vec[6:7] += jnp.sum(g_routed, axis=0, keepdims=True)
    g_attended = grad + norm_back(g_routed, unit, rstd, vec[5:6])
    branch = g_attended.astype(BF16)
    g_vec[4:5] += jnp.sum(branch.astype(F32), axis=0, keepdims=True)
    g_out[...] += mm(mixed[0], branch, TN)
    g_mixed = mm(branch, w_out[...], NT).astype(BF16)
    scale = (width // HEADS) ** (-0.5)
    for pair in range(HEADS // 2):
        cols = pair * 128
        q = joint[0, :, cols : cols + 128]
        k = joint[0, :, width + cols : width + cols + 128]
        v = joint[0, :, 2 * width + cols : 2 * width + cols + 128]
        gm = g_mixed[:, cols : cols + 128]
        g_q = jnp.zeros((sp, 128), F32)
        g_k = jnp.zeros((sp, 128), F32)
        g_v = jnp.zeros((sp, 128), F32)
        for half in range(2):
            sel = half_mask(sp, half)
            w = weights[0, pair * 2 + half]
            g_p = mm(gm, jnp.where(sel, v, 0), NT)
            wf = w.astype(F32)
            g_s = (wf * (g_p - jnp.sum(wf * g_p, axis=-1, keepdims=True))).astype(BF16)
            g_v = g_v + mm(w, jnp.where(sel, gm, 0), TN)
            g_q = g_q + mm(g_s, jnp.where(sel, k, 0))
            g_k = g_k + mm(g_s, jnp.where(sel, q, 0), TN)
        g_joint[:, cols : cols + 128] = (g_q * scale).astype(BF16)
        g_joint[:, width + cols : width + cols + 128] = (g_k * scale).astype(BF16)
        g_joint[:, 2 * width + cols : 2 * width + cols + 128] = g_v.astype(BF16)
    unit, rstd = norm_parts(inputs)
    hidden = (unit * vec[0:1] + vec[1:2]).astype(BF16)
    gj = g_joint[...]
    g_qkv[...] += mm(hidden, gj, TN)
    g_vec[2:3] += jnp.sum(gj[:, 0:width].astype(F32), axis=0, keepdims=True)
    g_vec[3:4] += jnp.sum(gj[:, 2 * width :].astype(F32), axis=0, keepdims=True)
    g_hidden = mm(gj, w_qkv[...], NT)
    g_vec[0:1] += jnp.sum(g_hidden * unit, axis=0, keepdims=True)
    g_vec[1:2] += jnp.sum(g_hidden, axis=0, keepdims=True)
    g_in = g_attended + norm_back(g_hidden, unit, rstd, vec[0:1])
    g_images[0] = g_in[0:seq]


def attention_backward(
    count, images, cotangent, joint, weights, mixed, attended, routed, probs, slots,
    w_qkv, w_out, vec, router, grows, ggs,
):
    n, seq, width = images.shape
    sp = joint.shape[1]
    streams = [images, cotangent, joint, weights, mixed, attended, routed, probs, slots]
    fixed = [w_qkv, w_out, vec, router, *grows, *ggs]
    shapes = [
        jax.ShapeDtypeStruct((n, seq, width), F32),
        jax.ShapeDtypeStruct(w_qkv.shape, F32),
        jax.ShapeDtypeStruct(w_out.shape, F32),
        jax.ShapeDtypeStruct(vec.shape, F32),
    ]
    return pl.pallas_call(
        backward_kernel,
        grid=(n,),
        in_specs=[pl.BlockSpec(memory_space=pltpu.SMEM)]
        + [part(a.shape[1:]) for a in streams]
        + [whole(a.shape) for a in fixed],
        out_specs=[part((seq, width))] + [whole(s.shape) for s in shapes[1:]],
        out_shape=shapes,
        scratch_shapes=[
            pltpu.VMEM((sp, width), F32),
            pltpu.VMEM((sp, width), F32),
            pltpu.VMEM((sp, 3 * width), BF16),
        ],
        compiler_params=params("arbitrary"),
        cost_estimate=cost(2 * n * seq * width * width * 30, 40e6),
        name="attention_backward",
    )(count, *streams, *fixed)


MESH = pl.DeviceIdType.MESH


def partners():
    e, w = lax.axis_index("expert"), lax.axis_index("wshard")
    return {
        "z": {"expert": lax.rem(e + 2, 8)},
        "z_back": {"expert": lax.rem(e + 6, 8)},
        "x": {"expert": e + 1 - 2 * lax.rem(e, 2)},
        "y": {"wshard": lax.rem(w + 2, 4)},
        "core": {"wshard": w + 1 - 2 * lax.rem(w, 2)},
    }


def meet(devices):
    barrier = pltpu.get_barrier_semaphore()
    for device in devices:
        pl.semaphore_signal(barrier, inc=1, device_id=device, device_id_type=MESH)
    pl.semaphore_wait(barrier, len(devices))


def sender(send, recv, slot, device, src, dst):
    return pltpu.make_async_remote_copy(
        src_ref=src,
        dst_ref=dst,
        send_sem=send.at[slot],
        recv_sem=recv.at[slot],
        device_id=device,
        device_id_type=MESH,
    )


def any_space():
    return pl.BlockSpec(memory_space=pl.ANY)


def gather_kernel(
    images, cotangent, slot_rows, w_qkv, w_out, small, e_in, e_out, e_bias,
    joint_o, weights_o, mixed_o, attended_o, routed_o, probs_o,
    cots_o, pieces_o, qkv_o, out_o, vec_o, router_o,
    rows, flat, placed, qkv, out, smalls, vec, router, send, recv, local,
):
    step = pl.program_id(0)
    last = pl.num_programs(0) - 1
    w = lax.axis_index("wshard")
    to = partners()
    width = w_out.shape[1]
    cap = placed.shape[1]
    share = w_qkv.shape[0]
    w_core = w + 1 - 2 * lax.rem(w, 2)
    w_far = lax.rem(w + 2, 4)

    def rows_of(ref, which):
        return ref.at[pl.ds(pl.multiple_of(which * share, share), share)]

    dense = ((w_qkv, qkv, rows_of), (w_out, out, rows_of), (small, smalls, lambda r, i: r.at[i]))
    own = [pltpu.make_async_copy(a, at(b, w), local.at[i]) for i, (a, b, at) in enumerate(dense)]
    far = [sender(send, recv, i, to["y"], a, at(b, w)) for i, (a, b, at) in enumerate(dense)]
    near = [sender(send, recv, 3 + i, to["core"], a, at(b, w)) for i, (a, b, at) in enumerate(dense)]
    onward = [
        sender(send, recv, 6 + i, to["core"], at(b, w_far), at(b, w_far))
        for i, (a, b, at) in enumerate(dense)
    ]
    pack = [
        pltpu.make_async_copy(e_in.at[0], pieces_o.at[0, 0:width], local.at[3]),
        pltpu.make_async_copy(e_out.at[0], pieces_o.at[0, width : 2 * width], local.at[4]),
        pltpu.make_async_copy(e_bias, pieces_o.at[0, 2 * width : 2 * width + 16], local.at[5]),
    ]
    spread = [
        sender(send, recv, 9, to["z"], pieces_o.at[0], pieces_o.at[4]),
        sender(send, recv, 10, to["y"], pieces_o.at[0], pieces_o.at[2]),
        sender(send, recv, 11, to["core"], pieces_o.at[0], pieces_o.at[1]),
    ]
    cots = [
        sender(send, recv, 12 + k, to["x"], placed.at[4 + k], cots_o.at[k, cap : 2 * cap])
        for k in range(4)
    ]
    kept = [
        pltpu.make_async_copy(placed.at[k], cots_o.at[k, 0:cap], local.at[6 + k]) for k in range(4)
    ]
    saved = [
        pltpu.make_async_copy(qkv, qkv_o, local.at[10]),
        pltpu.make_async_copy(out, out_o, local.at[11]),
    ]

    @pl.when(step == 0)
    def _():
        for copy in own + pack:
            copy.start()
        meet(list(to.values()))
        for copy in far + near:
            copy.start()
        for copy in pack:
            copy.wait()
        for copy in spread:
            copy.start()
        n, seq = cotangent.shape[:2]
        sp = flat.shape[0] // n
        for i in range(n):
            flat[(i + 1) * sp - 16 : (i + 1) * sp] = jnp.zeros((16, width), BF16)
            flat[i * sp : i * sp + seq] = cotangent[i]
        for k in range(4):
            placed[4 + k] = mm(hot_rows(slot_rows[4 + k], cap), flat[...]).astype(BF16)
            cots[k].start()
        for copy in far:
            copy.wait_recv()
        for copy in onward:
            copy.start()
        for k in range(4):
            placed[k] = mm(hot_rows(slot_rows[k], cap), flat[...]).astype(BF16)
            kept[k].start()
        for copy in own:
            copy.wait()
        for copy in near + onward:
            copy.wait_recv()
        for copy in far + near + onward:
            copy.wait_send()
        vec[...] = jnp.concatenate([smalls[i] for i in range(4)], axis=1).astype(F32)
        router[...] = jnp.zeros_like(router)
        router[0:8] = vec[8:16].astype(BF16)
        vec_o[...] = vec[...]
        router_o[...] = router[...]
        for copy in saved:
            copy.start()

    forward_kernel(
        images, qkv, out, vec, router, joint_o, weights_o, mixed_o, attended_o, routed_o,
        probs_o, rows,
    )

    @pl.when(step == last)
    def _():
        for copy in kept + saved:
            copy.wait()
        for copy in cots + spread:
            copy.wait()


def gather_forward(images, cotangent, slot_rows, w_qkv, w_out, small, e_in, e_out, e_bias, sp, cap):
    n, seq, width = images.shape
    piece = 2 * width + 16
    blocks = [
        jax.ShapeDtypeStruct((n, sp, 3 * width), BF16),
        jax.ShapeDtypeStruct((n, HEADS, sp, sp), BF16),
        jax.ShapeDtypeStruct((n, sp, width), BF16),
        jax.ShapeDtypeStruct((n, sp, width), F32),
        jax.ShapeDtypeStruct((n, sp, width), BF16),
        jax.ShapeDtypeStruct((n, sp, 128), F32),
    ]
    far = [
        jax.ShapeDtypeStruct((4, 2 * cap, width), BF16),
        jax.ShapeDtypeStruct((5, piece, width), BF16),
        jax.ShapeDtypeStruct((width, 3 * width), BF16),
        jax.ShapeDtypeStruct((width, width), BF16),
    ]
    small_shapes = [
        jax.ShapeDtypeStruct((16, width), F32),
        jax.ShapeDtypeStruct((128, width), BF16),
    ]
    return pl.pallas_call(
        gather_kernel,
        grid=(n,),
        in_specs=[part((seq, width)), whole(cotangent.shape), whole(slot_rows.shape)]
        + [any_space()] * 6,
        out_specs=[part(s.shape[1:]) for s in blocks]
        + [any_space()] * 4
        + [whole(s.shape) for s in small_shapes],
        out_shape=blocks + far + small_shapes,
        scratch_shapes=[
            pltpu.VMEM((sp, width), F32),
            pltpu.VMEM((n * sp, width), BF16),
            pltpu.VMEM((8, cap, width), BF16),
            pltpu.VMEM((width, 3 * width), BF16),
            pltpu.VMEM((width, width), BF16),
            pltpu.VMEM((4, 16, width // 4), BF16),
            pltpu.VMEM((16, width), F32),
            pltpu.VMEM((128, width), BF16),
            pltpu.SemaphoreType.DMA((16,)),
            pltpu.SemaphoreType.DMA((16,)),
            pltpu.SemaphoreType.DMA((12,)),
        ],
        compiler_params=pltpu.CompilerParams(
            dimension_semantics=("arbitrary",),
            vmem_limit_bytes=VMEM_LIMIT,
            collective_id=0,
            has_side_effects=True,
        ),
        cost_estimate=cost(2 * n * seq * width * width * 20, 40e6),
        name="gather_forward",
    )(images, cotangent, slot_rows, w_qkv, w_out, small, e_in, e_out, e_bias)


def core_swap(a):
    return lax.ppermute(a, "wshard", [(w, w ^ 1) for w in range(4)])


def y_swap(a):
    return lax.ppermute(a, "wshard", [(w, w ^ 2) for w in range(4)])


def x_swap(a):
    return lax.ppermute(a, "expert", [(e, e ^ 1) for e in range(8)])


def z_next(a):
    return lax.ppermute(a, "expert", [(e, (e + 2) % 8) for e in range(8)])


def z_swap(a, bit):
    return lax.ppermute(a, "expert", [(e, e ^ (2 * bit)) for e in range(8)])


def in_order(own, core, far, far_core, shard, axis):
    odd = shard % 2 == 1
    low = [jnp.where(odd, core, own), jnp.where(odd, own, core)]
    high = [jnp.where(odd, far_core, far), jnp.where(odd, far, far_core)]
    up = shard >= 2
    return jnp.concatenate(
        [jnp.where(up, b, a) for a, b in zip(low, high)]
        + [jnp.where(up, a, b) for a, b in zip(low, high)],
        axis=axis,
    )


def gather_shares(piece, shard, axis):
    far = y_swap(piece)
    return in_order(piece, core_swap(piece), far, core_swap(far), shard, axis)


def add16(a, b):
    return (a.astype(F32) + b.astype(F32)).astype(BF16)


def weight_body(
    images, cotangent, image_count, routes, attn_norm_gain, attn_norm_bias, w_qkv, b_query,
    b_value, w_attn_out, b_attn_out, moe_norm_gain, moe_norm_bias, w_router, expert_in,
    expert_in_bias, expert_out, expert_out_bias,
):
    n, seq, width = images.shape
    sp = -(-seq // 16) * 16
    experts = lax.axis_size("expert")
    capacity = (2 * n * seq + experts - 1) // experts
    cap = -(-capacity // 16) * 16
    shard = lax.axis_index("wshard")
    place = lax.axis_index("expert")
    near = jnp.stack([(place - 2 * k) % 8 for k in range(4)])
    order = jnp.concatenate([near, near ^ 1])

    vectors = jnp.stack(
        [attn_norm_gain, attn_norm_bias, b_query, b_value, b_attn_out, moe_norm_gain, moe_norm_bias]
    )
    small = jnp.concatenate([jnp.pad(vectors, ((0, 1), (0, 0))), w_router.T[order]])
    e_bias = jnp.concatenate(
        [
            expert_in_bias,
            jnp.pad(expert_out_bias, ((0, 0), (0, width - expert_out_bias.shape[1]))),
            jnp.zeros((14, width), BF16),
        ]
    )

    live = jnp.arange(n, dtype=jnp.int32) < image_count[0]
    member = (routes[:, :, 0:1] == order) | (routes[:, :, 1:2] == order)
    member = (member & live[:, None, None]).astype(BF16)
    lower = jnp.tril(jnp.ones((seq, seq), BF16), -1)
    earlier = jnp.einsum("ts,ise->ite", lower, member, preferred_element_type=F32)
    counts = jnp.sum(member.astype(F32), axis=1)
    base = jnp.cumsum(counts, axis=0) - counts
    position = (earlier + base[:, None, :]).astype(jnp.int32)
    slots = jnp.where((member > 0) & (position < capacity), position, -1)
    slots = jnp.pad(slots, ((0, 0), (0, sp - seq), (0, 0)), constant_values=-1)
    slot_rows = slots.transpose(2, 0, 1).reshape(8, 1, n * sp)

    (
        joint, weights, mixed, attended, routed, probs,
        cots, ring, w_qkv_full, w_out_full, vec, router,
    ) = gather_forward(
        images, cotangent, slot_rows, w_qkv, w_attn_out, small, expert_in, expert_out, e_bias, sp, cap
    )
    cot_l, cot_r = cots[:, :cap], cots[:, cap:]
    pieces = [(ring[0], ring[1], ring[2], core_swap(ring[2]))]
    item = ring[4]
    for k in range(3):
        far = y_swap(item)
        pieces.append((item, core_swap(item), far, core_swap(far)))
        item = z_next(item)
    flat_routed = routed.reshape(n * sp, width)
    flat_probs = probs.reshape(n * sp, 128)
    rows_sent, gate_sent = dispatch_routed(4, slot_rows[4:8], flat_routed, flat_probs, cap)
    rows_r = x_swap(rows_sent)
    gate_r = x_swap(gate_sent.reshape(4, cap)).reshape(4, cap, 1)
    rows_l, gate_l = dispatch_routed(0, slot_rows[0:4], flat_routed, flat_probs, cap)

    answers_l, answers_r, grows_l, grows_r, ggs_l, ggs_r = [], [], [], [], [], []
    totals = []
    for k in range(4):
        bias_out = in_order(
            *[p[2 * width + 1 : 2 * width + 2, : width // 4] for p in pieces[k]], shard, 1
        ).astype(F32)
        out = expert_step(k, rows_l, rows_r, cot_l, cot_r, gate_l, gate_r, pieces[k], bias_out)
        answers_l.append(out[0])
        answers_r.append(x_swap(out[1]))
        grows_l.append(out[2])
        grows_r.append(x_swap(out[3]))
        ggs_l.append(out[4])
        ggs_r.append(x_swap(out[5].reshape(1, cap)).reshape(cap, 1))
        g_own, g_core, g_far, g_far_core = out[6:10]
        a_own = add16(g_own, core_swap(g_core))
        a_far = add16(g_far, core_swap(g_far_core))
        totals.append(add16(a_own, y_swap(a_far)))
    passing = totals[1]
    for k in (2, 3):
        passing = add16(totals[k], z_next(passing))
    final = totals[0].astype(F32) + z_next(passing).astype(F32)

    grad_images, g_qkv, g_out, g_vec = attention_backward(
        image_count, images, cotangent, joint, weights, mixed, attended, routed, probs, slots,
        w_qkv_full, w_out_full, vec, router, grows_l + grows_r, ggs_l + ggs_r,
    )
    output = combine_output(image_count, slots, attended, answers_l + answers_r, seq)

    g_vec = jnp.concatenate([g_vec[0:8], jnp.zeros((8, width), F32).at[order].set(g_vec[8:16])])
    g_dense = jnp.concatenate([g_qkv, g_out], axis=1).astype(BF16)

    def share(a, which, axis):
        size = a.shape[axis] // 4
        return lax.dynamic_slice_in_dim(a, (shard ^ which) * size, size, axis)

    def total_over_all(a, axis):
        own = share(a, 0, axis) + core_swap(share(a, 1, axis))
        far = share(a, 2, axis) + core_swap(share(a, 3, axis))
        own = own + y_swap(far)
        own = own + x_swap(own)
        own = own + z_swap(own, 1)
        return own + z_swap(own, 2)

    g_dense = total_over_all(g_dense, 0).astype(F32)
    g_small = total_over_all(g_vec, 1)
    quarter = width // 4
    g_bias_out = lax.dynamic_slice_in_dim(
        final[2 * width + 1 : 2 * width + 2], shard * quarter, quarter, 1
    )
    return (
        output,
        grad_images,
        g_small[0],
        g_small[1],
        g_dense[:, : 3 * width],
        g_small[2],
        g_small[3],
        g_dense[:, 3 * width :],
        g_small[4],
        g_small[5],
        g_small[6],
        g_small[8:16].T,
        final[0:width][None],
        final[2 * width : 2 * width + 1],
        final[width : 2 * width][None],
        g_bias_out,
    )


def solution(mesh):
    in_specs = (
        P(("expert", "wshard"), None, None),
        P(("expert", "wshard"), None, None),
        P(("expert", "wshard")),
        P(("expert", "wshard"), None, None),
        P("wshard"),
        P("wshard"),
        P("wshard", None),
        P("wshard"),
        P("wshard"),
        P("wshard", None),
        P("wshard"),
        P("wshard"),
        P("wshard"),
        P("wshard", None),
        P("expert", None, "wshard"),
        P("expert", "wshard"),
        P("expert", "wshard", None),
        P("expert", "wshard"),
    )
    out_specs = (
        P(("expert", "wshard"), None, None),
        P(("expert", "wshard"), None, None),
        P("wshard"),
        P("wshard"),
        P("wshard", None),
        P("wshard"),
        P("wshard"),
        P("wshard", None),
        P("wshard"),
        P("wshard"),
        P("wshard"),
        P("wshard", None),
        P("expert", None, "wshard"),
        P("expert", "wshard"),
        P("expert", "wshard", None),
        P("expert", "wshard"),
    )
    small_slice = mesh.shape["expert"] == 8 and mesh.shape["wshard"] == 4
    body = weight_body if small_slice else token_body
    return jax.shard_map(body, mesh=mesh, in_specs=in_specs, out_specs=out_specs, check_vma=False)
```

```python
import functools

import jax
import jax.numpy as jnp
from jax import lax
from jax.experimental import pallas as pl
from jax.experimental.pallas import tpu as pltpu
from jax.sharding import PartitionSpec as P

HEADS = 8


norm_eps = 1e-06


def layer_norm(values, gain, bias):
    centre = values - jnp.mean(values, axis=-1, keepdims=True)
    spread = jnp.mean(centre * centre, axis=-1, keepdims=True)
    return centre * lax.rsqrt(spread + norm_eps) * gain + bias


def take_share(full, shard_index, shard_count):
    piece = full.shape[0] // shard_count
    return lax.dynamic_slice_in_dim(full, shard_index * piece, piece, 0)


def place_rows(slot_index, rows_here, total_slots):
    buffer = (
        jnp.zeros((total_slots + 1, rows_here.shape[1]), rows_here.dtype)
        .at[slot_index]
        .set(rows_here)
    )
    return buffer[:total_slots]


def token_body(
    images,
    cotangent,
    image_count,
    routes,
    attn_norm_gain,
    attn_norm_bias,
    w_qkv,
    b_query,
    b_value,
    w_attn_out,
    b_attn_out,
    moe_norm_gain,
    moe_norm_bias,
    w_router,
    expert_in,
    expert_in_bias,
    expert_out,
    expert_out_bias,
):
    image_slots, seq_len, model_width = images.shape
    tok_count = image_slots * seq_len
    experts = lax.axis_size("expert")
    shard_count = lax.axis_size("wshard")
    shard_index = lax.axis_index("wshard")
    capacity = (2 * tok_count + experts - 1) // experts
    total_slots = experts * capacity
    head_dim = model_width // HEADS
    score_scale = head_dim ** (-0.5)
    gathered = (
        lax.all_gather(attn_norm_gain, "wshard", axis=0, tiled=True),
        lax.all_gather(attn_norm_bias, "wshard", axis=0, tiled=True),
        lax.all_gather(w_qkv, "wshard", axis=0, tiled=True),
        lax.all_gather(b_query, "wshard", axis=0, tiled=True),
        lax.all_gather(b_value, "wshard", axis=0, tiled=True),
        lax.all_gather(w_attn_out, "wshard", axis=0, tiled=True),
        lax.all_gather(b_attn_out, "wshard", axis=0, tiled=True),
        lax.all_gather(moe_norm_gain, "wshard", axis=0, tiled=True),
        lax.all_gather(moe_norm_bias, "wshard", axis=0, tiled=True),
        lax.all_gather(w_router, "wshard", axis=0, tiled=True),
    )
    gain_one = gathered[0].astype(jnp.float32)
    bias_one = gathered[1].astype(jnp.float32)
    query_key_value_weight = gathered[2]
    query_bias = gathered[3].astype(jnp.float32)
    value_bias = gathered[4].astype(jnp.float32)
    projection_weight = gathered[5]
    projection_bias = gathered[6].astype(jnp.float32)
    gain_two = gathered[7].astype(jnp.float32)
    bias_two = gathered[8].astype(jnp.float32)
    router_weight = gathered[9]
    live_tokens = jnp.repeat(
        (jnp.arange(image_slots, dtype=jnp.int32) < image_count[0]).astype(jnp.float32), seq_len
    )
    inputs = images.astype(jnp.float32).reshape(tok_count, model_width)
    normed_one, norm_one_back = jax.vjp(layer_norm, inputs, gain_one, bias_one)
    hidden_state = normed_one.astype(jnp.bfloat16)
    merged_bias = jnp.concatenate([query_bias, jnp.zeros((model_width,), jnp.float32), value_bias])
    merged_rows = (
        jnp.dot(hidden_state, query_key_value_weight, preferred_element_type=jnp.float32)
        + merged_bias
    ).astype(jnp.bfloat16)
    queries = merged_rows[:, :model_width].reshape(image_slots, seq_len, HEADS, head_dim)
    key_rows = merged_rows[:, model_width : 2 * model_width].reshape(
        image_slots, seq_len, HEADS, head_dim
    )
    value_rows = merged_rows[:, 2 * model_width :].reshape(image_slots, seq_len, HEADS, head_dim)
    scores = (
        jnp.einsum("slhc,smhc->shlm", queries, key_rows, preferred_element_type=jnp.float32)
        * score_scale
    )
    log_total = jax.nn.logsumexp(scores, axis=-1, keepdims=True)
    weights = jnp.exp(scores - log_total).astype(jnp.bfloat16)
    blended_rows = (
        jnp.einsum("shlm,smhc->slhc", weights, value_rows, preferred_element_type=jnp.float32)
        .astype(jnp.bfloat16)
        .reshape(tok_count, model_width)
    )
    attended = (
        inputs
        + jnp.dot(blended_rows, projection_weight, preferred_element_type=jnp.float32)
        + projection_bias
    )
    normed_two, norm_two_back = jax.vjp(layer_norm, attended, gain_two, bias_two)
    routed = normed_two.astype(jnp.bfloat16)
    logits = jnp.dot(routed, router_weight, preferred_element_type=jnp.float32)
    router_probs = jax.nn.softmax(logits, axis=-1)
    route_pairs = routes.reshape(tok_count, 2)
    gate_values = jnp.take_along_axis(router_probs, route_pairs, axis=1)
    pair_expert = route_pairs.reshape(2 * tok_count)
    pair_live = jnp.repeat(live_tokens, 2) > 0.5
    onehot = (
        (pair_expert[:, None] == jnp.arange(experts, dtype=jnp.int32)[None, :]) & pair_live[:, None]
    ).astype(jnp.int32)
    earlier = jnp.cumsum(onehot, axis=0) - onehot
    position = jnp.sum(earlier * onehot, axis=1)
    keeping = pair_live & (position < capacity)
    slot_index = jnp.where(keeping, pair_expert * capacity + position, total_slots)
    outgoing = place_rows(slot_index, jnp.repeat(routed, 2, axis=0), total_slots).reshape(
        experts, capacity, model_width
    )
    arrived = lax.all_to_all(outgoing, "expert", split_axis=0, concat_axis=0, tiled=True).reshape(
        total_slots, model_width
    )
    full_in, full_in_bias, full_out, full_out_bias = (
        lax.all_gather(expert_in, "wshard", axis=2, tiled=True),
        lax.all_gather(expert_in_bias, "wshard", axis=1, tiled=True),
        lax.all_gather(expert_out, "wshard", axis=1, tiled=True),
        lax.all_gather(expert_out_bias, "wshard", axis=1, tiled=True),
    )
    full_in = full_in[0]
    full_out = full_out[0]
    before = jnp.dot(arrived, full_in, preferred_element_type=jnp.float32) + full_in_bias[0].astype(
        jnp.float32
    )
    active, gelu_back = jax.vjp(jax.nn.gelu, before)
    active = active.astype(jnp.bfloat16)
    leaving = (
        jnp.dot(active, full_out, preferred_element_type=jnp.float32)
        + full_out_bias[0].astype(jnp.float32)
    ).astype(jnp.bfloat16)
    coming_back = lax.all_to_all(
        leaving.reshape(experts, capacity, model_width),
        "expert",
        split_axis=0,
        concat_axis=0,
        tiled=True,
    )
    padded = jnp.concatenate(
        [coming_back.reshape(total_slots, model_width), jnp.zeros((1, model_width), jnp.bfloat16)],
        axis=0,
    )
    picked = padded[slot_index].reshape(tok_count, 2, model_width).astype(jnp.float32)
    combined = jnp.sum(gate_values[:, :, None] * picked, axis=1)
    output = (
        ((attended + combined) * live_tokens[:, None])
        .astype(jnp.bfloat16)
        .reshape(image_slots, seq_len, model_width)
    )
    grad_out = cotangent.astype(jnp.float32).reshape(tok_count, model_width) * live_tokens[:, None]
    grad_gates = jnp.einsum("td,tkd->tk", grad_out, picked)
    pair_grads = (
        (gate_values[:, :, None] * grad_out[:, None, :])
        .reshape(2 * tok_count, model_width)
        .astype(jnp.bfloat16)
    )
    outgoing_grads = place_rows(slot_index, pair_grads, total_slots).reshape(
        experts, capacity, model_width
    )
    arrived_grads = lax.all_to_all(
        outgoing_grads, "expert", split_axis=0, concat_axis=0, tiled=True
    ).reshape(total_slots, model_width)
    grad_active = jnp.einsum(
        "rd,hd->rh", arrived_grads, full_out, preferred_element_type=jnp.float32
    )
    grad_before = gelu_back(grad_active)[0].astype(jnp.bfloat16)
    grad_full_out = jnp.einsum(
        "rh,rd->hd", active, arrived_grads, preferred_element_type=jnp.float32
    )
    grad_full_out_bias = jnp.sum(arrived_grads.astype(jnp.float32), axis=0)
    grad_full_in = jnp.einsum("rd,rh->dh", arrived, grad_before, preferred_element_type=jnp.float32)
    grad_full_in_bias = jnp.sum(grad_before.astype(jnp.float32), axis=0)
    grad_arrived = jnp.einsum(
        "rh,dh->rd", grad_before, full_in, preferred_element_type=jnp.float32
    ).astype(jnp.bfloat16)
    expert_grads = (
        lax.psum_scatter(grad_full_in[None], "wshard", scatter_dimension=2, tiled=True),
        lax.psum_scatter(grad_full_in_bias[None], "wshard", scatter_dimension=1, tiled=True),
        lax.psum_scatter(grad_full_out[None], "wshard", scatter_dimension=1, tiled=True),
        lax.psum_scatter(grad_full_out_bias[None], "wshard", scatter_dimension=1, tiled=True),
    )
    returned_grads = lax.all_to_all(
        grad_arrived.reshape(experts, capacity, model_width),
        "expert",
        split_axis=0,
        concat_axis=0,
        tiled=True,
    )
    padded_grads = jnp.concatenate(
        [
            returned_grads.reshape(total_slots, model_width),
            jnp.zeros((1, model_width), jnp.bfloat16),
        ],
        axis=0,
    )
    grad_routed = jnp.sum(
        padded_grads[slot_index].reshape(tok_count, 2, model_width).astype(jnp.float32), axis=1
    )
    route_onehot = (
        route_pairs[:, :, None] == jnp.arange(experts, dtype=jnp.int32)[None, None, :]
    ).astype(jnp.float32)
    grad_probs = jnp.einsum("tk,tke->te", grad_gates, route_onehot)
    grad_logits = (
        router_probs * (grad_probs - jnp.sum(router_probs * grad_probs, axis=-1, keepdims=True))
    ).astype(jnp.bfloat16)
    grad_router = jnp.einsum("td,te->de", routed, grad_logits, preferred_element_type=jnp.float32)
    grad_routed = grad_routed + jnp.einsum(
        "te,de->td", grad_logits, router_weight, preferred_element_type=jnp.float32
    )
    grad_attended, grad_gain_two, grad_bias_two = norm_two_back(grad_routed)
    grad_attended = grad_attended + grad_out
    grad_branch = grad_attended.astype(jnp.bfloat16)
    grad_proj = jnp.einsum(
        "td,te->de", blended_rows, grad_branch, preferred_element_type=jnp.float32
    )
    grad_proj_bias = jnp.sum(grad_branch.astype(jnp.float32), axis=0)
    grad_mixed = (
        jnp.einsum("te,de->td", grad_branch, projection_weight, preferred_element_type=jnp.float32)
        .astype(jnp.bfloat16)
        .reshape(image_slots, seq_len, HEADS, head_dim)
    )
    scores_again = (
        jnp.einsum("slhc,smhc->shlm", queries, key_rows, preferred_element_type=jnp.float32)
        * score_scale
    )
    probs_again = jnp.exp(scores_again - log_total)
    grad_weights = jnp.einsum(
        "slhc,smhc->shlm", grad_mixed, value_rows, preferred_element_type=jnp.float32
    )
    grad_values = jnp.einsum(
        "shlm,slhc->smhc", weights, grad_mixed, preferred_element_type=jnp.float32
    )
    grad_scores = (
        probs_again * (grad_weights - jnp.sum(probs_again * grad_weights, axis=-1, keepdims=True))
    ).astype(jnp.bfloat16)
    grad_queries = (
        jnp.einsum("shlm,smhc->slhc", grad_scores, key_rows, preferred_element_type=jnp.float32)
        * score_scale
    )
    grad_keys = (
        jnp.einsum("shlm,slhc->smhc", grad_scores, queries, preferred_element_type=jnp.float32)
        * score_scale
    )
    grad_joint = jnp.concatenate(
        [
            grad_queries.reshape(tok_count, model_width),
            grad_keys.reshape(tok_count, model_width),
            grad_values.reshape(tok_count, model_width),
        ],
        axis=1,
    ).astype(jnp.bfloat16)
    grad_qkv = jnp.einsum("td,te->de", hidden_state, grad_joint, preferred_element_type=jnp.float32)
    grad_query_bias = jnp.sum(grad_joint[:, :model_width].astype(jnp.float32), axis=0)
    grad_value_bias = jnp.sum(grad_joint[:, 2 * model_width :].astype(jnp.float32), axis=0)
    grad_hidden = jnp.einsum(
        "te,de->td", grad_joint, query_key_value_weight, preferred_element_type=jnp.float32
    )
    grad_inputs, grad_gain_one, grad_bias_one = norm_one_back(grad_hidden)
    grad_images = (grad_attended + grad_inputs).reshape(image_slots, seq_len, model_width)
    full_grads = (
        grad_gain_one,
        grad_bias_one,
        grad_qkv,
        grad_query_bias,
        grad_value_bias,
        grad_proj,
        grad_proj_bias,
        grad_gain_two,
        grad_bias_two,
        grad_router,
    )
    total_grads = lax.psum(
        (
            full_grads[0],
            full_grads[1],
            full_grads[2],
            full_grads[3],
            full_grads[4],
            full_grads[5],
            full_grads[6],
            full_grads[7],
            full_grads[8],
            full_grads[9],
        ),
        ("expert", "wshard"),
    )
    final_grads = tuple((take_share(item, shard_index, shard_count) for item in total_grads))
    return (
        output,
        grad_images,
        final_grads[0],
        final_grads[1],
        final_grads[2],
        final_grads[3],
        final_grads[4],
        final_grads[5],
        final_grads[6],
        final_grads[7],
        final_grads[8],
        final_grads[9],
        expert_grads[0],
        expert_grads[1],
        expert_grads[2],
        expert_grads[3],
    )


F32 = jnp.float32
BF16 = jnp.bfloat16
VMEM_LIMIT = 56 * 1024 * 1024
NN = (((1,), (0,)), ((), ()))
NT = (((1,), (1,)), ((), ()))
TN = (((0,), (0,)), ((), ()))
ROUTER_ROW = 8


def mm(a, b, dims=NN):
    return lax.dot_general(a, b, dims, preferred_element_type=F32)


def whole(shape):
    return pl.BlockSpec(shape, lambda *_: (0,) * len(shape))


def part(shape):
    return pl.BlockSpec((1,) + shape, lambda i: (i,) + (0,) * len(shape))


def params(*semantics):
    return pltpu.CompilerParams(
        dimension_semantics=semantics or None, vmem_limit_bytes=VMEM_LIMIT
    )


def cost(flops, nbytes):
    return pl.CostEstimate(flops=int(flops), bytes_accessed=int(nbytes), transcendentals=0)


def norm_parts(values):
    centre = values - jnp.mean(values, axis=-1, keepdims=True)
    rstd = lax.rsqrt(jnp.mean(centre * centre, axis=-1, keepdims=True) + norm_eps)
    return centre * rstd, rstd


def norm_back(grad, unit, rstd, gain):
    scaled = grad * gain
    return rstd * (
        scaled
        - jnp.mean(scaled, axis=-1, keepdims=True)
        - unit * jnp.mean(scaled * unit, axis=-1, keepdims=True)
    )


def padded_rows(ref, scratch):
    seq, rows = ref.shape[1], scratch.shape[0]
    scratch[rows - 16 : rows] = jnp.zeros((16, scratch.shape[1]), scratch.dtype)
    scratch[0:seq] = ref[0].astype(scratch.dtype)
    return scratch[...]


def half_mask(rows, half):
    return (lax.broadcasted_iota(jnp.int32, (rows, 128), 1) // 64) == half


def forward_kernel(
    images, w_qkv, w_out, vec, router, joint_o, weights_o, mixed_o, attended_o, routed_o, probs_o, rows
):
    seq, width = images.shape[1:]
    inputs = padded_rows(images, rows)
    sp = rows.shape[0]
    unit, _ = norm_parts(inputs)
    hidden = (unit * vec[0:1] + vec[1:2]).astype(BF16)
    bias = jnp.concatenate([vec[2:3], jnp.zeros((1, width), F32), vec[3:4]], axis=1)
    joint_o[0] = (mm(hidden, w_qkv[...]) + bias).astype(BF16)
    scale = (width // HEADS) ** (-0.5)
    key_ok = lax.broadcasted_iota(jnp.int32, (sp, sp), 1) < seq
    for pair in range(HEADS // 2):
        cols = pair * 128
        q = joint_o[0, :, cols : cols + 128]
        k = joint_o[0, :, width + cols : width + cols + 128]
        v = joint_o[0, :, 2 * width + cols : 2 * width + cols + 128]
        total = jnp.zeros((sp, 128), F32)
        for half in range(2):
            sel = half_mask(sp, half)
            km = jnp.where(sel, k, 0)
            vm = jnp.where(sel, v, 0)
            scores = mm(q, km, NT) * scale
            scores = jnp.where(key_ok, scores, -1e30)
            top = jnp.max(scores, axis=-1, keepdims=True)
            power = jnp.exp(scores - top)
            weights = (power / jnp.sum(power, axis=-1, keepdims=True)).astype(BF16)
            weights_o[0, pair * 2 + half] = weights
            total = total + mm(weights, vm)
        mixed_o[0, :, cols : cols + 128] = total.astype(BF16)
    attended = inputs + mm(mixed_o[0], w_out[...]) + vec[4:5]
    attended_o[0] = attended
    unit, _ = norm_parts(attended)
    routed = (unit * vec[5:6] + vec[6:7]).astype(BF16)
    routed_o[0] = routed
    logits = mm(routed, router[...], NT)
    experts = HEADS
    logits = jnp.where(
        lax.broadcasted_iota(jnp.int32, (sp, 128), 1) < experts, logits, -1e30
    )
    power = jnp.exp(logits - jnp.max(logits, axis=-1, keepdims=True))
    probs_o[0] = power / jnp.sum(power, axis=-1, keepdims=True)


def attention_forward(images, w_qkv, w_out, vec, router, sp):
    n, seq, width = images.shape
    shapes = [
        jax.ShapeDtypeStruct((n, sp, 3 * width), BF16),
        jax.ShapeDtypeStruct((n, HEADS, sp, sp), BF16),
        jax.ShapeDtypeStruct((n, sp, width), BF16),
        jax.ShapeDtypeStruct((n, sp, width), F32),
        jax.ShapeDtypeStruct((n, sp, width), BF16),
        jax.ShapeDtypeStruct((n, sp, 128), F32),
    ]
    return pl.pallas_call(
        forward_kernel,
        grid=(n,),
        in_specs=[
            part((seq, width)),
            whole(w_qkv.shape),
            whole(w_out.shape),
            whole(vec.shape),
            whole(router.shape),
        ],
        out_specs=[part(s.shape[1:]) for s in shapes],
        out_shape=shapes,
        scratch_shapes=[pltpu.VMEM((sp, width), F32)],
        compiler_params=params("arbitrary"),
        cost_estimate=cost(2 * n * seq * width * width * 10, 30e6),
        name="attention_forward",
    )(images, w_qkv, w_out, vec, router)


def hot_rows(slots, cap_rows):
    places = lax.broadcasted_iota(jnp.int32, (cap_rows, slots.shape[1]), 0)
    return jnp.where(places == slots, 1.0, 0.0).astype(BF16)


ROOT = 0.7978845608028654
CUBE = 0.044715


def hot_tokens(slots, r, cap_rows):
    places = lax.broadcasted_iota(jnp.int32, (slots.shape[0], cap_rows), 1)
    return jnp.where(places == slots[:, r : r + 1], 1.0, 0.0).astype(BF16)


def output_kernel(step, count, slots, attended, answers_l, answers_r, output):
    cap = answers_l.shape[1]
    total = attended[0]
    for r in range(8):
        rows = answers_l[r] if r < 4 else answers_r[r - 4]
        total = total + mm(hot_tokens(slots[0], r, cap), rows)
    live = (step < count[0]).astype(F32)
    output[0] = (total * live).astype(BF16)[0 : output.shape[1]]


def backward_kernel(
    step, count, images, cotangent, joint, weights, mixed, attended, routed, probs, slots,
    w_qkv, w_out, vec, router, grows, ggs, g_images, g_qkv, g_out, g_vec, rows, cots, g_joint
):
    seq, width = images.shape[1:]
    sp = rows.shape[0]
    cap = grows.shape[1]

    live = (step < count[0]).astype(F32)
    inputs = padded_rows(images, rows)
    grad = padded_rows(cotangent, cots) * live
    g_routed = jnp.zeros((sp, width), F32)
    g_probs = jnp.zeros((sp, 128), F32)
    for r in range(8):
        hot = hot_tokens(slots[0], r, cap)
        g_routed = g_routed + mm(hot, grows[r])
        g_probs = g_probs + mm(hot, ggs[r])
    p = probs[0]
    g_logits = (p * (g_probs - jnp.sum(p * g_probs, axis=-1, keepdims=True))).astype(BF16)
    g_routed = g_routed + mm(g_logits, router[...])
    g_vec[8:16] += mm(g_logits, routed[0], TN)[0:8]
    unit, rstd = norm_parts(attended[0])
    g_vec[5:6] += jnp.sum(g_routed * unit, axis=0, keepdims=True)
    g_vec[6:7] += jnp.sum(g_routed, axis=0, keepdims=True)
    g_attended = grad + norm_back(g_routed, unit, rstd, vec[5:6])
    branch = g_attended.astype(BF16)
    g_vec[4:5] += jnp.sum(branch.astype(F32), axis=0, keepdims=True)
    g_out[...] += mm(mixed[0], branch, TN)
    g_mixed = mm(branch, w_out[...], NT).astype(BF16)
    scale = (width // HEADS) ** (-0.5)
    for pair in range(HEADS // 2):
        cols = pair * 128
        q = joint[0, :, cols : cols + 128]
        k = joint[0, :, width + cols : width + cols + 128]
        v = joint[0, :, 2 * width + cols : 2 * width + cols + 128]
        gm = g_mixed[:, cols : cols + 128]
        g_q = jnp.zeros((sp, 128), F32)
        g_k = jnp.zeros((sp, 128), F32)
        g_v = jnp.zeros((sp, 128), F32)
        for half in range(2):
            sel = half_mask(sp, half)
            w = weights[0, pair * 2 + half]
            g_p = mm(gm, jnp.where(sel, v, 0), NT)
            wf = w.astype(F32)
            g_s = (wf * (g_p - jnp.sum(wf * g_p, axis=-1, keepdims=True))).astype(BF16)
            g_v = g_v + mm(w, jnp.where(sel, gm, 0), TN)
            g_q = g_q + mm(g_s, jnp.where(sel, k, 0))
            g_k = g_k + mm(g_s, jnp.where(sel, q, 0), TN)
        g_joint[:, cols : cols + 128] = (g_q * scale).astype(BF16)
        g_joint[:, width + cols : width + cols + 128] = (g_k * scale).astype(BF16)
        g_joint[:, 2 * width + cols : 2 * width + cols + 128] = g_v.astype(BF16)
    unit, rstd = norm_parts(inputs)
    hidden = (unit * vec[0:1] + vec[1:2]).astype(BF16)
    gj = g_joint[...]
    g_qkv[...] += mm(hidden, gj, TN)
    g_vec[2:3] += jnp.sum(gj[:, 0:width].astype(F32), axis=0, keepdims=True)
    g_vec[3:4] += jnp.sum(gj[:, 2 * width :].astype(F32), axis=0, keepdims=True)
    g_hidden = mm(gj, w_qkv[...], NT)
    g_vec[0:1] += jnp.sum(g_hidden * unit, axis=0, keepdims=True)
    g_vec[1:2] += jnp.sum(g_hidden, axis=0, keepdims=True)
    g_in = g_attended + norm_back(g_hidden, unit, rstd, vec[0:1])
    g_images[0] = g_in[0:seq]


MESH = pl.DeviceIdType.MESH


def partners():
    e, w = lax.axis_index("expert"), lax.axis_index("wshard")
    return {
        "z": {"expert": lax.rem(e + 2, 8)},
        "z_back": {"expert": lax.rem(e + 6, 8)},
        "x": {"expert": e + 1 - 2 * lax.rem(e, 2)},
        "y": {"wshard": lax.rem(w + 2, 4)},
        "core": {"wshard": w + 1 - 2 * lax.rem(w, 2)},
    }


def meet(devices):
    barrier = pltpu.get_barrier_semaphore()
    for device in devices:
        pl.semaphore_signal(barrier, inc=1, device_id=device, device_id_type=MESH)
    pl.semaphore_wait(barrier, len(devices))


def sender(send, recv, slot, device, src, dst):
    return pltpu.make_async_remote_copy(
        src_ref=src,
        dst_ref=dst,
        send_sem=send.at[slot],
        recv_sem=recv.at[slot],
        device_id=device,
        device_id_type=MESH,
    )


def any_space():
    return pl.BlockSpec(memory_space=pl.ANY)


def gather_kernel(
    images, cotangent, slot_rows, w_qkv, w_out, small, e_in, e_out, e_bias,
    joint_o, weights_o, mixed_o, attended_o, routed_o, probs_o,
    cots_o, pieces_o, qkv_o, out_o, vec_o, router_o,
    rows, flat, placed, pack, qkv, out, smalls, vec, router, send, recv, local,
):
    step = pl.program_id(0)
    last = pl.num_programs(0) - 1
    w = lax.axis_index("wshard")
    to = partners()
    width = w_out.shape[1]
    cap = placed.shape[1]
    share = w_qkv.shape[0]
    w_core = w + 1 - 2 * lax.rem(w, 2)
    w_far = lax.rem(w + 2, 4)

    def rows_of(ref, which):
        return ref.at[pl.ds(pl.multiple_of(which * share, share), share)]

    dense = ((w_qkv, qkv, rows_of), (w_out, out, rows_of), (small, smalls, lambda r, i: r.at[i]))
    far = [sender(send, recv, i, to["y"], a, at(b, w)) for i, (a, b, at) in enumerate(dense)]
    near = [sender(send, recv, 3 + i, to["core"], a, at(b, w)) for i, (a, b, at) in enumerate(dense)]
    onward = [
        sender(send, recv, 6 + i, to["core"], at(b, w_far), at(b, w_far))
        for i, (a, b, at) in enumerate(dense)
    ]
    spread = [
        sender(send, recv, 9, to["z"], pack, pieces_o.at[4]),
        sender(send, recv, 10, to["y"], pack, pieces_o.at[2]),
        sender(send, recv, 11, to["core"], pack, pieces_o.at[1]),
    ]
    cots = [
        sender(send, recv, 12 + k, to["x"], placed.at[4 + k], cots_o.at[k, cap : 2 * cap])
        for k in range(4)
    ]
    kept = [
        pltpu.make_async_copy(placed.at[k], cots_o.at[k, 0:cap], local.at[k]) for k in range(4)
    ]
    saved = [
        pltpu.make_async_copy(qkv, qkv_o, local.at[4]),
        pltpu.make_async_copy(out, out_o, local.at[5]),
        pltpu.make_async_copy(pack, pieces_o.at[0], local.at[6]),
    ]

    @pl.when(step == 0)
    def _():
        meet(list(to.values()))
        for copy in far + near:
            copy.start()
        pack[0:width] = e_in[0]
        pack[width : 2 * width] = e_out[0]
        pack[2 * width : 2 * width + 16] = e_bias[...]
        for copy in spread:
            copy.start()
        mine = pl.ds(pl.multiple_of(w * share, share), share)
        qkv[mine] = w_qkv[...]
        out[mine] = w_out[...]
        smalls[w] = small[...]
        n, seq = cotangent.shape[:2]
        sp = flat.shape[0] // n
        for i in range(n):
            flat[(i + 1) * sp - 16 : (i + 1) * sp] = jnp.zeros((16, width), BF16)
            flat[i * sp : i * sp + seq] = cotangent[i]
        for k in range(4):
            placed[4 + k] = mm(hot_rows(slot_rows[4 + k], cap), flat[...]).astype(BF16)
            cots[k].start()
        for copy in far:
            copy.wait_recv()
        for copy in onward:
            copy.start()
        for k in range(4):
            placed[k] = mm(hot_rows(slot_rows[k], cap), flat[...]).astype(BF16)
            kept[k].start()
        for copy in near + onward:
            copy.wait_recv()
        for copy in far + near + onward:
            copy.wait_send()
        vec[...] = jnp.concatenate([smalls[i] for i in range(4)], axis=1).astype(F32)
        router[...] = jnp.zeros_like(router)
        router[0:8] = vec[8:16].astype(BF16)
        vec_o[...] = vec[...]
        router_o[...] = router[...]
        for copy in saved:
            copy.start()

    forward_kernel(
        images, qkv, out, vec, router, joint_o, weights_o, mixed_o, attended_o, routed_o,
        probs_o, rows,
    )

    @pl.when(step == last)
    def _():
        for copy in kept + saved:
            copy.wait()
        for copy in cots + spread:
            copy.wait()


def gather_forward(images, cotangent, slot_rows, w_qkv, w_out, small, e_in, e_out, e_bias, sp, cap):
    n, seq, width = images.shape
    piece = 2 * width + 16
    blocks = [
        jax.ShapeDtypeStruct((n, sp, 3 * width), BF16),
        jax.ShapeDtypeStruct((n, HEADS, sp, sp), BF16),
        jax.ShapeDtypeStruct((n, sp, width), BF16),
        jax.ShapeDtypeStruct((n, sp, width), F32),
        jax.ShapeDtypeStruct((n, sp, width), BF16),
        jax.ShapeDtypeStruct((n, sp, 128), F32),
    ]
    far = [
        jax.ShapeDtypeStruct((4, 2 * cap, width), BF16),
        jax.ShapeDtypeStruct((5, piece, width), BF16),
        jax.ShapeDtypeStruct((width, 3 * width), BF16),
        jax.ShapeDtypeStruct((width, width), BF16),
    ]
    small_shapes = [
        jax.ShapeDtypeStruct((16, width), F32),
        jax.ShapeDtypeStruct((128, width), BF16),
    ]
    return pl.pallas_call(
        gather_kernel,
        grid=(n,),
        in_specs=[part((seq, width))]
        + [
            whole(a.shape)
            for a in (cotangent, slot_rows, w_qkv, w_out, small, e_in, e_out, e_bias)
        ],
        out_specs=[part(s.shape[1:]) for s in blocks]
        + [any_space()] * 4
        + [whole(s.shape) for s in small_shapes],
        out_shape=blocks + far + small_shapes,
        scratch_shapes=[
            pltpu.VMEM((sp, width), F32),
            pltpu.VMEM((n * sp, width), BF16),
            pltpu.VMEM((8, cap, width), BF16),
            pltpu.VMEM((piece, width), BF16),
            pltpu.VMEM((width, 3 * width), BF16),
            pltpu.VMEM((width, width), BF16),
            pltpu.VMEM((4, 16, width // 4), BF16),
            pltpu.VMEM((16, width), F32),
            pltpu.VMEM((128, width), BF16),
            pltpu.SemaphoreType.DMA((16,)),
            pltpu.SemaphoreType.DMA((16,)),
            pltpu.SemaphoreType.DMA((7,)),
        ],
        compiler_params=pltpu.CompilerParams(
            dimension_semantics=("arbitrary",),
            vmem_limit_bytes=VMEM_LIMIT,
            collective_id=0,
            has_side_effects=True,
        ),
        cost_estimate=cost(2 * n * seq * width * width * 20, 40e6),
        name="gather_forward",
    )(images, cotangent, slot_rows, w_qkv, w_out, small, e_in, e_out, e_bias)


def add16(a, b):
    return (a.astype(F32) + b.astype(F32)).astype(BF16)


def once(shape):
    return pl.BlockSpec(shape, lambda *_: (0,) * len(shape), pipeline_mode=pl.Buffered(1))


def high_low(values, lane):
    high = values.astype(BF16).astype(F32)
    return jnp.where(lane == 0, high, jnp.where(lane == 1, values - high, 0.0)).astype(BF16)


def experts_kernel(
    slot_rows, routed, probs, cots, pieces,
    grows_o, ggs_o, answers_o, sent_o, own_o, far_o, far_in,
    weights, rows, gates, rows_s, gates_s, grad, core_in, ans_s, grow_s, ans_b, grow_b, gg_b,
    send, recv, local,
):
    k = pl.program_id(0)
    w = lax.axis_index("wshard")
    to = partners()
    cap = rows_s.shape[1]
    width = rows.shape[2]
    near, away = pl.ds(0, cap), pl.ds(cap, cap)

    def link(slot, device, src, dst):
        return sender(send, recv, slot, to[device], src, dst)

    loads = [
        pltpu.make_async_copy(pieces.at[i], weights.at[i // 4, i % 4], local.at[j])
        for j, i in enumerate((0, 1, 2, 4))
    ]
    ring = [
        link(0, "z", pieces.at[4], weights.at[2, 0]),
        link(1, "z", weights.at[2, 0], weights.at[3, 0]),
    ]
    held = [None, pieces.at[4], weights.at[2, 0], weights.at[3, 0]]
    beside = [None] + [link(1 + i, "core", held[i], weights.at[i, 1]) for i in (1, 2, 3)]
    across = [None] + [link(4 + i, "y", held[i], weights.at[i, 2]) for i in (1, 2, 3)]
    onward = [link(8, "core", pieces.at[2], weights.at[0, 3])] + [
        link(8 + i, "core", weights.at[i, 2], weights.at[i, 3]) for i in (1, 2, 3)
    ]
    rows_out = [link(12 + i, "x", rows_s.at[i], rows.at[i, away]) for i in range(4)]
    gates_out = [link(16 + i, "x", gates_s.at[i], gates.at[i, away]) for i in range(4)]
    slot = lax.rem(k, 2)
    grow_out = link(20 + k, "x", grow_b.at[k, away], grows_o.at[4 + k])
    gg_out = link(24 + k, "x", gg_b.at[k, away], ggs_o.at[4 + k])
    core_out = [
        link(28 + 2 * k + i, "core", grad.at[1 + 2 * i], core_in.at[slot, i]) for i in range(2)
    ]
    far_out = link(36, "y", far_o.at[1], far_in)

    def results(j):
        return [
            pltpu.make_async_copy(src, dst, local.at[4 + 6 * j + i])
            for i, (src, dst) in enumerate(
                (
                    (grow_b.at[j, near], grows_o.at[j]),
                    (gg_b.at[j, near], ggs_o.at[j]),
                    (ans_b.at[j, near], answers_o.at[j]),
                    (ans_b.at[j, away], sent_o.at[j]),
                    (grad.at[0], own_o.at[j]),
                    (grad.at[2], far_o.at[j]),
                )
            )
        ]

    @pl.when(k == 0)
    def _():
        for copy in loads:
            copy.start()
        meet(list(to.values()))
        for copy in (ring[0], across[1], beside[1], onward[0]):
            copy.start()
        lane = lax.broadcasted_iota(jnp.int32, (cap, 128), 1)
        high = probs[...].astype(BF16)
        low = (probs[...] - high.astype(F32)).astype(BF16)
        for r in (4, 5, 6, 7, 0, 1, 2, 3):
            hot = hot_rows(slot_rows[r], cap)
            placed = mm(hot, routed[...]).astype(BF16)
            gate = mm(hot, high) + mm(hot, low)
            gate = jnp.sum(jnp.where(lane == r, gate, 0.0), axis=1, keepdims=True)
            gate = high_low(gate, lane)
            if r >= 4:
                rows_s[r - 4] = placed
                gates_s[r - 4] = gate
                rows_out[r - 4].start()
                gates_out[r - 4].start()
            else:
                rows[r, 0:cap] = placed
                gates[r, 0:cap] = gate
        for copy in loads:
            copy.wait()
        onward[0].wait_recv()

    @pl.when(k == 1)
    def _():
        beside[1].wait_recv()
        onward[1].wait_recv()

    @pl.when(k == 2)
    def _():
        beside[2].wait_recv()
        onward[2].wait_recv()

    @pl.when(k == 3)
    def _():
        across[3].wait_recv()
        onward[3].start()
        beside[3].wait_recv()

    for i in range(4):

        @pl.when(k == i)
        def _(i=i):
            rows_out[i].wait_recv()
            gates_out[i].wait_recv()

    x = rows[k]
    cot = cots[k].astype(F32)
    gate = jnp.sum(gates[k].astype(F32), axis=1, keepdims=True)
    scaled = (cot * gate).astype(BF16)
    g_bias_out = jnp.sum(scaled.astype(F32), axis=0, keepdims=True)
    for turn, q in enumerate((1, 0, 3, 2)):
        if turn == 2:

            @pl.when(k == 3)
            def _():
                onward[3].wait_recv()

        w_in = weights[k, q, 0:width]
        w_out = weights[k, q, width : 2 * width]
        before = mm(x, w_in) + weights[k, q, 2 * width : 2 * width + 16].astype(F32)[0:1]
        square = before * before
        inner = before * (ROOT + ROOT * CUBE * square)
        curve = jnp.tanh(inner)
        half = 0.5 * curve + 0.5
        active = (before * half).astype(BF16)
        slope = half + (0.5 * before) * (1.0 - curve * curve) * (ROOT + 3.0 * ROOT * CUBE * square)
        grad_active = mm(scaled, w_out, NT)
        grad_before = (grad_active * slope).astype(BF16)
        if turn == 0:
            ans_s[...] = mm(active, w_out)
            grow_s[...] = mm(grad_before, w_in, NT)
        else:
            ans_s[...] += mm(active, w_out)
            grow_s[...] += mm(grad_before, w_in, NT)
        g_bias_in = jnp.sum(grad_before.astype(F32), axis=0, keepdims=True)
        tail = lax.broadcasted_iota(jnp.int32, (16, width), 0)

        @pl.when(k > 0)
        def _(q=q):
            if q % 2:
                link(28 + 2 * (k - 1) + q // 2, "core", grad.at[q], core_in.at[1 - slot, q // 2]).wait_send()
            else:
                results(k - 1)[4 + q // 2].wait()

        grad[q, 0:width] = mm(x, grad_before, TN).astype(BF16)
        grad[q, width : 2 * width] = mm(active, scaled, TN).astype(BF16)
        grad[q, 2 * width : 2 * width + 16] = jnp.where(
            tail == 0, g_bias_in, jnp.where(tail == 1, g_bias_out, 0.0)
        ).astype(BF16)
        if q % 2:
            core_out[q // 2].start()
        if turn == 1:

            @pl.when(k == 0)
            def _():
                ring[0].wait_recv()
                for copy in (ring[1], across[2], beside[2]):
                    copy.start()

        if turn == 3:

            @pl.when(k == 2)
            def _():
                far_out.start()

        if turn == 2:

            @pl.when(k == 0)
            def _():
                across[1].wait_recv()
                onward[1].start()

            @pl.when(k == 1)
            def _():
                ring[1].wait_recv()
                for copy in (across[3], beside[3]):
                    copy.start()
                across[2].wait_recv()
                onward[2].start()

    bias = []
    for j in range(4):
        q = lax.rem(j + w, 2) + 2 * lax.rem(j // 2 + w // 2, 2)
        bias.append(weights[k, q, 2 * width : 2 * width + 16, 0:128].astype(F32)[1:2])
    bias_out = jnp.concatenate(bias, axis=1)
    answer = (ans_s[...] + bias_out).astype(BF16).astype(F32)
    gg = jnp.sum(answer * cot, axis=1, keepdims=True)
    lane = lax.broadcasted_iota(jnp.int32, gg_b.shape[1:], 1)
    row = lax.broadcasted_iota(jnp.int32, gg_b.shape[1:], 0)
    own_lane = k + jnp.where(row >= cap, 4, 0)
    gg_b[k] = jnp.where(lane == own_lane, gg, 0.0).astype(BF16)
    grow_b[k] = grow_s[...].astype(BF16)
    grow_out.start()
    gg_out.start()
    ans_b[k] = (answer * gate).astype(BF16)
    for copy in core_out:
        copy.wait_recv()
    grad[0] = add16(grad[0], core_in[slot, 0])
    grad[2] = add16(grad[2], core_in[slot, 1])
    done = results(k)
    for copy in done:
        copy.start()

    @pl.when(k == 3)
    def _():
        for copy in core_out:
            copy.wait_send()
        done[4].wait()
        done[5].wait()
        for j in range(4):
            for copy in results(j)[:4]:
                copy.wait()
            for copy in (
                link(20 + j, "x", grow_b.at[j, away], grows_o.at[4 + j]),
                link(24 + j, "x", gg_b.at[j, away], ggs_o.at[4 + j]),
            ):
                copy.wait()
        for copy in ring + beside[1:] + across[1:] + onward + rows_out + gates_out:
            copy.wait_send()
        far_out.wait()


def run_experts(slot_rows, routed, probs, cots, pieces):
    _, both, width = cots.shape
    cap = both // 2
    piece = pieces.shape[1]
    shapes = [
        jax.ShapeDtypeStruct((8, cap, width), BF16),
        jax.ShapeDtypeStruct((8, cap, 128), BF16),
        jax.ShapeDtypeStruct((4, cap, width), BF16),
        jax.ShapeDtypeStruct((4, cap, width), BF16),
        jax.ShapeDtypeStruct((4, piece, width), BF16),
        jax.ShapeDtypeStruct((4, piece, width), BF16),
        jax.ShapeDtypeStruct((piece, width), BF16),
    ]
    return pl.pallas_call(
        experts_kernel,
        grid=(4,),
        in_specs=[once(a.shape) for a in (slot_rows, routed, probs, cots)] + [any_space()],
        out_specs=[any_space()] * len(shapes),
        out_shape=shapes,
        scratch_shapes=[
            pltpu.VMEM((4, 4, piece, width), BF16),
            pltpu.VMEM((4, both, width), BF16),
            pltpu.VMEM((4, both, 128), BF16),
            pltpu.VMEM((4, cap, width), BF16),
            pltpu.VMEM((4, cap, 128), BF16),
            pltpu.VMEM((4, piece, width), BF16),
            pltpu.VMEM((2, 2, piece, width), BF16),
            pltpu.VMEM((both, width), F32),
            pltpu.VMEM((both, width), F32),
            pltpu.VMEM((4, both, width), BF16),
            pltpu.VMEM((4, both, width), BF16),
            pltpu.VMEM((4, both, 128), BF16),
            pltpu.SemaphoreType.DMA((37,)),
            pltpu.SemaphoreType.DMA((37,)),
            pltpu.SemaphoreType.DMA((28,)),
        ],
        compiler_params=pltpu.CompilerParams(
            dimension_semantics=("arbitrary",),
            vmem_limit_bytes=62 * 1024 * 1024,
            collective_id=1,
            has_side_effects=True,
        ),
        cost_estimate=cost(2 * 2 * cap * width * width * 4 * 6 * 4, 60e6),
        name="run_experts",
    )(slot_rows, routed, probs, cots, pieces)


def backward_all_kernel(
    count, images, cotangent, joint, weights, mixed, attended, routed, probs, slots,
    w_qkv, w_out, vec, router, grows, ggs, answers_l, answers_s, own, far, far_in,
    output, g_images, g_qkv_o, g_out_o, g_small_o, e_in_o, e_out_o, e_bias_o,
    rows, cots, g_joint, g_qkv, g_out, g_vec, g_rows, answers_r, mine, far_got, ring_got, passing,
    dense, core_got, y_got, ours, chunk_got, chunk_all, send, recv, local,
):
    step = pl.program_id(0)
    n = pl.num_programs(0) // 2
    e, w = lax.axis_index("expert"), lax.axis_index("wshard")
    to = partners()
    peers = [{"expert": lax.rem(e + d, 8)} for d in range(1, 8)]
    width = w_out.shape[0]
    piece = mine.shape[1]
    quarter = width // 4
    wide = dense.shape[2]
    block = wide // 8
    w_core = w + 1 - 2 * lax.rem(w, 2)
    w_far = lax.rem(w + 2, 4)
    w_last = lax.rem(w_core + 2, 4)

    def load(j):
        src, dst = [(own.at[i], mine.at[i]) for i in range(4)][j] if j < 4 else (far_in, far_got.at[1])
        return pltpu.make_async_copy(src, dst, local.at[j])

    def answer(k):
        return sender(send, recv, k, to["x"], answers_s.at[k], answers_r.at[k])

    def beyond(k):
        return sender(send, recv, 4 + k, to["y"], far.at[k], far_got.at[k])

    def ring(k):
        return sender(send, recv, 8 + k, to["z"], passing.at[k], ring_got.at[k])

    def core(i):
        return sender(send, recv, 12 + i, to["core"], dense.at[(w_core, w_last)[i]], core_got.at[i])

    def y_side():
        return sender(send, recv, 14, to["y"], dense.at[w_far], y_got)

    def scatter(d):
        src = ours.at[:, pl.ds(pl.multiple_of(lax.rem(e + d, 8) * block, block), block)]
        return sender(send, recv, 14 + d, peers[d - 1], src, chunk_got.at[d - 1])

    def share(d):
        return sender(send, recv, 21 + d, peers[d - 1], chunk_all.at[e], chunk_all.at[e])

    @pl.when(step == 0)
    def _():
        g_qkv[...] = jnp.zeros_like(g_qkv)
        g_out[...] = jnp.zeros_like(g_out)
        g_vec[...] = jnp.zeros_like(g_vec)
        dense[:, quarter : quarter + 16] = jnp.zeros((4, 16, wide), BF16)
        for j in range(5):
            load(j).start()
        meet([to["y"], to["core"]] + peers)
        for k in range(4):
            answer(k).start()
        for k in (2, 3):
            beyond(k).start()
        for j in range(5):
            load(j).wait()
        passing[1] = add16(mine[1], far_got[1])
        ring(1).start()

    for k, at in ((2, n // 2), (3, n)):

        @pl.when(step == at)
        def _(k=k):
            beyond(k).wait_recv()
            ring(k - 1).wait_recv()
            total = mine[k].astype(F32) + far_got[k].astype(F32) + ring_got[k - 1].astype(F32)
            passing[k] = total.astype(BF16)
            ring(k).start()

    @pl.when(step < n)
    def _():
        backward_kernel(
            step, count, images, cotangent, joint, weights, mixed, attended, routed, probs, slots,
            w_qkv, w_out, vec, router, grows, ggs, g_images, g_qkv, g_out, g_vec, rows, cots, g_joint,
        )

    @pl.when(step == n - 1)
    def _():
        g_rows[0:8] = g_vec[0:8]
        for r in range(8):
            expert = lax.rem(e + 8 - 2 * (r % 4), 8)
            expert = expert if r < 4 else expert + 1 - 2 * lax.rem(expert, 2)
            g_rows[pl.ds(8 + expert, 1)] = g_vec[8 + r : 9 + r]
        for j in range(4):
            band = slice(j * quarter, (j + 1) * quarter)
            dense[j, 0:quarter, 0 : 3 * width] = g_qkv[band].astype(BF16)
            dense[j, 0:quarter, 3 * width :] = g_out[band].astype(BF16)
            dense[j, quarter : quarter + 16, 0:quarter] = g_rows[:, band].astype(BF16)
        for i in range(2):
            core(i).start()

    @pl.when(step == n + 1)
    def _():
        for i in range(2):
            core(i).wait()
        dense[w_far] = add16(dense[w_far], core_got[1])
        y_side().start()
        beyond(0).start()
        ours[...] = add16(dense[w], core_got[0])

    @pl.when(step == n)
    def _():
        for k in range(4):
            answer(k).wait_recv()

    @pl.when(step >= n)
    def _():
        output_kernel(step - n, count, slots, attended, answers_l, answers_r, output)

    @pl.when(step == 2 * n - 1)
    def _():
        y_side().wait()
        ours[...] = add16(ours[...], y_got[...])
        for d in range(1, 8):
            scatter(d).start()
        ring(3).wait_recv()
        beyond(0).wait_recv()
        for d in range(1, 8):
            scatter(d).wait_recv()
        total = ours[:, pl.ds(pl.multiple_of(e * block, block), block)].astype(F32)
        for d in range(1, 8):
            total = total + chunk_got[d - 1].astype(F32)
        chunk_all[e] = total.astype(BF16)
        for d in range(1, 8):
            share(d).start()
        total = mine[0].astype(F32) + far_got[0].astype(F32) + ring_got[3].astype(F32)
        e_in_o[0] = total[0:width]
        e_out_o[0] = total[width : 2 * width]
        e_bias_o[...] = total[2 * width : 2 * width + 16]
        for d in range(1, 8):
            share(d).wait_recv()
        for i in range(8):
            part_of = chunk_all[i].astype(F32)
            if i < 6:
                g_qkv_o[:, i * block : (i + 1) * block] = part_of[0:quarter]
            else:
                g_out_o[:, (i - 6) * block : (i - 5) * block] = part_of[0:quarter]
            if i == 0:
                g_small_o[...] = part_of[quarter : quarter + 16, 0:quarter]
        for d in range(1, 8):
            scatter(d).wait_send()
            share(d).wait_send()
        for k in range(4):
            answer(k).wait_send()
        for k in (2, 3, 0):
            beyond(k).wait_send()
        for k in (1, 2, 3):
            ring(k).wait_send()


def backward_all(
    count, images, cotangent, joint, weights, mixed, attended, routed, probs, slots,
    w_qkv, w_out, vec, router, grows, ggs, answers_l, answers_s, own, far, far_in,
):
    n, seq, width = images.shape
    sp = joint.shape[1]
    cap = grows.shape[1]
    piece = own.shape[1]
    quarter = width // 4
    wide = 4 * width
    block = wide // 8

    def early(shape):
        return pl.BlockSpec((1,) + shape, lambda i: (jnp.minimum(i, n - 1),) + (0,) * len(shape))

    def both(shape):
        return pl.BlockSpec((1,) + shape, lambda i: (lax.rem(i, n),) + (0,) * len(shape))

    def late(shape):
        return pl.BlockSpec((1,) + shape, lambda i: (jnp.maximum(i - n, 0),) + (0,) * len(shape))

    streams = [
        (images, early), (cotangent, early), (joint, early), (weights, early), (mixed, early),
        (attended, both), (routed, early), (probs, early), (slots, both),
    ]
    fixed = [w_qkv, w_out, vec, router, grows, ggs, answers_l]
    far_refs = [answers_s, own, far, far_in]
    shapes = [
        jax.ShapeDtypeStruct((n, seq, width), BF16),
        jax.ShapeDtypeStruct((n, seq, width), F32),
        jax.ShapeDtypeStruct((quarter, 3 * width), F32),
        jax.ShapeDtypeStruct((quarter, width), F32),
        jax.ShapeDtypeStruct((16, quarter), F32),
        jax.ShapeDtypeStruct((1, width, width), F32),
        jax.ShapeDtypeStruct((1, width, width), F32),
        jax.ShapeDtypeStruct((16, width), F32),
    ]
    band = (quarter + 16, wide)
    return pl.pallas_call(
        backward_all_kernel,
        grid=(2 * n,),
        in_specs=[pl.BlockSpec(memory_space=pltpu.SMEM)]
        + [kind(a.shape[1:]) for a, kind in streams]
        + [once(a.shape) for a in fixed]
        + [any_space()] * len(far_refs),
        out_specs=[late((seq, width)), early((seq, width))] + [whole(s.shape) for s in shapes[2:]],
        out_shape=shapes,
        scratch_shapes=[
            pltpu.VMEM((sp, width), F32),
            pltpu.VMEM((sp, width), F32),
            pltpu.VMEM((sp, 3 * width), BF16),
            pltpu.VMEM((width, 3 * width), F32),
            pltpu.VMEM((width, width), F32),
            pltpu.VMEM((16, width), F32),
            pltpu.VMEM((16, width), F32),
            pltpu.VMEM((4, cap, width), BF16),
            pltpu.VMEM((4, piece, width), BF16),
            pltpu.VMEM((4, piece, width), BF16),
            pltpu.VMEM((4, piece, width), BF16),
            pltpu.VMEM((4, piece, width), BF16),
            pltpu.VMEM((4,) + band, BF16),
            pltpu.VMEM((2,) + band, BF16),
            pltpu.VMEM(band, BF16),
            pltpu.VMEM(band, BF16),
            pltpu.VMEM((7, quarter + 16, block), BF16),
            pltpu.VMEM((8, quarter + 16, block), BF16),
            pltpu.SemaphoreType.DMA((29,)),
            pltpu.SemaphoreType.DMA((29,)),
            pltpu.SemaphoreType.DMA((5,)),
        ],
        compiler_params=pltpu.CompilerParams(
            dimension_semantics=("arbitrary",),
            vmem_limit_bytes=62 * 1024 * 1024,
            collective_id=2,
            has_side_effects=True,
        ),
        cost_estimate=cost(2 * n * seq * width * width * 30, 40e6),
        name="backward_all",
    )(count, *[a for a, _ in streams], *fixed, *far_refs)


def weight_body(
    images, cotangent, image_count, routes, attn_norm_gain, attn_norm_bias, w_qkv, b_query,
    b_value, w_attn_out, b_attn_out, moe_norm_gain, moe_norm_bias, w_router, expert_in,
    expert_in_bias, expert_out, expert_out_bias,
):
    n, seq, width = images.shape
    sp = -(-seq // 16) * 16
    experts = lax.axis_size("expert")
    capacity = (2 * n * seq + experts - 1) // experts
    cap = -(-capacity // 16) * 16
    shard = lax.axis_index("wshard")
    place = lax.axis_index("expert")
    near = jnp.stack([(place - 2 * k) % 8 for k in range(4)])
    order = jnp.concatenate([near, near ^ 1])

    vectors = jnp.stack(
        [attn_norm_gain, attn_norm_bias, b_query, b_value, b_attn_out, moe_norm_gain, moe_norm_bias]
    )
    small = jnp.concatenate([jnp.pad(vectors, ((0, 1), (0, 0))), w_router.T[order]])
    e_bias = jnp.concatenate(
        [
            expert_in_bias,
            jnp.pad(expert_out_bias, ((0, 0), (0, width - expert_out_bias.shape[1]))),
            jnp.zeros((14, width), BF16),
        ]
    )

    live = jnp.arange(n, dtype=jnp.int32) < image_count[0]
    member = (routes[:, :, 0:1] == order) | (routes[:, :, 1:2] == order)
    member = (member & live[:, None, None]).astype(BF16)
    lower = jnp.tril(jnp.ones((seq, seq), BF16), -1)
    earlier = jnp.einsum("ts,ise->ite", lower, member, preferred_element_type=F32)
    counts = jnp.sum(member.astype(F32), axis=1)
    base = jnp.cumsum(counts, axis=0) - counts
    position = (earlier + base[:, None, :]).astype(jnp.int32)
    slots = jnp.where((member > 0) & (position < capacity), position, -1)
    slots = jnp.pad(slots, ((0, 0), (0, sp - seq), (0, 0)), constant_values=-1)
    slot_rows = slots.transpose(2, 0, 1).reshape(8, 1, n * sp)

    (
        joint, weights, mixed, attended, routed, probs,
        cots, pieces, w_qkv_full, w_out_full, vec, router,
    ) = gather_forward(
        images, cotangent, slot_rows, w_qkv, w_attn_out, small, expert_in, expert_out, e_bias, sp, cap
    )
    grows, ggs, answers_l, answers_s, g_own, g_far, far_in = run_experts(
        slot_rows, routed.reshape(n * sp, width), probs.reshape(n * sp, 128), cots, pieces
    )
    output, grad_images, g_qkv, g_out, g_small, e_in, e_out, e_bias = backward_all(
        image_count, images, cotangent, joint, weights, mixed, attended, routed, probs, slots,
        w_qkv_full, w_out_full, vec, router, grows, ggs, answers_l, answers_s, g_own, g_far, far_in,
    )
    quarter = width // 4
    g_bias_out = lax.dynamic_slice_in_dim(e_bias[1:2], shard * quarter, quarter, 1)
    return (
        output,
        grad_images,
        g_small[0],
        g_small[1],
        g_qkv,
        g_small[2],
        g_small[3],
        g_out,
        g_small[4],
        g_small[5],
        g_small[6],
        g_small[8:16].T,
        e_in,
        e_bias[0:1],
        e_out,
        g_bias_out,
    )


def solution(mesh):
    in_specs = (
        P(("expert", "wshard"), None, None),
        P(("expert", "wshard"), None, None),
        P(("expert", "wshard")),
        P(("expert", "wshard"), None, None),
        P("wshard"),
        P("wshard"),
        P("wshard", None),
        P("wshard"),
        P("wshard"),
        P("wshard", None),
        P("wshard"),
        P("wshard"),
        P("wshard"),
        P("wshard", None),
        P("expert", None, "wshard"),
        P("expert", "wshard"),
        P("expert", "wshard", None),
        P("expert", "wshard"),
    )
    out_specs = (
        P(("expert", "wshard"), None, None),
        P(("expert", "wshard"), None, None),
        P("wshard"),
        P("wshard"),
        P("wshard", None),
        P("wshard"),
        P("wshard"),
        P("wshard", None),
        P("wshard"),
        P("wshard"),
        P("wshard"),
        P("wshard", None),
        P("expert", None, "wshard"),
        P("expert", "wshard"),
        P("expert", "wshard", None),
        P("expert", "wshard"),
    )
    small_slice = mesh.shape["expert"] == 8 and mesh.shape["wshard"] == 4
    body = weight_body if small_slice else token_body
    return jax.shard_map(body, mesh=mesh, in_specs=in_specs, out_specs=out_specs, check_vma=False)
```

```python
import functools

import jax
import jax.numpy as jnp
from jax import lax
from jax.experimental import pallas as pl
from jax.experimental.pallas import tpu as pltpu
from jax.sharding import PartitionSpec as P

HEADS = 8


norm_eps = 1e-06


def layer_norm(values, gain, bias):
    centre = values - jnp.mean(values, axis=-1, keepdims=True)
    spread = jnp.mean(centre * centre, axis=-1, keepdims=True)
    return centre * lax.rsqrt(spread + norm_eps) * gain + bias


def take_share(full, shard_index, shard_count):
    piece = full.shape[0] // shard_count
    return lax.dynamic_slice_in_dim(full, shard_index * piece, piece, 0)


def place_rows(slot_index, rows_here, total_slots):
    buffer = (
        jnp.zeros((total_slots + 1, rows_here.shape[1]), rows_here.dtype)
        .at[slot_index]
        .set(rows_here)
    )
    return buffer[:total_slots]


def token_body(
    images,
    cotangent,
    image_count,
    routes,
    attn_norm_gain,
    attn_norm_bias,
    w_qkv,
    b_query,
    b_value,
    w_attn_out,
    b_attn_out,
    moe_norm_gain,
    moe_norm_bias,
    w_router,
    expert_in,
    expert_in_bias,
    expert_out,
    expert_out_bias,
):
    image_slots, seq_len, model_width = images.shape
    tok_count = image_slots * seq_len
    experts = lax.axis_size("expert")
    shard_count = lax.axis_size("wshard")
    shard_index = lax.axis_index("wshard")
    capacity = (2 * tok_count + experts - 1) // experts
    total_slots = experts * capacity
    head_dim = model_width // HEADS
    score_scale = head_dim ** (-0.5)
    gathered = (
        lax.all_gather(attn_norm_gain, "wshard", axis=0, tiled=True),
        lax.all_gather(attn_norm_bias, "wshard", axis=0, tiled=True),
        lax.all_gather(w_qkv, "wshard", axis=0, tiled=True),
        lax.all_gather(b_query, "wshard", axis=0, tiled=True),
        lax.all_gather(b_value, "wshard", axis=0, tiled=True),
        lax.all_gather(w_attn_out, "wshard", axis=0, tiled=True),
        lax.all_gather(b_attn_out, "wshard", axis=0, tiled=True),
        lax.all_gather(moe_norm_gain, "wshard", axis=0, tiled=True),
        lax.all_gather(moe_norm_bias, "wshard", axis=0, tiled=True),
        lax.all_gather(w_router, "wshard", axis=0, tiled=True),
    )
    gain_one = gathered[0].astype(jnp.float32)
    bias_one = gathered[1].astype(jnp.float32)
    query_key_value_weight = gathered[2]
    query_bias = gathered[3].astype(jnp.float32)
    value_bias = gathered[4].astype(jnp.float32)
    projection_weight = gathered[5]
    projection_bias = gathered[6].astype(jnp.float32)
    gain_two = gathered[7].astype(jnp.float32)
    bias_two = gathered[8].astype(jnp.float32)
    router_weight = gathered[9]
    live_tokens = jnp.repeat(
        (jnp.arange(image_slots, dtype=jnp.int32) < image_count[0]).astype(jnp.float32), seq_len
    )
    inputs = images.astype(jnp.float32).reshape(tok_count, model_width)
    normed_one, norm_one_back = jax.vjp(layer_norm, inputs, gain_one, bias_one)
    hidden_state = normed_one.astype(jnp.bfloat16)
    merged_bias = jnp.concatenate([query_bias, jnp.zeros((model_width,), jnp.float32), value_bias])
    merged_rows = (
        jnp.dot(hidden_state, query_key_value_weight, preferred_element_type=jnp.float32)
        + merged_bias
    ).astype(jnp.bfloat16)
    queries = merged_rows[:, :model_width].reshape(image_slots, seq_len, HEADS, head_dim)
    key_rows = merged_rows[:, model_width : 2 * model_width].reshape(
        image_slots, seq_len, HEADS, head_dim
    )
    value_rows = merged_rows[:, 2 * model_width :].reshape(image_slots, seq_len, HEADS, head_dim)
    scores = (
        jnp.einsum("slhc,smhc->shlm", queries, key_rows, preferred_element_type=jnp.float32)
        * score_scale
    )
    log_total = jax.nn.logsumexp(scores, axis=-1, keepdims=True)
    weights = jnp.exp(scores - log_total).astype(jnp.bfloat16)
    blended_rows = (
        jnp.einsum("shlm,smhc->slhc", weights, value_rows, preferred_element_type=jnp.float32)
        .astype(jnp.bfloat16)
        .reshape(tok_count, model_width)
    )
    attended = (
        inputs
        + jnp.dot(blended_rows, projection_weight, preferred_element_type=jnp.float32)
        + projection_bias
    )
    normed_two, norm_two_back = jax.vjp(layer_norm, attended, gain_two, bias_two)
    routed = normed_two.astype(jnp.bfloat16)
    logits = jnp.dot(routed, router_weight, preferred_element_type=jnp.float32)
    router_probs = jax.nn.softmax(logits, axis=-1)
    route_pairs = routes.reshape(tok_count, 2)
    gate_values = jnp.take_along_axis(router_probs, route_pairs, axis=1)
    pair_expert = route_pairs.reshape(2 * tok_count)
    pair_live = jnp.repeat(live_tokens, 2) > 0.5
    onehot = (
        (pair_expert[:, None] == jnp.arange(experts, dtype=jnp.int32)[None, :]) & pair_live[:, None]
    ).astype(jnp.int32)
    earlier = jnp.cumsum(onehot, axis=0) - onehot
    position = jnp.sum(earlier * onehot, axis=1)
    keeping = pair_live & (position < capacity)
    slot_index = jnp.where(keeping, pair_expert * capacity + position, total_slots)
    outgoing = place_rows(slot_index, jnp.repeat(routed, 2, axis=0), total_slots).reshape(
        experts, capacity, model_width
    )
    arrived = lax.all_to_all(outgoing, "expert", split_axis=0, concat_axis=0, tiled=True).reshape(
        total_slots, model_width
    )
    full_in, full_in_bias, full_out, full_out_bias = (
        lax.all_gather(expert_in, "wshard", axis=2, tiled=True),
        lax.all_gather(expert_in_bias, "wshard", axis=1, tiled=True),
        lax.all_gather(expert_out, "wshard", axis=1, tiled=True),
        lax.all_gather(expert_out_bias, "wshard", axis=1, tiled=True),
    )
    full_in = full_in[0]
    full_out = full_out[0]
    before = jnp.dot(arrived, full_in, preferred_element_type=jnp.float32) + full_in_bias[0].astype(
        jnp.float32
    )
    active, gelu_back = jax.vjp(jax.nn.gelu, before)
    active = active.astype(jnp.bfloat16)
    leaving = (
        jnp.dot(active, full_out, preferred_element_type=jnp.float32)
        + full_out_bias[0].astype(jnp.float32)
    ).astype(jnp.bfloat16)
    coming_back = lax.all_to_all(
        leaving.reshape(experts, capacity, model_width),
        "expert",
        split_axis=0,
        concat_axis=0,
        tiled=True,
    )
    padded = jnp.concatenate(
        [coming_back.reshape(total_slots, model_width), jnp.zeros((1, model_width), jnp.bfloat16)],
        axis=0,
    )
    picked = padded[slot_index].reshape(tok_count, 2, model_width).astype(jnp.float32)
    combined = jnp.sum(gate_values[:, :, None] * picked, axis=1)
    output = (
        ((attended + combined) * live_tokens[:, None])
        .astype(jnp.bfloat16)
        .reshape(image_slots, seq_len, model_width)
    )
    grad_out = cotangent.astype(jnp.float32).reshape(tok_count, model_width) * live_tokens[:, None]
    grad_gates = jnp.einsum("td,tkd->tk", grad_out, picked)
    pair_grads = (
        (gate_values[:, :, None] * grad_out[:, None, :])
        .reshape(2 * tok_count, model_width)
        .astype(jnp.bfloat16)
    )
    outgoing_grads = place_rows(slot_index, pair_grads, total_slots).reshape(
        experts, capacity, model_width
    )
    arrived_grads = lax.all_to_all(
        outgoing_grads, "expert", split_axis=0, concat_axis=0, tiled=True
    ).reshape(total_slots, model_width)
    grad_active = jnp.einsum(
        "rd,hd->rh", arrived_grads, full_out, preferred_element_type=jnp.float32
    )
    grad_before = gelu_back(grad_active)[0].astype(jnp.bfloat16)
    grad_full_out = jnp.einsum(
        "rh,rd->hd", active, arrived_grads, preferred_element_type=jnp.float32
    )
    grad_full_out_bias = jnp.sum(arrived_grads.astype(jnp.float32), axis=0)
    grad_full_in = jnp.einsum("rd,rh->dh", arrived, grad_before, preferred_element_type=jnp.float32)
    grad_full_in_bias = jnp.sum(grad_before.astype(jnp.float32), axis=0)
    grad_arrived = jnp.einsum(
        "rh,dh->rd", grad_before, full_in, preferred_element_type=jnp.float32
    ).astype(jnp.bfloat16)
    expert_grads = (
        lax.psum_scatter(grad_full_in[None], "wshard", scatter_dimension=2, tiled=True),
        lax.psum_scatter(grad_full_in_bias[None], "wshard", scatter_dimension=1, tiled=True),
        lax.psum_scatter(grad_full_out[None], "wshard", scatter_dimension=1, tiled=True),
        lax.psum_scatter(grad_full_out_bias[None], "wshard", scatter_dimension=1, tiled=True),
    )
    returned_grads = lax.all_to_all(
        grad_arrived.reshape(experts, capacity, model_width),
        "expert",
        split_axis=0,
        concat_axis=0,
        tiled=True,
    )
    padded_grads = jnp.concatenate(
        [
            returned_grads.reshape(total_slots, model_width),
            jnp.zeros((1, model_width), jnp.bfloat16),
        ],
        axis=0,
    )
    grad_routed = jnp.sum(
        padded_grads[slot_index].reshape(tok_count, 2, model_width).astype(jnp.float32), axis=1
    )
    route_onehot = (
        route_pairs[:, :, None] == jnp.arange(experts, dtype=jnp.int32)[None, None, :]
    ).astype(jnp.float32)
    grad_probs = jnp.einsum("tk,tke->te", grad_gates, route_onehot)
    grad_logits = (
        router_probs * (grad_probs - jnp.sum(router_probs * grad_probs, axis=-1, keepdims=True))
    ).astype(jnp.bfloat16)
    grad_router = jnp.einsum("td,te->de", routed, grad_logits, preferred_element_type=jnp.float32)
    grad_routed = grad_routed + jnp.einsum(
        "te,de->td", grad_logits, router_weight, preferred_element_type=jnp.float32
    )
    grad_attended, grad_gain_two, grad_bias_two = norm_two_back(grad_routed)
    grad_attended = grad_attended + grad_out
    grad_branch = grad_attended.astype(jnp.bfloat16)
    grad_proj = jnp.einsum(
        "td,te->de", blended_rows, grad_branch, preferred_element_type=jnp.float32
    )
    grad_proj_bias = jnp.sum(grad_branch.astype(jnp.float32), axis=0)
    grad_mixed = (
        jnp.einsum("te,de->td", grad_branch, projection_weight, preferred_element_type=jnp.float32)
        .astype(jnp.bfloat16)
        .reshape(image_slots, seq_len, HEADS, head_dim)
    )
    scores_again = (
        jnp.einsum("slhc,smhc->shlm", queries, key_rows, preferred_element_type=jnp.float32)
        * score_scale
    )
    probs_again = jnp.exp(scores_again - log_total)
    grad_weights = jnp.einsum(
        "slhc,smhc->shlm", grad_mixed, value_rows, preferred_element_type=jnp.float32
    )
    grad_values = jnp.einsum(
        "shlm,slhc->smhc", weights, grad_mixed, preferred_element_type=jnp.float32
    )
    grad_scores = (
        probs_again * (grad_weights - jnp.sum(probs_again * grad_weights, axis=-1, keepdims=True))
    ).astype(jnp.bfloat16)
    grad_queries = (
        jnp.einsum("shlm,smhc->slhc", grad_scores, key_rows, preferred_element_type=jnp.float32)
        * score_scale
    )
    grad_keys = (
        jnp.einsum("shlm,slhc->smhc", grad_scores, queries, preferred_element_type=jnp.float32)
        * score_scale
    )
    grad_joint = jnp.concatenate(
        [
            grad_queries.reshape(tok_count, model_width),
            grad_keys.reshape(tok_count, model_width),
            grad_values.reshape(tok_count, model_width),
        ],
        axis=1,
    ).astype(jnp.bfloat16)
    grad_qkv = jnp.einsum("td,te->de", hidden_state, grad_joint, preferred_element_type=jnp.float32)
    grad_query_bias = jnp.sum(grad_joint[:, :model_width].astype(jnp.float32), axis=0)
    grad_value_bias = jnp.sum(grad_joint[:, 2 * model_width :].astype(jnp.float32), axis=0)
    grad_hidden = jnp.einsum(
        "te,de->td", grad_joint, query_key_value_weight, preferred_element_type=jnp.float32
    )
    grad_inputs, grad_gain_one, grad_bias_one = norm_one_back(grad_hidden)
    grad_images = (grad_attended + grad_inputs).reshape(image_slots, seq_len, model_width)
    full_grads = (
        grad_gain_one,
        grad_bias_one,
        grad_qkv,
        grad_query_bias,
        grad_value_bias,
        grad_proj,
        grad_proj_bias,
        grad_gain_two,
        grad_bias_two,
        grad_router,
    )
    total_grads = lax.psum(
        (
            full_grads[0],
            full_grads[1],
            full_grads[2],
            full_grads[3],
            full_grads[4],
            full_grads[5],
            full_grads[6],
            full_grads[7],
            full_grads[8],
            full_grads[9],
        ),
        ("expert", "wshard"),
    )
    final_grads = tuple((take_share(item, shard_index, shard_count) for item in total_grads))
    return (
        output,
        grad_images,
        final_grads[0],
        final_grads[1],
        final_grads[2],
        final_grads[3],
        final_grads[4],
        final_grads[5],
        final_grads[6],
        final_grads[7],
        final_grads[8],
        final_grads[9],
        expert_grads[0],
        expert_grads[1],
        expert_grads[2],
        expert_grads[3],
    )


F32 = jnp.float32
BF16 = jnp.bfloat16
VMEM_LIMIT = 56 * 1024 * 1024
NN = (((1,), (0,)), ((), ()))
NT = (((1,), (1,)), ((), ()))
TN = (((0,), (0,)), ((), ()))
ROUTER_ROW = 8


def mm(a, b, dims=NN):
    return lax.dot_general(a, b, dims, preferred_element_type=F32)


def whole(shape):
    return pl.BlockSpec(shape, lambda *_: (0,) * len(shape))


def part(shape):
    return pl.BlockSpec((1,) + shape, lambda i: (i,) + (0,) * len(shape))


def params(*semantics):
    return pltpu.CompilerParams(
        dimension_semantics=semantics or None, vmem_limit_bytes=VMEM_LIMIT
    )


def cost(flops, nbytes):
    return pl.CostEstimate(flops=int(flops), bytes_accessed=int(nbytes), transcendentals=0)


def norm_parts(values):
    centre = values - jnp.mean(values, axis=-1, keepdims=True)
    rstd = lax.rsqrt(jnp.mean(centre * centre, axis=-1, keepdims=True) + norm_eps)
    return centre * rstd, rstd


def norm_back(grad, unit, rstd, gain):
    scaled = grad * gain
    return rstd * (
        scaled
        - jnp.mean(scaled, axis=-1, keepdims=True)
        - unit * jnp.mean(scaled * unit, axis=-1, keepdims=True)
    )


def padded_rows(ref, scratch):
    seq, rows = ref.shape[1], scratch.shape[0]
    scratch[rows - 16 : rows] = jnp.zeros((16, scratch.shape[1]), scratch.dtype)
    scratch[0:seq] = ref[0].astype(scratch.dtype)
    return scratch[...]


def half_mask(rows, half):
    return (lax.broadcasted_iota(jnp.int32, (rows, 128), 1) // 64) == half


def forward_kernel(
    images, w_qkv, w_out, vec, router, joint_o, weights_o, mixed_o, attended_o, routed_o, probs_o, rows
):
    seq, width = images.shape[1:]
    inputs = padded_rows(images, rows)
    sp = rows.shape[0]
    unit, _ = norm_parts(inputs)
    hidden = (unit * vec[0:1] + vec[1:2]).astype(BF16)
    bias = jnp.concatenate([vec[2:3], jnp.zeros((1, width), F32), vec[3:4]], axis=1)
    joint_o[0] = (mm(hidden, w_qkv[...]) + bias).astype(BF16)
    scale = (width // HEADS) ** (-0.5)
    key_ok = lax.broadcasted_iota(jnp.int32, (sp, sp), 1) < seq
    for pair in range(HEADS // 2):
        cols = pair * 128
        q = joint_o[0, :, cols : cols + 128]
        k = joint_o[0, :, width + cols : width + cols + 128]
        v = joint_o[0, :, 2 * width + cols : 2 * width + cols + 128]
        total = jnp.zeros((sp, 128), F32)
        for half in range(2):
            sel = half_mask(sp, half)
            km = jnp.where(sel, k, 0)
            vm = jnp.where(sel, v, 0)
            scores = mm(q, km, NT) * scale
            scores = jnp.where(key_ok, scores, -1e30)
            top = jnp.max(scores, axis=-1, keepdims=True)
            power = jnp.exp(scores - top)
            weights = (power / jnp.sum(power, axis=-1, keepdims=True)).astype(BF16)
            weights_o[0, pair * 2 + half] = weights
            total = total + mm(weights, vm)
        mixed_o[0, :, cols : cols + 128] = total.astype(BF16)
    attended = inputs + mm(mixed_o[0], w_out[...]) + vec[4:5]
    attended_o[0] = attended
    unit, _ = norm_parts(attended)
    routed = (unit * vec[5:6] + vec[6:7]).astype(BF16)
    routed_o[0] = routed
    logits = mm(routed, router[...], NT)
    experts = HEADS
    logits = jnp.where(
        lax.broadcasted_iota(jnp.int32, (sp, 128), 1) < experts, logits, -1e30
    )
    power = jnp.exp(logits - jnp.max(logits, axis=-1, keepdims=True))
    probs_o[0] = power / jnp.sum(power, axis=-1, keepdims=True)


def attention_forward(images, w_qkv, w_out, vec, router, sp):
    n, seq, width = images.shape
    shapes = [
        jax.ShapeDtypeStruct((n, sp, 3 * width), BF16),
        jax.ShapeDtypeStruct((n, HEADS, sp, sp), BF16),
        jax.ShapeDtypeStruct((n, sp, width), BF16),
        jax.ShapeDtypeStruct((n, sp, width), F32),
        jax.ShapeDtypeStruct((n, sp, width), BF16),
        jax.ShapeDtypeStruct((n, sp, 128), F32),
    ]
    return pl.pallas_call(
        forward_kernel,
        grid=(n,),
        in_specs=[
            part((seq, width)),
            whole(w_qkv.shape),
            whole(w_out.shape),
            whole(vec.shape),
            whole(router.shape),
        ],
        out_specs=[part(s.shape[1:]) for s in shapes],
        out_shape=shapes,
        scratch_shapes=[pltpu.VMEM((sp, width), F32)],
        compiler_params=params("arbitrary"),
        cost_estimate=cost(2 * n * seq * width * width * 10, 30e6),
        name="attention_forward",
    )(images, w_qkv, w_out, vec, router)


def hot_rows(slots, cap_rows):
    places = lax.broadcasted_iota(jnp.int32, (cap_rows, slots.shape[1]), 0)
    return jnp.where(places == slots, 1.0, 0.0).astype(BF16)


ROOT = 0.7978845608028654
CUBE = 0.044715


def hot_tokens(slots, r, cap_rows):
    places = lax.broadcasted_iota(jnp.int32, (slots.shape[0], cap_rows), 1)
    return jnp.where(places == slots[:, r : r + 1], 1.0, 0.0).astype(BF16)


def output_kernel(step, count, slots, attended, answers_l, answers_r, output):
    cap = answers_l.shape[1]
    total = attended[0]
    for r in range(8):
        rows = answers_l[r] if r < 4 else answers_r[r - 4]
        total = total + mm(hot_tokens(slots[0], r, cap), rows)
    live = (step < count[0]).astype(F32)
    output[0] = (total * live).astype(BF16)[0 : output.shape[1]]


def mm_split(a, b):
    high = a.astype(BF16)
    low = (a - high.astype(F32)).astype(BF16)
    return mm(high, b, NT) + mm(low, b, NT)


def early_kernel(
    step, count, images, cotangent, joint, weights, mixed, attended, routed, probs, slots,
    w_out, vec, router, grows, ggs, g_out, g_vec, rows, cots, g_attend, g_mix,
):
    seq, width = images.shape[1:]
    sp = rows.shape[0]
    cap = grows.shape[1]
    live = (step < count[0]).astype(F32)
    grad = padded_rows(cotangent, cots) * live
    lane = lax.broadcasted_iota(jnp.int32, (cap, 128), 1)
    g_routed = jnp.zeros((sp, width), F32)
    g_probs = jnp.zeros((sp, 128), F32)
    for r in range(8):
        hot = hot_tokens(slots[0], r, cap)
        g_routed = g_routed + mm(hot, grows[r])
        g_probs = g_probs + mm(hot, jnp.where(lane == r, ggs[r // 4], jnp.zeros((), BF16)))
    p = probs[0]
    g_logits = (p * (g_probs - jnp.sum(p * g_probs, axis=-1, keepdims=True))).astype(BF16)
    g_routed = g_routed + mm(g_logits, router[...])
    g_vec[8:16] += mm(g_logits, routed[0], TN)[0:8]
    unit, rstd = norm_parts(attended[0])
    g_vec[5:6] += jnp.sum(g_routed * unit, axis=0, keepdims=True)
    g_vec[6:7] += jnp.sum(g_routed, axis=0, keepdims=True)
    g_attended = grad + norm_back(g_routed, unit, rstd, vec[5:6])
    g_attend[...] = g_attended
    branch = g_attended.astype(BF16)
    g_vec[4:5] += jnp.sum(branch.astype(F32), axis=0, keepdims=True)
    g_out[...] += mm(mixed[0], branch, TN)
    g_mix[...] = mm(branch, w_out[...], NT).astype(BF16)


def attention_part(which, images, vec, joint, weights, g_mix, g_joint, g_qkv, g_sum, rows):
    width = images.shape[2]
    sp = rows.shape[0]
    half = width // 2
    scale = (width // HEADS) ** (-0.5)
    for pair in range(HEADS // 4):
        cols = which * half + pair * 128
        q = joint[0, :, cols : cols + 128]
        k = joint[0, :, width + cols : width + cols + 128]
        v = joint[0, :, 2 * width + cols : 2 * width + cols + 128]
        gm = g_mix[:, cols : cols + 128]
        g_q = jnp.zeros((sp, 128), F32)
        g_k = jnp.zeros((sp, 128), F32)
        g_v = jnp.zeros((sp, 128), F32)
        for side in range(2):
            sel = half_mask(sp, side)
            w = weights[0, pair * 2 + side]
            g_p = mm(gm, jnp.where(sel, v, 0), NT)
            wf = w.astype(F32)
            g_s = (wf * (g_p - jnp.sum(wf * g_p, axis=-1, keepdims=True))).astype(BF16)
            g_v = g_v + mm(w, jnp.where(sel, gm, 0), TN)
            g_q = g_q + mm(g_s, jnp.where(sel, k, 0))
            g_k = g_k + mm(g_s, jnp.where(sel, q, 0), TN)
        g_joint[:, cols : cols + 128] = (g_q * scale).astype(BF16)
        g_joint[:, width + cols : width + cols + 128] = (g_k * scale).astype(BF16)
        g_joint[:, 2 * width + cols : 2 * width + cols + 128] = g_v.astype(BF16)
    unit, _ = norm_parts(padded_rows(images, rows))
    hidden = (unit * vec[0:1] + vec[1:2]).astype(BF16)
    for third in range(3):
        cols = slice(third * width + which * half, third * width + (which + 1) * half)
        part_of = g_joint[:, cols]
        g_qkv[:, third * half : (third + 1) * half] += mm(hidden, part_of, TN)
        g_sum[0:1, cols] += jnp.sum(part_of.astype(F32), axis=0, keepdims=True)


def late_kernel(images, vec, w_qkv, rows, g_joint, g_attend, g_images):
    unit, rstd = norm_parts(padded_rows(images, rows))
    g_hidden = mm(g_joint[...], w_qkv[...], NT)
    g_in = g_attend[...] + norm_back(g_hidden, unit, rstd, vec[0:1])
    g_images[0] = g_in[0 : images.shape[1]]


MESH = pl.DeviceIdType.MESH
CUT = 352
HALF = 528


def partners():
    e, w = lax.axis_index("expert"), lax.axis_index("wshard")
    return {
        "z": {"expert": lax.rem(e + 2, 8)},
        "z_back": {"expert": lax.rem(e + 6, 8)},
        "x": {"expert": e + 1 - 2 * lax.rem(e, 2)},
        "y": {"wshard": lax.rem(w + 2, 4)},
        "core": {"wshard": w + 1 - 2 * lax.rem(w, 2)},
    }


def meet(devices):
    barrier = pltpu.get_barrier_semaphore()
    for device in devices:
        pl.semaphore_signal(barrier, inc=1, device_id=device, device_id_type=MESH)
    pl.semaphore_wait(barrier, len(devices))


def sender(send, recv, slot, device, src, dst):
    return pltpu.make_async_remote_copy(
        src_ref=src,
        dst_ref=dst,
        send_sem=send.at[slot],
        recv_sem=recv.at[slot],
        device_id=device,
        device_id_type=MESH,
    )


def any_space():
    return pl.BlockSpec(memory_space=pl.ANY)


def split_probs(probs):
    high = probs.astype(BF16)
    low = (probs - high.astype(F32)).astype(BF16)
    lane = lax.broadcasted_iota(jnp.int32, probs.shape, 1)
    return jnp.where(lane < 64, high, jnp.roll(low, 64, axis=1))


def gate_lanes(gate, r):
    lane = lax.broadcasted_iota(jnp.int32, gate.shape, 1)
    gate = jnp.sum(jnp.where(lane % 64 == r, gate, 0.0), axis=1, keepdims=True)
    return high_low(gate, lane - 2 * (r % 4))


def gather_kernel(
    images, cotangent, slot_rows, w_qkv, w_out, small, e_in, e_out, e_bias,
    joint_o, weights_o, mixed_o, attended_o, routed_o, probs_o,
    cots_o, pieces_o, qkv_o, out_o, rows_o, gates_o, vec_o, router_o,
    rows, flat, placed, pack, qkv, out, smalls, vec, router, flat_probs, gates, send, recv, local,
):
    step = pl.program_id(0)
    last = pl.num_programs(0) - 1
    w = lax.axis_index("wshard")
    to = partners()
    width = w_out.shape[1]
    cap = placed.shape[1]
    share = w_qkv.shape[0]
    w_core = w + 1 - 2 * lax.rem(w, 2)
    w_far = lax.rem(w + 2, 4)

    def rows_of(ref, which):
        return ref.at[pl.ds(pl.multiple_of(which * share, share), share)]

    dense = ((w_qkv, qkv, rows_of), (w_out, out, rows_of), (small, smalls, lambda r, i: r.at[i]))
    far = [sender(send, recv, i, to["y"], a, at(b, w)) for i, (a, b, at) in enumerate(dense)]
    near = [sender(send, recv, 3 + i, to["core"], a, at(b, w)) for i, (a, b, at) in enumerate(dense)]
    onward = [
        sender(send, recv, 6 + i, to["core"], at(b, w_far), at(b, w_far))
        for i, (a, b, at) in enumerate(dense)
    ]
    first, rest = pl.ds(0, HALF), pl.ds(HALF, pack.shape[0] - HALF)
    spread = [
        sender(send, recv, 9, to["z"], pack.at[first], pieces_o.at[4, first]),
        sender(send, recv, 10, to["y"], pack, pieces_o.at[2]),
        sender(send, recv, 11, to["core"], pack, pieces_o.at[1]),
        sender(send, recv, 16, to["z"], pack.at[rest], pieces_o.at[4, rest]),
    ]
    ahead = sender(send, recv, 17, to["z"], pieces_o.at[4, first], pieces_o.at[5, first])
    cots = [
        sender(send, recv, 12 + k, to["x"], placed.at[4 + k], cots_o.at[k, cap : 2 * cap])
        for k in range(4)
    ]
    kept = [
        pltpu.make_async_copy(placed.at[k], cots_o.at[k, 0:cap], local.at[k]) for k in range(4)
    ]
    sent = [
        pltpu.make_async_copy(placed.at[k], rows_o.at[k], local.at[7 + k]) for k in range(4)
    ] + [pltpu.make_async_copy(gates, gates_o, local.at[11])]
    saved = [
        pltpu.make_async_copy(qkv, qkv_o, local.at[4]),
        pltpu.make_async_copy(out, out_o, local.at[5]),
        pltpu.make_async_copy(pack, pieces_o.at[0], local.at[6]),
    ]

    @pl.when(step == 0)
    def _():
        meet(list(to.values()))
        for copy in far + near:
            copy.start()
        pack[0:width] = e_in[0]
        pack[width : 2 * width] = e_out[0]
        pack[2 * width : 2 * width + 16] = e_bias[...]
        spread[0].start()
        mine = pl.ds(pl.multiple_of(w * share, share), share)
        qkv[mine] = w_qkv[...]
        out[mine] = w_out[...]
        smalls[w] = small[...]
        n, seq = cotangent.shape[:2]
        sp = flat.shape[0] // n
        for i in range(n):
            flat[(i + 1) * sp - 16 : (i + 1) * sp] = jnp.zeros((16, width), BF16)
            flat[i * sp : i * sp + seq] = cotangent[i]
        for k in range(4):
            placed[4 + k] = mm(hot_rows(slot_rows[4 + k], cap), flat[...]).astype(BF16)
            cots[k].start()
        for copy in far:
            copy.wait_recv()
        for copy in onward + spread[1:]:
            copy.start()
        for k in range(4):
            placed[k] = mm(hot_rows(slot_rows[k], cap), flat[...]).astype(BF16)
            kept[k].start()
        for copy in near + onward:
            copy.wait_recv()
        for copy in far + near + onward:
            copy.wait_send()
        vec[...] = jnp.concatenate([smalls[i] for i in range(4)], axis=1).astype(F32)
        router[...] = jnp.zeros_like(router)
        router[0:8] = vec[8:16].astype(BF16)
        vec_o[...] = vec[...]
        router_o[...] = router[...]
        for copy in saved:
            copy.start()

    @pl.when(step == last - 3)
    def _():
        spread[0].wait_recv()
        spread[3].wait_send()
        ahead.start()

    forward_kernel(
        images, qkv, out, vec, router, joint_o, weights_o, mixed_o, attended_o, routed_o,
        probs_o, rows,
    )

    sp = rows.shape[0]
    band = pl.ds(pl.multiple_of(step * sp, sp), sp)
    flat[band] = routed_o[0]
    flat_probs[band] = probs_o[0]

    @pl.when(step == last)
    def _():
        for copy in kept + saved:
            copy.wait()
        split = split_probs(flat_probs[...])
        total = jnp.zeros(gates.shape, BF16)
        for k in range(4):
            hot = hot_rows(slot_rows[4 + k], cap)
            placed[k] = mm(hot, flat[...]).astype(BF16)
            total = total + gate_lanes(mm(hot, split), 4 + k)
            sent[k].start()
        gates[...] = total
        sent[4].start()
        for copy in sent:
            copy.wait()
        for copy in cots + [spread[1], spread[2], ahead]:
            copy.wait()
        spread[3].wait_recv()
        spread[0].wait_send()


def gather_forward(images, cotangent, slot_rows, w_qkv, w_out, small, e_in, e_out, e_bias, sp, cap):
    n, seq, width = images.shape
    piece = 2 * width + 16
    blocks = [
        jax.ShapeDtypeStruct((n, sp, 3 * width), BF16),
        jax.ShapeDtypeStruct((n, HEADS, sp, sp), BF16),
        jax.ShapeDtypeStruct((n, sp, width), BF16),
        jax.ShapeDtypeStruct((n, sp, width), F32),
        jax.ShapeDtypeStruct((n, sp, width), BF16),
        jax.ShapeDtypeStruct((n, sp, 128), F32),
    ]
    far = [
        jax.ShapeDtypeStruct((4, 2 * cap, width), BF16),
        jax.ShapeDtypeStruct((6, piece, width), BF16),
        jax.ShapeDtypeStruct((width, 3 * width), BF16),
        jax.ShapeDtypeStruct((width, width), BF16),
        jax.ShapeDtypeStruct((4, cap, width), BF16),
        jax.ShapeDtypeStruct((cap, 128), BF16),
    ]
    small_shapes = [
        jax.ShapeDtypeStruct((16, width), F32),
        jax.ShapeDtypeStruct((128, width), BF16),
    ]
    return pl.pallas_call(
        gather_kernel,
        grid=(n,),
        in_specs=[part((seq, width))]
        + [
            whole(a.shape)
            for a in (cotangent, slot_rows, w_qkv, w_out, small, e_in, e_out, e_bias)
        ],
        out_specs=[part(s.shape[1:]) for s in blocks]
        + [any_space()] * 6
        + [whole(s.shape) for s in small_shapes],
        out_shape=blocks + far + small_shapes,
        scratch_shapes=[
            pltpu.VMEM((sp, width), F32),
            pltpu.VMEM((n * sp, width), BF16),
            pltpu.VMEM((8, cap, width), BF16),
            pltpu.VMEM((piece, width), BF16),
            pltpu.VMEM((width, 3 * width), BF16),
            pltpu.VMEM((width, width), BF16),
            pltpu.VMEM((4, 16, width // 4), BF16),
            pltpu.VMEM((16, width), F32),
            pltpu.VMEM((128, width), BF16),
            pltpu.VMEM((n * sp, 128), F32),
            pltpu.VMEM((cap, 128), BF16),
            pltpu.SemaphoreType.DMA((18,)),
            pltpu.SemaphoreType.DMA((18,)),
            pltpu.SemaphoreType.DMA((12,)),
        ],
        compiler_params=pltpu.CompilerParams(
            dimension_semantics=("arbitrary",),
            vmem_limit_bytes=VMEM_LIMIT,
            collective_id=0,
            has_side_effects=True,
        ),
        cost_estimate=cost(2 * n * seq * width * width * 20, 40e6),
        name="gather_forward",
    )(images, cotangent, slot_rows, w_qkv, w_out, small, e_in, e_out, e_bias)


def add16(a, b):
    return (a.astype(F32) + b.astype(F32)).astype(BF16)


def once(shape):
    return pl.BlockSpec(shape, lambda *_: (0,) * len(shape), pipeline_mode=pl.Buffered(1))


def high_low(values, lane):
    high = values.astype(BF16).astype(F32)
    return jnp.where(lane == 0, high, jnp.where(lane == 1, values - high, 0.0)).astype(BF16)


def experts_kernel(
    slot_rows, routed, probs, cots, pieces, rows_s, gates_s,
    grows_o, ggs_o, answers_o, sent_o, own_o, far_o, far_in,
    weights, rows, gates, grad, core_in, ans_s, grow_s, ans_b, grow_b, gg_b,
    send, recv, local,
):
    k = pl.program_id(0)
    w = lax.axis_index("wshard")
    to = partners()
    cap = rows.shape[1] // 2
    width = rows.shape[2]
    near, away = pl.ds(0, cap), pl.ds(cap, cap)

    def link(slot, device, src, dst):
        return sender(send, recv, slot, to[device], src, dst)

    first, rest = pl.ds(0, HALF), pl.ds(HALF, pieces.shape[1] - HALF)
    shared = [None, None, pl.ds(0, CUT), rest]
    other = [None, None, pl.ds(CUT, pieces.shape[1] - CUT), first]
    loads = [
        pltpu.make_async_copy(src, dst, local.at[j])
        for j, (src, dst) in enumerate(
            (
                (pieces.at[0], weights.at[0, 0]),
                (pieces.at[1], weights.at[0, 1]),
                (pieces.at[2], weights.at[0, 2]),
                (pieces.at[4], weights.at[1, 0]),
                (pieces.at[5, first], weights.at[2, 0, first]),
            )
        )
    ]
    ring = [
        link(0, "z", pieces.at[4, rest], weights.at[2, 0, rest]),
        link(1, "z", pieces.at[5, first], weights.at[3, 0, first]),
        link(2, "z", weights.at[2, 0, rest], weights.at[3, 0, rest]),
    ]
    ride = [None, None] + [
        link(3, "z", weights.at[1, 2, shared[2]], weights.at[2, 2, shared[2]]),
        link(4, "z", weights.at[2, 2, shared[3]], weights.at[3, 2, shared[3]]),
    ]
    held = [None, pieces.at[4], weights.at[2, 0], weights.at[3, 0]]
    beside = [None] + [link(37 + i, "core", held[i], weights.at[i, 1]) for i in (1, 2, 3)]
    across = [None, link(5, "y", held[1], weights.at[1, 2])] + [
        link(4 + i, "y", held[i].at[other[i]], weights.at[i, 2, other[i]]) for i in (2, 3)
    ]
    onward = [link(8, "core", pieces.at[2], weights.at[0, 3])] + [
        link(8 + i, "core", weights.at[i, 2], weights.at[i, 3]) for i in (1, 2, 3)
    ]
    rows_out = [link(12 + i, "x", rows_s.at[i], rows.at[i, away]) for i in range(4)]
    gates_out = link(16, "x", gates_s, gates.at[away])
    slot = lax.rem(k, 2)
    grow_out = link(20 + k, "x", grow_b.at[k, away], grows_o.at[4 + k])
    gg_out = link(24, "x", gg_b.at[away], ggs_o.at[1])
    gg_own = pltpu.make_async_copy(gg_b.at[near], ggs_o.at[0], local.at[28])
    core_out = [
        link(28 + 2 * k + i, "core", grad.at[1 + 2 * i], core_in.at[slot, i]) for i in range(2)
    ]
    far_out = link(36, "y", far_o.at[1], far_in)

    def results(j):
        return [
            pltpu.make_async_copy(src, dst, local.at[5 + 5 * j + i])
            for i, (src, dst) in enumerate(
                (
                    (grow_b.at[j, near], grows_o.at[j]),
                    (ans_b.at[j, near], answers_o.at[j]),
                    (ans_b.at[j, away], sent_o.at[j]),
                    (grad.at[0], own_o.at[j]),
                    (grad.at[2], far_o.at[j]),
                )
            )
        ]

    @pl.when(k == 0)
    def _():
        for copy in loads:
            copy.start()
        gg_b[...] = jnp.zeros_like(gg_b)
        meet(list(to.values()))
        for copy in (ring[0], across[1], beside[1], onward[0]):
            copy.start()
        rows_out[0].start()
        gates_out.start()
        split = split_probs(probs[...])
        total = jnp.zeros((cap, 128), BF16)
        for r in range(4):
            hot = hot_rows(slot_rows[r], cap)
            rows[r, 0:cap] = mm(hot, routed[...]).astype(BF16)
            total = total + gate_lanes(mm(hot, split), r)
        gates[0:cap] = total
        rows_out[0].wait_send()
        rows_out[1].start()
        gates_out.wait_recv()
        for copy in loads:
            copy.wait()
        onward[0].wait_recv()

    for i in (1, 2, 3):

        @pl.when(k == i)
        def _(i=i):
            beside[i].wait_recv()

    for i in range(4):

        @pl.when(k == i)
        def _(i=i):
            rows_out[i].wait_recv()

    x = rows[k]
    cot = cots[k].astype(F32)
    lane = lax.broadcasted_iota(jnp.int32, gates.shape, 1)
    gate = jnp.where(lane // 2 == k, gates[...].astype(F32), 0.0)
    gate = jnp.sum(gate, axis=1, keepdims=True)
    scaled = (cot * gate).astype(BF16)
    g_bias_out = jnp.sum(scaled.astype(F32), axis=0, keepdims=True)
    for turn, q in enumerate((1, 0, 3, 2)):
        if turn == 2:
            for i in (1, 2, 3):

                @pl.when(k == i)
                def _(i=i):
                    onward[i].wait_recv()

        w_in = weights[k, q, 0:width]
        w_out = weights[k, q, width : 2 * width]
        before = mm(x, w_in) + weights[k, q, 2 * width : 2 * width + 16].astype(F32)[0:1]
        square = before * before
        inner = before * (ROOT + ROOT * CUBE * square)
        curve = jnp.tanh(inner)
        half = 0.5 * curve + 0.5
        active = (before * half).astype(BF16)
        slope = half + (0.5 * before) * (1.0 - curve * curve) * (ROOT + 3.0 * ROOT * CUBE * square)
        grad_active = mm(scaled, w_out, NT)
        grad_before = (grad_active * slope).astype(BF16)
        if turn == 0:
            ans_s[...] = mm(active, w_out)
            grow_s[...] = mm(grad_before, w_in, NT)
        else:
            ans_s[...] += mm(active, w_out)
            grow_s[...] += mm(grad_before, w_in, NT)
        g_bias_in = jnp.sum(grad_before.astype(F32), axis=0, keepdims=True)
        tail = lax.broadcasted_iota(jnp.int32, (16, width), 0)

        @pl.when(k > 0)
        def _(q=q):
            if q % 2:
                link(28 + 2 * (k - 1) + q // 2, "core", grad.at[q], core_in.at[1 - slot, q // 2]).wait_send()
            elif q == 0:
                results(k - 1)[3].wait()

        if q == 2:

            @pl.when(k == 3)
            def _():
                results(2)[4].wait()

        grad[q, 0:width] = mm(x, grad_before, TN).astype(BF16)
        grad[q, width : 2 * width] = mm(active, scaled, TN).astype(BF16)
        grad[q, 2 * width : 2 * width + 16] = jnp.where(
            tail == 0, g_bias_in, jnp.where(tail == 1, g_bias_out, 0.0)
        ).astype(BF16)
        if q % 2:
            core_out[q // 2].start()
        if turn == 0:

            @pl.when(k == 0)
            def _():
                ring[0].wait_recv()
                for copy in (ring[1], beside[2]):
                    copy.start()

            @pl.when(k == 1)
            def _():
                results(0)[4].wait()

            @pl.when(k == 2)
            def _():
                results(1)[4].wait()
                ride[2].wait_recv()
                across[2].wait_recv()
                ring[1].wait_recv()
                for copy in (onward[2], across[3], ride[3]):
                    copy.start()

            @pl.when(k == 3)
            def _():
                ride[3].wait_recv()
                across[3].wait_recv()
                onward[3].start()

        if turn == 1:

            @pl.when(k == 2)
            def _():
                ring[2].wait_recv()
                beside[3].start()

        if turn == 2:

            @pl.when(k == 0)
            def _():
                rows_out[1].wait_send()
                rows_out[2].start()

            @pl.when(k == 1)
            def _():
                rows_out[2].wait_send()
                rows_out[3].start()

        if turn == 3:

            @pl.when(k == 0)
            def _():
                across[1].wait_recv()
                for copy in (onward[1], across[2], ride[2], ring[2]):
                    copy.start()

            @pl.when(k == 2)
            def _():
                far_out.start()

    bias = []
    for j in range(4):
        q = lax.rem(j + w, 2) + 2 * lax.rem(j // 2 + w // 2, 2)
        bias.append(weights[k, q, 2 * width : 2 * width + 16, 0:128].astype(F32)[1:2])
    bias_out = jnp.concatenate(bias, axis=1)
    answer = (ans_s[...] + bias_out).astype(BF16).astype(F32)
    gg = jnp.sum(answer * cot, axis=1, keepdims=True)
    row = lax.broadcasted_iota(jnp.int32, gg_b.shape, 0)
    own_lane = k + jnp.where(row >= cap, 4, 0)
    gg_b[...] = jnp.where(lane == own_lane, gg, gg_b[...].astype(F32)).astype(BF16)
    grow_b[k] = grow_s[...].astype(BF16)
    grow_out.start()
    ans_b[k] = (answer * gate).astype(BF16)
    for copy in core_out:
        copy.wait_recv()
    grad[0] = add16(grad[0], core_in[slot, 0])
    grad[2] = add16(grad[2], core_in[slot, 1])
    done = results(k)
    for copy in done:
        copy.start()

    @pl.when(k == 3)
    def _():
        gg_out.start()
        gg_own.start()
        for copy in core_out:
            copy.wait_send()
        done[3].wait()
        done[4].wait()
        for j in range(4):
            for copy in results(j)[:3]:
                copy.wait()
            link(20 + j, "x", grow_b.at[j, away], grows_o.at[4 + j]).wait()
        for copy in ring + ride[2:] + beside[1:] + across[1:] + onward:
            copy.wait_send()
        gates_out.wait_send()
        rows_out[3].wait_send()
        gg_out.wait()
        gg_own.wait()
        far_out.wait()


def run_experts(slot_rows, routed, probs, cots, pieces, rows_s, gates_s):
    _, both, width = cots.shape
    cap = both // 2
    piece = pieces.shape[1]
    shapes = [
        jax.ShapeDtypeStruct((8, cap, width), BF16),
        jax.ShapeDtypeStruct((2, cap, 128), BF16),
        jax.ShapeDtypeStruct((4, cap, width), BF16),
        jax.ShapeDtypeStruct((4, cap, width), BF16),
        jax.ShapeDtypeStruct((4, piece, width), BF16),
        jax.ShapeDtypeStruct((4, piece, width), BF16),
        jax.ShapeDtypeStruct((piece, width), BF16),
    ]
    return pl.pallas_call(
        experts_kernel,
        grid=(4,),
        in_specs=[once(a.shape) for a in (slot_rows, routed, probs, cots)] + [any_space()] * 3,
        out_specs=[any_space()] * len(shapes),
        out_shape=shapes,
        scratch_shapes=[
            pltpu.VMEM((4, 4, piece, width), BF16),
            pltpu.VMEM((4, both, width), BF16),
            pltpu.VMEM((both, 128), BF16),
            pltpu.VMEM((4, piece, width), BF16),
            pltpu.VMEM((2, 2, piece, width), BF16),
            pltpu.VMEM((both, width), F32),
            pltpu.VMEM((both, width), F32),
            pltpu.VMEM((4, both, width), BF16),
            pltpu.VMEM((4, both, width), BF16),
            pltpu.VMEM((both, 128), BF16),
            pltpu.SemaphoreType.DMA((41,)),
            pltpu.SemaphoreType.DMA((41,)),
            pltpu.SemaphoreType.DMA((29,)),
        ],
        compiler_params=pltpu.CompilerParams(
            dimension_semantics=("arbitrary",),
            vmem_limit_bytes=62 * 1024 * 1024,
            collective_id=1,
            has_side_effects=True,
        ),
        cost_estimate=cost(2 * 2 * cap * width * width * 4 * 6 * 4, 60e6),
        name="run_experts",
    )(slot_rows, routed, probs, cots, pieces, rows_s, gates_s)


def backward_all_kernel(
    count, images, cotangent, joint, weights, mixed, attended, routed, probs, slots,
    w_qkv, w_out, vec, router, grows, ggs, answers_l, answers_s, own, far, far_in,
    output, g_images, g_qkv_o, g_out_o, g_small_o, e_in_o, e_out_o, e_bias_o,
    rows, cots, g_joints, g_attends, g_mixes, g_near, g_away, g_out, g_vec, g_sum, g_rows,
    answers_r, mine, far_got, ring_got,
    dense_a, core_a, y_a, ours_a, x_a, z_a, all_a, dense_b, core_b, y_b, ours_b, x_b, z_b, all_b,
    send, recv, local,
):
    step = pl.program_id(0)
    n = pl.num_programs(0) // 3
    e, w = lax.axis_index("expert"), lax.axis_index("wshard")
    to = partners()
    zs = [{"expert": lax.rem(e + 2 * d, 8)} for d in range(1, 4)]
    e_x, e_z = lax.rem(e, 2), e // 2
    width = w_out.shape[0]
    quarter = width // 4
    part_rows = quarter // 8
    half = width // 2
    w_core = w + 1 - 2 * lax.rem(w, 2)
    w_far = lax.rem(w + 2, 4)
    w_last = lax.rem(w_core + 2, 4)

    def load(j):
        pairs = [(own.at[i], mine.at[i]) for i in range(4)]
        pairs += [(far_in, far_got.at[1])]
        return pltpu.make_async_copy(*pairs[j], local.at[j])

    def answer(k):
        return sender(send, recv, k, to["x"], answers_s.at[k], answers_r.at[k])

    def beyond(k):
        return sender(send, recv, 4 + k, to["y"], far.at[k], far_got.at[k])

    def ring(k):
        return sender(send, recv, 8 + k, to["z"], mine.at[k], ring_got.at[k])

    sides = (
        (12, dense_a, core_a, y_a, ours_a, x_a, z_a, all_a),
        (23, dense_b, core_b, y_b, ours_b, x_b, z_b, all_b),
    )

    def core(side, i):
        base, dense, core_got = sides[side][:3]
        return sender(send, recv, base + i, to["core"], dense.at[(w_core, w_last)[i]], core_got.at[i])

    def y_side(side):
        base, dense, _, y_got = sides[side][:4]
        return sender(send, recv, base + 2, to["y"], dense.at[w_far], y_got)

    def x_half(which):
        return pl.ds(pl.multiple_of(which * 4 * part_rows, 4 * part_rows), 4 * part_rows)

    def x_side(side):
        base, ours, x_got = sides[side][0], sides[side][4], sides[side][5]
        return sender(send, recv, base + 3, to["x"], ours.at[x_half(1 - e_x)], x_got)

    def chunk(which):
        return pl.ds(
            pl.multiple_of(e_x * 4 * part_rows + which * part_rows, part_rows), part_rows
        )

    def scatter(side, d):
        base, ours, z_got = sides[side][0], sides[side][4], sides[side][6]
        src = ours.at[chunk(lax.rem(e_z + d, 4))]
        return sender(send, recv, base + 3 + d, zs[d - 1], src, z_got.at[d - 1])

    def share(side, d):
        base, every = sides[side][0], sides[side][7]
        return sender(send, recv, base + 6 + d, zs[d - 1], every.at[e_x, e_z], every.at[e_x, e_z])

    def x_share(side):
        base, every = sides[side][0], sides[side][7]
        return sender(send, recv, base + 10, to["x"], every.at[e_x], every.at[e_x])

    def core_done(side):
        _, dense, core_got, _, ours = sides[side][:5]
        for i in range(2):
            core(side, i).wait()
        dense[w_far] = add16(dense[w_far], core_got[1])
        y_side(side).start()
        ours[...] = add16(dense[w], core_got[0])

    def y_done(side):
        ours, y_got = sides[side][4], sides[side][3]
        y_side(side).wait()
        ours[...] = add16(ours[...], y_got[...])
        x_side(side).start()

    def x_done(side):
        ours, x_got = sides[side][4:6]
        x_side(side).wait()
        ours[x_half(e_x)] = add16(ours[x_half(e_x)], x_got[...])
        for d in range(1, 4):
            scatter(side, d).start()

    def z_done(side):
        ours, _, z_got, every = sides[side][4:8]
        for d in range(1, 4):
            scatter(side, d).wait_recv()
        total = ours[chunk(e_z)].astype(F32)
        for d in range(1, 4):
            total = total + z_got[d - 1].astype(F32)
        every[e_x, e_z] = total.astype(BF16)
        for d in range(1, 4):
            share(side, d).start()

    def share_done(side):
        for d in range(1, 4):
            share(side, d).wait_recv()
        x_share(side).start()

    def at(which):
        return pl.when(step == which)

    @at(0)
    def _():
        g_near[...] = jnp.zeros_like(g_near)
        g_away[...] = jnp.zeros_like(g_away)
        g_out[...] = jnp.zeros_like(g_out)
        g_vec[...] = jnp.zeros_like(g_vec)
        g_sum[...] = jnp.zeros_like(g_sum)
        for j in (1, 4, 0, 2, 3):
            load(j).start()
        meet([to["y"], to["core"], to["x"]] + zs)
        beyond(2).start()
        load(1).wait()
        load(4).wait()
        mine[1] = add16(mine[1], far_got[1])
        ring(1).start()
        for k in range(4):
            answer(k).start()

    for k, when in ((2, 6), (3, 2 * n + 1)):

        @at(when)
        def _(k=k):
            if k == 2:
                for j in (0, 2, 3):
                    load(j).wait()
            beyond(k).wait_recv()
            ring(k - 1).wait_recv()
            total = mine[k].astype(F32) + far_got[k].astype(F32) + ring_got[k - 1].astype(F32)
            mine[k] = total.astype(BF16)
            ring(k).start()
            if k == 2:
                beyond(3).start()

    @pl.when(step < n)
    def _():
        early_kernel(
            step, count, images, cotangent, joint, weights, mixed, attended, routed, probs, slots,
            w_out, vec, router, grows, ggs, g_out, g_vec, rows, cots,
            g_attends.at[step], g_mixes.at[step],
        )
        attention_part(
            0, images, vec, joint, weights, g_mixes.at[step], g_joints.at[step], g_near, g_sum, rows
        )

    @at(n - 1)
    def _():
        for j in range(4):
            band = slice(j * quarter, (j + 1) * quarter)
            dense_a[j, :, 0 : 3 * half] = g_near[band].astype(BF16)
            dense_a[j, :, 3 * half :] = g_out[band].astype(BF16)
        for i in range(2):
            core(0, i).start()

    @pl.when((step >= n) & (step < 2 * n))
    def _():
        attention_part(
            1, images, vec, joint, weights, g_mixes.at[step - n], g_joints.at[step - n], g_away,
            g_sum, rows,
        )

    @at(2 * n - 1)
    def _():
        sums = g_sum[...]
        g_bias = (mm_split(sums, w_qkv[...]))[0:1]
        ones = jnp.ones((16, half), BF16)
        g_gain = jnp.zeros((16, width), F32)
        for third in range(3):
            for part_of, at_col in ((g_near, 0), (g_away, half)):
                col = third * width + at_col
                product = w_qkv[:, col : col + half].astype(F32)
                product = product * part_of[:, third * half : (third + 1) * half]
                high = product.astype(BF16)
                low = (product - high.astype(F32)).astype(BF16)
                g_gain = g_gain + mm(ones, high, NT) + mm(ones, low, NT)
        g_vec[0:1] = (g_gain[0:1] - vec[1:2] * g_bias) / vec[0:1]
        g_vec[1:2] = g_bias
        g_vec[2:3] = sums[0:1, 0:width]
        g_vec[3:4] = sums[0:1, 2 * width :]
        g_rows[0:8] = g_vec[0:8]
        for r in range(8):
            expert = lax.rem(e + 8 - 2 * (r % 4), 8)
            expert = expert if r < 4 else expert + 1 - 2 * lax.rem(expert, 2)
            g_rows[pl.ds(8 + expert, 1)] = g_vec[8 + r : 9 + r]
        dense_b[:, 16:quarter, 3 * half :] = jnp.zeros((4, quarter - 16, quarter), BF16)
        for j in range(4):
            band = slice(j * quarter, (j + 1) * quarter)
            dense_b[j, :, 0 : 3 * half] = g_away[band].astype(BF16)
            dense_b[j, 0:16, 3 * half :] = g_rows[:, band].astype(BF16)
        for i in range(2):
            core(1, i).start()

    @at(2 * n)
    def _():
        core_done(0)
        for k in range(4):
            answer(k).wait_recv()

    @at(2 * n + 1)
    def _():
        core_done(1)

    @at(2 * n + 3)
    def _():
        y_done(0)

    @at(2 * n + 4)
    def _():
        x_done(0)

    @at(2 * n + 5)
    def _():
        y_done(1)
        beyond(0).start()

    @at(2 * n + 6)
    def _():
        x_done(1)
        z_done(0)

    @pl.when(step >= 2 * n)
    def _():
        i = step - 2 * n
        late_kernel(images, vec, w_qkv, rows, g_joints.at[i], g_attends.at[i], g_images)
        output_kernel(i, count, slots, attended, answers_l, answers_r, output)

    @at(3 * n - 1)
    def _():
        z_done(1)
        share_done(0)
        share_done(1)
        for side in range(2):
            x_share(side).wait_recv()
        for i in range(8):
            band = slice(i * part_rows, (i + 1) * part_rows)
            near, away = all_a[i // 4, i % 4].astype(F32), all_b[i // 4, i % 4].astype(F32)
            for third in range(3):
                col = third * width
                cols = slice(third * half, (third + 1) * half)
                g_qkv_o[band, col : col + half] = near[:, cols]
                g_qkv_o[band, col + half : col + width] = away[:, cols]
            g_out_o[band] = near[:, 3 * half :]
            if i == 0:
                g_small_o[...] = away[0:16, 3 * half :]
        ring(3).wait_recv()
        beyond(0).wait_recv()
        total = mine[0].astype(F32) + far_got[0].astype(F32) + ring_got[3].astype(F32)
        e_in_o[0] = total[0:width]
        e_out_o[0] = total[width : 2 * width]
        e_bias_o[...] = total[2 * width : 2 * width + 16]
        for side in range(2):
            x_share(side).wait_send()
            for d in range(1, 4):
                scatter(side, d).wait_send()
                share(side, d).wait_send()
        for k in range(4):
            answer(k).wait_send()
        for k in (2, 3, 0):
            beyond(k).wait_send()
        for k in (1, 2, 3):
            ring(k).wait_send()


def backward_all(
    count, images, cotangent, joint, weights, mixed, attended, routed, probs, slots,
    w_qkv, w_out, vec, router, grows, ggs, answers_l, answers_s, own, far, far_in,
):
    n, seq, width = images.shape
    sp = joint.shape[1]
    cap = grows.shape[1]
    piece = own.shape[1]
    quarter = width // 4
    half = width // 2

    def early(shape):
        return pl.BlockSpec((1,) + shape, lambda i: (jnp.minimum(i, n - 1),) + (0,) * len(shape))

    def image(i):
        return jnp.where(i < n, i, jnp.where(i < 2 * n, i - n, n - 1))

    def twice(shape):
        return pl.BlockSpec((1,) + shape, lambda i: (image(i),) + (0,) * len(shape))

    def halves(shape):
        half_heads = (1, shape[0] // 2) + shape[1:]
        return pl.BlockSpec(half_heads, lambda i: (image(i), jnp.where(i < n, 0, 1), 0, 0))

    def both(shape):
        return pl.BlockSpec((1,) + shape, lambda i: (lax.rem(i, n),) + (0,) * len(shape))

    def late(shape):
        return pl.BlockSpec((1,) + shape, lambda i: (jnp.maximum(i - 2 * n, 0),) + (0,) * len(shape))

    streams = [
        (images, both), (cotangent, early), (joint, twice), (weights, halves), (mixed, early),
        (attended, both), (routed, early), (probs, early), (slots, both),
    ]
    fixed = [w_qkv, w_out, vec, router, grows, ggs, answers_l]
    far_refs = [answers_s, own, far, far_in]
    shapes = [
        jax.ShapeDtypeStruct((n, seq, width), BF16),
        jax.ShapeDtypeStruct((n, seq, width), F32),
        jax.ShapeDtypeStruct((quarter, 3 * width), F32),
        jax.ShapeDtypeStruct((quarter, width), F32),
        jax.ShapeDtypeStruct((16, quarter), F32),
        jax.ShapeDtypeStruct((1, width, width), F32),
        jax.ShapeDtypeStruct((1, width, width), F32),
        jax.ShapeDtypeStruct((16, width), F32),
    ]

    def side(cols):
        return [
            pltpu.VMEM((4, quarter, cols), BF16),
            pltpu.VMEM((2, quarter, cols), BF16),
            pltpu.VMEM((quarter, cols), BF16),
            pltpu.VMEM((quarter, cols), BF16),
            pltpu.VMEM((quarter // 2, cols), BF16),
            pltpu.VMEM((3, quarter // 8, cols), BF16),
            pltpu.VMEM((2, 4, quarter // 8, cols), BF16),
        ]

    return pl.pallas_call(
        backward_all_kernel,
        grid=(3 * n,),
        in_specs=[pl.BlockSpec(memory_space=pltpu.SMEM)]
        + [kind(a.shape[1:]) for a, kind in streams]
        + [once(a.shape) for a in fixed]
        + [any_space()] * len(far_refs),
        out_specs=[late((seq, width)), late((seq, width))] + [whole(s.shape) for s in shapes[2:]],
        out_shape=shapes,
        scratch_shapes=[
            pltpu.VMEM((sp, width), F32),
            pltpu.VMEM((sp, width), F32),
            pltpu.VMEM((n, sp, 3 * width), BF16),
            pltpu.VMEM((n, sp, width), F32),
            pltpu.VMEM((n, sp, width), BF16),
            pltpu.VMEM((width, 3 * half), F32),
            pltpu.VMEM((width, 3 * half), F32),
            pltpu.VMEM((width, width), F32),
            pltpu.VMEM((16, width), F32),
            pltpu.VMEM((16, 3 * width), F32),
            pltpu.VMEM((16, width), F32),
            pltpu.VMEM((4, cap, width), BF16),
            pltpu.VMEM((4, piece, width), BF16),
            pltpu.VMEM((4, piece, width), BF16),
            pltpu.VMEM((4, piece, width), BF16),
        ]
        + side(3 * half + width)
        + side(3 * half + quarter)
        + [
            pltpu.SemaphoreType.DMA((34,)),
            pltpu.SemaphoreType.DMA((34,)),
            pltpu.SemaphoreType.DMA((5,)),
        ],
        compiler_params=pltpu.CompilerParams(
            dimension_semantics=("arbitrary",),
            vmem_limit_bytes=62 * 1024 * 1024,
            collective_id=2,
            has_side_effects=True,
        ),
        cost_estimate=cost(2 * n * seq * width * width * 30, 40e6),
        name="backward_all",
    )(count, *[a for a, _ in streams], *fixed, *far_refs)


def weight_body(
    images, cotangent, image_count, routes, attn_norm_gain, attn_norm_bias, w_qkv, b_query,
    b_value, w_attn_out, b_attn_out, moe_norm_gain, moe_norm_bias, w_router, expert_in,
    expert_in_bias, expert_out, expert_out_bias,
):
    n, seq, width = images.shape
    sp = -(-seq // 16) * 16
    experts = lax.axis_size("expert")
    capacity = (2 * n * seq + experts - 1) // experts
    cap = -(-capacity // 16) * 16
    shard = lax.axis_index("wshard")
    place = lax.axis_index("expert")
    near = jnp.stack([(place - 2 * k) % 8 for k in range(4)])
    order = jnp.concatenate([near, near ^ 1])

    vectors = jnp.stack(
        [attn_norm_gain, attn_norm_bias, b_query, b_value, b_attn_out, moe_norm_gain, moe_norm_bias]
    )
    small = jnp.concatenate([jnp.pad(vectors, ((0, 1), (0, 0))), w_router.T[order]])
    e_bias = jnp.concatenate(
        [
            expert_in_bias,
            jnp.pad(expert_out_bias, ((0, 0), (0, width - expert_out_bias.shape[1]))),
            jnp.zeros((14, width), BF16),
        ]
    )

    live = jnp.arange(n, dtype=jnp.int32) < image_count[0]
    member = (routes[:, :, 0:1] == order) | (routes[:, :, 1:2] == order)
    member = (member & live[:, None, None]).astype(BF16)
    lower = jnp.tril(jnp.ones((seq, seq), BF16), -1)
    earlier = jnp.einsum("ts,ise->ite", lower, member, preferred_element_type=F32)
    counts = jnp.sum(member.astype(F32), axis=1)
    base = jnp.cumsum(counts, axis=0) - counts
    position = (earlier + base[:, None, :]).astype(jnp.int32)
    slots = jnp.where((member > 0) & (position < capacity), position, -1)
    slots = jnp.pad(slots, ((0, 0), (0, sp - seq), (0, 0)), constant_values=-1)
    slot_rows = slots.transpose(2, 0, 1).reshape(8, 1, n * sp)

    (
        joint, weights, mixed, attended, routed, probs,
        cots, pieces, w_qkv_full, w_out_full, rows_s, gates_s, vec, router,
    ) = gather_forward(
        images, cotangent, slot_rows, w_qkv, w_attn_out, small, expert_in, expert_out, e_bias, sp, cap
    )
    grows, ggs, answers_l, answers_s, g_own, g_far, far_in = run_experts(
        slot_rows, routed.reshape(n * sp, width), probs.reshape(n * sp, 128), cots, pieces, rows_s, gates_s
    )
    output, grad_images, g_qkv, g_out, g_small, e_in, e_out, e_bias = backward_all(
        image_count, images, cotangent, joint, weights, mixed, attended, routed, probs, slots,
        w_qkv_full, w_out_full, vec, router, grows, ggs, answers_l, answers_s, g_own, g_far, far_in,
    )
    quarter = width // 4
    g_bias_out = lax.dynamic_slice_in_dim(e_bias[1:2], shard * quarter, quarter, 1)
    return (
        output,
        grad_images,
        g_small[0],
        g_small[1],
        g_qkv,
        g_small[2],
        g_small[3],
        g_out,
        g_small[4],
        g_small[5],
        g_small[6],
        g_small[8:16].T,
        e_in,
        e_bias[0:1],
        e_out,
        g_bias_out,
    )


def solution(mesh):
    in_specs = (
        P(("expert", "wshard"), None, None),
        P(("expert", "wshard"), None, None),
        P(("expert", "wshard")),
        P(("expert", "wshard"), None, None),
        P("wshard"),
        P("wshard"),
        P("wshard", None),
        P("wshard"),
        P("wshard"),
        P("wshard", None),
        P("wshard"),
        P("wshard"),
        P("wshard"),
        P("wshard", None),
        P("expert", None, "wshard"),
        P("expert", "wshard"),
        P("expert", "wshard", None),
        P("expert", "wshard"),
    )
    out_specs = (
        P(("expert", "wshard"), None, None),
        P(("expert", "wshard"), None, None),
        P("wshard"),
        P("wshard"),
        P("wshard", None),
        P("wshard"),
        P("wshard"),
        P("wshard", None),
        P("wshard"),
        P("wshard"),
        P("wshard"),
        P("wshard", None),
        P("expert", None, "wshard"),
        P("expert", "wshard"),
        P("expert", "wshard", None),
        P("expert", "wshard"),
    )
    small_slice = mesh.shape["expert"] == 8 and mesh.shape["wshard"] == 4
    body = weight_body if small_slice else token_body
    return jax.shard_map(body, mesh=mesh, in_specs=in_specs, out_specs=out_specs, check_vma=False)
```

```python
import functools

import jax
import jax.numpy as jnp
from jax import lax
from jax.experimental import pallas as pl
from jax.experimental.pallas import tpu as pltpu
from jax.sharding import PartitionSpec as P

HEADS = 8


norm_eps = 1e-06


def layer_norm(values, gain, bias):
    centre = values - jnp.mean(values, axis=-1, keepdims=True)
    spread = jnp.mean(centre * centre, axis=-1, keepdims=True)
    return centre * lax.rsqrt(spread + norm_eps) * gain + bias


def take_share(full, shard_index, shard_count):
    piece = full.shape[0] // shard_count
    return lax.dynamic_slice_in_dim(full, shard_index * piece, piece, 0)


def place_rows(slot_index, rows_here, total_slots):
    buffer = (
        jnp.zeros((total_slots + 1, rows_here.shape[1]), rows_here.dtype)
        .at[slot_index]
        .set(rows_here)
    )
    return buffer[:total_slots]


def token_body(
    images,
    cotangent,
    image_count,
    routes,
    attn_norm_gain,
    attn_norm_bias,
    w_qkv,
    b_query,
    b_value,
    w_attn_out,
    b_attn_out,
    moe_norm_gain,
    moe_norm_bias,
    w_router,
    expert_in,
    expert_in_bias,
    expert_out,
    expert_out_bias,
):
    image_slots, seq_len, model_width = images.shape
    tok_count = image_slots * seq_len
    experts = lax.axis_size("expert")
    shard_count = lax.axis_size("wshard")
    shard_index = lax.axis_index("wshard")
    capacity = (2 * tok_count + experts - 1) // experts
    total_slots = experts * capacity
    head_dim = model_width // HEADS
    score_scale = head_dim ** (-0.5)
    gathered = (
        lax.all_gather(attn_norm_gain, "wshard", axis=0, tiled=True),
        lax.all_gather(attn_norm_bias, "wshard", axis=0, tiled=True),
        lax.all_gather(w_qkv, "wshard", axis=0, tiled=True),
        lax.all_gather(b_query, "wshard", axis=0, tiled=True),
        lax.all_gather(b_value, "wshard", axis=0, tiled=True),
        lax.all_gather(w_attn_out, "wshard", axis=0, tiled=True),
        lax.all_gather(b_attn_out, "wshard", axis=0, tiled=True),
        lax.all_gather(moe_norm_gain, "wshard", axis=0, tiled=True),
        lax.all_gather(moe_norm_bias, "wshard", axis=0, tiled=True),
        lax.all_gather(w_router, "wshard", axis=0, tiled=True),
    )
    gain_one = gathered[0].astype(jnp.float32)
    bias_one = gathered[1].astype(jnp.float32)
    query_key_value_weight = gathered[2]
    query_bias = gathered[3].astype(jnp.float32)
    value_bias = gathered[4].astype(jnp.float32)
    projection_weight = gathered[5]
    projection_bias = gathered[6].astype(jnp.float32)
    gain_two = gathered[7].astype(jnp.float32)
    bias_two = gathered[8].astype(jnp.float32)
    router_weight = gathered[9]
    live_tokens = jnp.repeat(
        (jnp.arange(image_slots, dtype=jnp.int32) < image_count[0]).astype(jnp.float32), seq_len
    )
    inputs = images.astype(jnp.float32).reshape(tok_count, model_width)
    normed_one, norm_one_back = jax.vjp(layer_norm, inputs, gain_one, bias_one)
    hidden_state = normed_one.astype(jnp.bfloat16)
    merged_bias = jnp.concatenate([query_bias, jnp.zeros((model_width,), jnp.float32), value_bias])
    merged_rows = (
        jnp.dot(hidden_state, query_key_value_weight, preferred_element_type=jnp.float32)
        + merged_bias
    ).astype(jnp.bfloat16)
    queries = merged_rows[:, :model_width].reshape(image_slots, seq_len, HEADS, head_dim)
    key_rows = merged_rows[:, model_width : 2 * model_width].reshape(
        image_slots, seq_len, HEADS, head_dim
    )
    value_rows = merged_rows[:, 2 * model_width :].reshape(image_slots, seq_len, HEADS, head_dim)
    scores = (
        jnp.einsum("slhc,smhc->shlm", queries, key_rows, preferred_element_type=jnp.float32)
        * score_scale
    )
    log_total = jax.nn.logsumexp(scores, axis=-1, keepdims=True)
    weights = jnp.exp(scores - log_total).astype(jnp.bfloat16)
    blended_rows = (
        jnp.einsum("shlm,smhc->slhc", weights, value_rows, preferred_element_type=jnp.float32)
        .astype(jnp.bfloat16)
        .reshape(tok_count, model_width)
    )
    attended = (
        inputs
        + jnp.dot(blended_rows, projection_weight, preferred_element_type=jnp.float32)
        + projection_bias
    )
    normed_two, norm_two_back = jax.vjp(layer_norm, attended, gain_two, bias_two)
    routed = normed_two.astype(jnp.bfloat16)
    logits = jnp.dot(routed, router_weight, preferred_element_type=jnp.float32)
    router_probs = jax.nn.softmax(logits, axis=-1)
    route_pairs = routes.reshape(tok_count, 2)
    gate_values = jnp.take_along_axis(router_probs, route_pairs, axis=1)
    pair_expert = route_pairs.reshape(2 * tok_count)
    pair_live = jnp.repeat(live_tokens, 2) > 0.5
    onehot = (
        (pair_expert[:, None] == jnp.arange(experts, dtype=jnp.int32)[None, :]) & pair_live[:, None]
    ).astype(jnp.int32)
    earlier = jnp.cumsum(onehot, axis=0) - onehot
    position = jnp.sum(earlier * onehot, axis=1)
    keeping = pair_live & (position < capacity)
    slot_index = jnp.where(keeping, pair_expert * capacity + position, total_slots)
    outgoing = place_rows(slot_index, jnp.repeat(routed, 2, axis=0), total_slots).reshape(
        experts, capacity, model_width
    )
    arrived = lax.all_to_all(outgoing, "expert", split_axis=0, concat_axis=0, tiled=True).reshape(
        total_slots, model_width
    )
    full_in, full_in_bias, full_out, full_out_bias = (
        lax.all_gather(expert_in, "wshard", axis=2, tiled=True),
        lax.all_gather(expert_in_bias, "wshard", axis=1, tiled=True),
        lax.all_gather(expert_out, "wshard", axis=1, tiled=True),
        lax.all_gather(expert_out_bias, "wshard", axis=1, tiled=True),
    )
    full_in = full_in[0]
    full_out = full_out[0]
    before = jnp.dot(arrived, full_in, preferred_element_type=jnp.float32) + full_in_bias[0].astype(
        jnp.float32
    )
    active, gelu_back = jax.vjp(jax.nn.gelu, before)
    active = active.astype(jnp.bfloat16)
    leaving = (
        jnp.dot(active, full_out, preferred_element_type=jnp.float32)
        + full_out_bias[0].astype(jnp.float32)
    ).astype(jnp.bfloat16)
    coming_back = lax.all_to_all(
        leaving.reshape(experts, capacity, model_width),
        "expert",
        split_axis=0,
        concat_axis=0,
        tiled=True,
    )
    padded = jnp.concatenate(
        [coming_back.reshape(total_slots, model_width), jnp.zeros((1, model_width), jnp.bfloat16)],
        axis=0,
    )
    picked = padded[slot_index].reshape(tok_count, 2, model_width).astype(jnp.float32)
    combined = jnp.sum(gate_values[:, :, None] * picked, axis=1)
    output = (
        ((attended + combined) * live_tokens[:, None])
        .astype(jnp.bfloat16)
        .reshape(image_slots, seq_len, model_width)
    )
    grad_out = cotangent.astype(jnp.float32).reshape(tok_count, model_width) * live_tokens[:, None]
    grad_gates = jnp.einsum("td,tkd->tk", grad_out, picked)
    pair_grads = (
        (gate_values[:, :, None] * grad_out[:, None, :])
        .reshape(2 * tok_count, model_width)
        .astype(jnp.bfloat16)
    )
    outgoing_grads = place_rows(slot_index, pair_grads, total_slots).reshape(
        experts, capacity, model_width
    )
    arrived_grads = lax.all_to_all(
        outgoing_grads, "expert", split_axis=0, concat_axis=0, tiled=True
    ).reshape(total_slots, model_width)
    grad_active = jnp.einsum(
        "rd,hd->rh", arrived_grads, full_out, preferred_element_type=jnp.float32
    )
    grad_before = gelu_back(grad_active)[0].astype(jnp.bfloat16)
    grad_full_out = jnp.einsum(
        "rh,rd->hd", active, arrived_grads, preferred_element_type=jnp.float32
    )
    grad_full_out_bias = jnp.sum(arrived_grads.astype(jnp.float32), axis=0)
    grad_full_in = jnp.einsum("rd,rh->dh", arrived, grad_before, preferred_element_type=jnp.float32)
    grad_full_in_bias = jnp.sum(grad_before.astype(jnp.float32), axis=0)
    grad_arrived = jnp.einsum(
        "rh,dh->rd", grad_before, full_in, preferred_element_type=jnp.float32
    ).astype(jnp.bfloat16)
    expert_grads = (
        lax.psum_scatter(grad_full_in[None], "wshard", scatter_dimension=2, tiled=True),
        lax.psum_scatter(grad_full_in_bias[None], "wshard", scatter_dimension=1, tiled=True),
        lax.psum_scatter(grad_full_out[None], "wshard", scatter_dimension=1, tiled=True),
        lax.psum_scatter(grad_full_out_bias[None], "wshard", scatter_dimension=1, tiled=True),
    )
    returned_grads = lax.all_to_all(
        grad_arrived.reshape(experts, capacity, model_width),
        "expert",
        split_axis=0,
        concat_axis=0,
        tiled=True,
    )
    padded_grads = jnp.concatenate(
        [
            returned_grads.reshape(total_slots, model_width),
            jnp.zeros((1, model_width), jnp.bfloat16),
        ],
        axis=0,
    )
    grad_routed = jnp.sum(
        padded_grads[slot_index].reshape(tok_count, 2, model_width).astype(jnp.float32), axis=1
    )
    route_onehot = (
        route_pairs[:, :, None] == jnp.arange(experts, dtype=jnp.int32)[None, None, :]
    ).astype(jnp.float32)
    grad_probs = jnp.einsum("tk,tke->te", grad_gates, route_onehot)
    grad_logits = (
        router_probs * (grad_probs - jnp.sum(router_probs * grad_probs, axis=-1, keepdims=True))
    ).astype(jnp.bfloat16)
    grad_router = jnp.einsum("td,te->de", routed, grad_logits, preferred_element_type=jnp.float32)
    grad_routed = grad_routed + jnp.einsum(
        "te,de->td", grad_logits, router_weight, preferred_element_type=jnp.float32
    )
    grad_attended, grad_gain_two, grad_bias_two = norm_two_back(grad_routed)
    grad_attended = grad_attended + grad_out
    grad_branch = grad_attended.astype(jnp.bfloat16)
    grad_proj = jnp.einsum(
        "td,te->de", blended_rows, grad_branch, preferred_element_type=jnp.float32
    )
    grad_proj_bias = jnp.sum(grad_branch.astype(jnp.float32), axis=0)
    grad_mixed = (
        jnp.einsum("te,de->td", grad_branch, projection_weight, preferred_element_type=jnp.float32)
        .astype(jnp.bfloat16)
        .reshape(image_slots, seq_len, HEADS, head_dim)
    )
    scores_again = (
        jnp.einsum("slhc,smhc->shlm", queries, key_rows, preferred_element_type=jnp.float32)
        * score_scale
    )
    probs_again = jnp.exp(scores_again - log_total)
    grad_weights = jnp.einsum(
        "slhc,smhc->shlm", grad_mixed, value_rows, preferred_element_type=jnp.float32
    )
    grad_values = jnp.einsum(
        "shlm,slhc->smhc", weights, grad_mixed, preferred_element_type=jnp.float32
    )
    grad_scores = (
        probs_again * (grad_weights - jnp.sum(probs_again * grad_weights, axis=-1, keepdims=True))
    ).astype(jnp.bfloat16)
    grad_queries = (
        jnp.einsum("shlm,smhc->slhc", grad_scores, key_rows, preferred_element_type=jnp.float32)
        * score_scale
    )
    grad_keys = (
        jnp.einsum("shlm,slhc->smhc", grad_scores, queries, preferred_element_type=jnp.float32)
        * score_scale
    )
    grad_joint = jnp.concatenate(
        [
            grad_queries.reshape(tok_count, model_width),
            grad_keys.reshape(tok_count, model_width),
            grad_values.reshape(tok_count, model_width),
        ],
        axis=1,
    ).astype(jnp.bfloat16)
    grad_qkv = jnp.einsum("td,te->de", hidden_state, grad_joint, preferred_element_type=jnp.float32)
    grad_query_bias = jnp.sum(grad_joint[:, :model_width].astype(jnp.float32), axis=0)
    grad_value_bias = jnp.sum(grad_joint[:, 2 * model_width :].astype(jnp.float32), axis=0)
    grad_hidden = jnp.einsum(
        "te,de->td", grad_joint, query_key_value_weight, preferred_element_type=jnp.float32
    )
    grad_inputs, grad_gain_one, grad_bias_one = norm_one_back(grad_hidden)
    grad_images = (grad_attended + grad_inputs).reshape(image_slots, seq_len, model_width)
    full_grads = (
        grad_gain_one,
        grad_bias_one,
        grad_qkv,
        grad_query_bias,
        grad_value_bias,
        grad_proj,
        grad_proj_bias,
        grad_gain_two,
        grad_bias_two,
        grad_router,
    )
    total_grads = lax.psum(
        (
            full_grads[0],
            full_grads[1],
            full_grads[2],
            full_grads[3],
            full_grads[4],
            full_grads[5],
            full_grads[6],
            full_grads[7],
            full_grads[8],
            full_grads[9],
        ),
        ("expert", "wshard"),
    )
    final_grads = tuple((take_share(item, shard_index, shard_count) for item in total_grads))
    return (
        output,
        grad_images,
        final_grads[0],
        final_grads[1],
        final_grads[2],
        final_grads[3],
        final_grads[4],
        final_grads[5],
        final_grads[6],
        final_grads[7],
        final_grads[8],
        final_grads[9],
        expert_grads[0],
        expert_grads[1],
        expert_grads[2],
        expert_grads[3],
    )


F32 = jnp.float32
BF16 = jnp.bfloat16
VMEM_LIMIT = 56 * 1024 * 1024
NN = (((1,), (0,)), ((), ()))
NT = (((1,), (1,)), ((), ()))
TN = (((0,), (0,)), ((), ()))
ROUTER_ROW = 8


def mm(a, b, dims=NN):
    return lax.dot_general(a, b, dims, preferred_element_type=F32)


def whole(shape):
    return pl.BlockSpec(shape, lambda *_: (0,) * len(shape))


def part(shape):
    return pl.BlockSpec((1,) + shape, lambda i: (i,) + (0,) * len(shape))


def params(*semantics):
    return pltpu.CompilerParams(
        dimension_semantics=semantics or None, vmem_limit_bytes=VMEM_LIMIT
    )


def cost(flops, nbytes):
    return pl.CostEstimate(flops=int(flops), bytes_accessed=int(nbytes), transcendentals=0)


def norm_parts(values):
    centre = values - jnp.mean(values, axis=-1, keepdims=True)
    rstd = lax.rsqrt(jnp.mean(centre * centre, axis=-1, keepdims=True) + norm_eps)
    return centre * rstd, rstd


def norm_back(grad, unit, rstd, gain):
    scaled = grad * gain
    return rstd * (
        scaled
        - jnp.mean(scaled, axis=-1, keepdims=True)
        - unit * jnp.mean(scaled * unit, axis=-1, keepdims=True)
    )


def padded_rows(ref, scratch):
    seq, rows = ref.shape[1], scratch.shape[0]
    scratch[rows - 16 : rows] = jnp.zeros((16, scratch.shape[1]), scratch.dtype)
    scratch[0:seq] = ref[0].astype(scratch.dtype)
    return scratch[...]


def half_mask(rows, half):
    return (lax.broadcasted_iota(jnp.int32, (rows, 128), 1) // 64) == half


def route_probs(rows, router):
    logits = mm(rows, router[...], NT)
    lane = lax.broadcasted_iota(jnp.int32, logits.shape, 1)
    logits = jnp.where(lane < 8, logits, -1e30)
    power = jnp.exp(logits - jnp.max(logits, axis=-1, keepdims=True))
    return power / jnp.sum(power, axis=-1, keepdims=True)


def forward_kernel(
    images, w_qkv, w_out, vec, router, joint_o, weights_o, mixed_o, attended_o, routed_o, probs_o, rows
):
    seq, width = images.shape[1:]
    inputs = padded_rows(images, rows)
    sp = rows.shape[0]
    unit, _ = norm_parts(inputs)
    hidden = (unit * vec[0:1] + vec[1:2]).astype(BF16)
    bias = jnp.concatenate([vec[2:3], jnp.zeros((1, width), F32), vec[3:4]], axis=1)
    joint_o[0] = (mm(hidden, w_qkv[...]) + bias).astype(BF16)
    scale = (width // HEADS) ** (-0.5)
    key_ok = lax.broadcasted_iota(jnp.int32, (sp, sp), 1) < seq
    for pair in range(HEADS // 2):
        cols = pair * 128
        q = joint_o[0, :, cols : cols + 128]
        k = joint_o[0, :, width + cols : width + cols + 128]
        v = joint_o[0, :, 2 * width + cols : 2 * width + cols + 128]
        total = jnp.zeros((sp, 128), F32)
        for half in range(2):
            sel = half_mask(sp, half)
            km = jnp.where(sel, k, 0)
            vm = jnp.where(sel, v, 0)
            scores = mm(q, km, NT) * scale
            scores = jnp.where(key_ok, scores, -1e30)
            top = jnp.max(scores, axis=-1, keepdims=True)
            power = jnp.exp(scores - top)
            weights = (power / jnp.sum(power, axis=-1, keepdims=True)).astype(BF16)
            weights_o[0, pair * 2 + half] = weights
            total = total + mm(weights, vm)
        mixed_o[0, :, cols : cols + 128] = total.astype(BF16)
    attended = inputs + mm(mixed_o[0], w_out[...]) + vec[4:5]
    attended_o[0] = attended
    unit, _ = norm_parts(attended)
    routed = (unit * vec[5:6] + vec[6:7]).astype(BF16)
    routed_o[0] = routed
    probs_o[0] = route_probs(routed, router)


def attention_forward(images, w_qkv, w_out, vec, router, sp):
    n, seq, width = images.shape
    shapes = [
        jax.ShapeDtypeStruct((n, sp, 3 * width), BF16),
        jax.ShapeDtypeStruct((n, HEADS, sp, sp), BF16),
        jax.ShapeDtypeStruct((n, sp, width), BF16),
        jax.ShapeDtypeStruct((n, sp, width), F32),
        jax.ShapeDtypeStruct((n, sp, width), BF16),
        jax.ShapeDtypeStruct((n, sp, 128), F32),
    ]
    return pl.pallas_call(
        forward_kernel,
        grid=(n,),
        in_specs=[
            part((seq, width)),
            whole(w_qkv.shape),
            whole(w_out.shape),
            whole(vec.shape),
            whole(router.shape),
        ],
        out_specs=[part(s.shape[1:]) for s in shapes],
        out_shape=shapes,
        scratch_shapes=[pltpu.VMEM((sp, width), F32)],
        compiler_params=params("arbitrary"),
        cost_estimate=cost(2 * n * seq * width * width * 10, 30e6),
        name="attention_forward",
    )(images, w_qkv, w_out, vec, router)


def hot_rows(slots, cap_rows):
    places = lax.broadcasted_iota(jnp.int32, (cap_rows, slots.shape[1]), 0)
    return jnp.where(places == slots, 1.0, 0.0).astype(BF16)


ROOT = 0.7978845608028654
CUBE = 0.044715


def hot_tokens(slots, r, cap_rows):
    places = lax.broadcasted_iota(jnp.int32, (slots.shape[0], cap_rows), 1)
    return jnp.where(places == slots[:, r : r + 1], 1.0, 0.0).astype(BF16)


def output_kernel(step, count, slots, attended, answers_l, answers_r, output):
    cap = answers_l.shape[1]
    total = attended[0]
    for r in range(8):
        rows = answers_l[r] if r < 4 else answers_r[r - 4]
        total = total + mm(hot_tokens(slots[0], r, cap), rows)
    live = (step < count[0]).astype(F32)
    output[0] = (total * live).astype(BF16)[0 : output.shape[1]]


def mm_split(a, b):
    high = a.astype(BF16)
    low = (a - high.astype(F32)).astype(BF16)
    return mm(high, b, NT) + mm(low, b, NT)


def early_kernel(
    step, count, images, cotangent, joint, weights, mixed, attended, routed, probs, slots,
    w_out, vec, router, grows, ggs, g_out, g_vec, rows, cots, g_attend, g_mix,
):
    seq, width = images.shape[1:]
    sp = rows.shape[0]
    cap = grows.shape[1]
    live = (step < count[0]).astype(F32)
    grad = padded_rows(cotangent, cots) * live
    lane = lax.broadcasted_iota(jnp.int32, (cap, 128), 1)
    g_routed = jnp.zeros((sp, width), F32)
    g_probs = jnp.zeros((sp, 128), F32)
    for r in range(8):
        hot = hot_tokens(slots[0], r, cap)
        g_routed = g_routed + mm(hot, grows[r])
        g_probs = g_probs + mm(hot, jnp.where(lane == r, ggs[r // 4], jnp.zeros((), BF16)))
    p = probs[0]
    g_logits = (p * (g_probs - jnp.sum(p * g_probs, axis=-1, keepdims=True))).astype(BF16)
    g_routed = g_routed + mm(g_logits, router[...])
    g_vec[8:16] += mm(g_logits, routed[0], TN)[0:8]
    unit, rstd = norm_parts(attended[0])
    g_vec[5:6] += jnp.sum(g_routed * unit, axis=0, keepdims=True)
    g_vec[6:7] += jnp.sum(g_routed, axis=0, keepdims=True)
    g_attended = grad + norm_back(g_routed, unit, rstd, vec[5:6])
    g_attend[...] = g_attended
    branch = g_attended.astype(BF16)
    g_vec[4:5] += jnp.sum(branch.astype(F32), axis=0, keepdims=True)
    g_out[...] += mm(mixed[0], branch, TN)
    g_mix[...] = mm(branch, w_out[...], NT).astype(BF16)


def attention_part(which, images, vec, joint, weights, g_mix, g_joint, g_qkv, g_sum, rows):
    width = images.shape[2]
    sp = rows.shape[0]
    half = width // 2
    scale = (width // HEADS) ** (-0.5)
    for pair in range(HEADS // 4):
        cols = which * half + pair * 128
        q = joint[0, :, cols : cols + 128]
        k = joint[0, :, width + cols : width + cols + 128]
        v = joint[0, :, 2 * width + cols : 2 * width + cols + 128]
        gm = g_mix[:, cols : cols + 128]
        g_q = jnp.zeros((sp, 128), F32)
        g_k = jnp.zeros((sp, 128), F32)
        g_v = jnp.zeros((sp, 128), F32)
        for side in range(2):
            sel = half_mask(sp, side)
            w = weights[0, pair * 2 + side]
            g_p = mm(gm, jnp.where(sel, v, 0), NT)
            wf = w.astype(F32)
            g_s = (wf * (g_p - jnp.sum(wf * g_p, axis=-1, keepdims=True))).astype(BF16)
            g_v = g_v + mm(w, jnp.where(sel, gm, 0), TN)
            g_q = g_q + mm(g_s, jnp.where(sel, k, 0))
            g_k = g_k + mm(g_s, jnp.where(sel, q, 0), TN)
        g_joint[:, cols : cols + 128] = (g_q * scale).astype(BF16)
        g_joint[:, width + cols : width + cols + 128] = (g_k * scale).astype(BF16)
        g_joint[:, 2 * width + cols : 2 * width + cols + 128] = g_v.astype(BF16)
    unit, _ = norm_parts(padded_rows(images, rows))
    hidden = (unit * vec[0:1] + vec[1:2]).astype(BF16)
    for third in range(3):
        cols = slice(third * width + which * half, third * width + (which + 1) * half)
        part_of = g_joint[:, cols]
        g_qkv[:, third * half : (third + 1) * half] += mm(hidden, part_of, TN)
        g_sum[0:1, cols] += jnp.sum(part_of.astype(F32), axis=0, keepdims=True)


def late_kernel(images, vec, w_qkv, rows, g_joint, g_attend, g_images):
    unit, rstd = norm_parts(padded_rows(images, rows))
    g_hidden = mm(g_joint[...], w_qkv[...], NT)
    g_in = g_attend[...] + norm_back(g_hidden, unit, rstd, vec[0:1])
    g_images[0] = g_in[0 : images.shape[1]]


MESH = pl.DeviceIdType.MESH
CUT = 352
HALF = 528


def partners():
    e, w = lax.axis_index("expert"), lax.axis_index("wshard")
    return {
        "z": {"expert": lax.rem(e + 2, 8)},
        "z_back": {"expert": lax.rem(e + 6, 8)},
        "x": {"expert": e + 1 - 2 * lax.rem(e, 2)},
        "y": {"wshard": lax.rem(w + 2, 4)},
        "core": {"wshard": w + 1 - 2 * lax.rem(w, 2)},
    }


def meet(devices):
    barrier = pltpu.get_barrier_semaphore()
    for device in devices:
        pl.semaphore_signal(barrier, inc=1, device_id=device, device_id_type=MESH)
    pl.semaphore_wait(barrier, len(devices))


def sender(send, recv, slot, device, src, dst):
    return pltpu.make_async_remote_copy(
        src_ref=src,
        dst_ref=dst,
        send_sem=send.at[slot],
        recv_sem=recv.at[slot],
        device_id=device,
        device_id_type=MESH,
    )


def any_space():
    return pl.BlockSpec(memory_space=pl.ANY)


def gather_kernel(
    images, cotangent, slot_rows, w_qkv, w_out, small, e_in, e_out, e_bias,
    joint_o, weights_o, mixed_o, attended_o, routed_o, probs_o,
    cots_o, pieces_o, qkv_o, out_o, rows_o, vec_o, router_o,
    rows, flat, placed, pack, qkv, out, smalls, vec, router, send, recv, local,
):
    step = pl.program_id(0)
    last = pl.num_programs(0) - 1
    w = lax.axis_index("wshard")
    to = partners()
    width = w_out.shape[1]
    cap = placed.shape[1]
    share = w_qkv.shape[0]
    w_core = w + 1 - 2 * lax.rem(w, 2)
    w_far = lax.rem(w + 2, 4)

    def rows_of(ref, which):
        return ref.at[pl.ds(pl.multiple_of(which * share, share), share)]

    dense = ((w_qkv, qkv, rows_of), (w_out, out, rows_of), (small, smalls, lambda r, i: r.at[i]))
    far = [sender(send, recv, i, to["y"], a, at(b, w)) for i, (a, b, at) in enumerate(dense)]
    near = [sender(send, recv, 3 + i, to["core"], a, at(b, w)) for i, (a, b, at) in enumerate(dense)]
    onward = [
        sender(send, recv, 6 + i, to["core"], at(b, w_far), at(b, w_far))
        for i, (a, b, at) in enumerate(dense)
    ]
    first, rest = pl.ds(0, HALF), pl.ds(HALF, pack.shape[0] - HALF)
    spread = [
        sender(send, recv, 9, to["z"], pack.at[first], pieces_o.at[4, first]),
        sender(send, recv, 10, to["y"], pack, pieces_o.at[2]),
        sender(send, recv, 11, to["core"], pack, pieces_o.at[1]),
        sender(send, recv, 16, to["z"], pack.at[rest], pieces_o.at[4, rest]),
    ]
    ahead = sender(send, recv, 17, to["z"], pieces_o.at[4, first], pieces_o.at[5, first])
    cots = [
        sender(send, recv, 12 + k, to["x"], placed.at[4 + k], cots_o.at[k, cap : 2 * cap])
        for k in range(4)
    ]
    kept = [
        pltpu.make_async_copy(placed.at[k], cots_o.at[k, 0:cap], local.at[k]) for k in range(4)
    ]
    sent = [
        pltpu.make_async_copy(placed.at[k], rows_o.at[k], local.at[7 + k]) for k in range(4)
    ]
    saved = [
        pltpu.make_async_copy(qkv, qkv_o, local.at[4]),
        pltpu.make_async_copy(out, out_o, local.at[5]),
        pltpu.make_async_copy(pack, pieces_o.at[0], local.at[6]),
    ]

    @pl.when(step == 0)
    def _():
        meet(list(to.values()))
        for copy in far + near:
            copy.start()
        pack[0:width] = e_in[0]
        pack[width : 2 * width] = e_out[0]
        pack[2 * width : 2 * width + 16] = e_bias[...]
        spread[0].start()
        mine = pl.ds(pl.multiple_of(w * share, share), share)
        qkv[mine] = w_qkv[...]
        out[mine] = w_out[...]
        smalls[w] = small[...]
        n, seq = cotangent.shape[:2]
        sp = flat.shape[0] // n
        for i in range(n):
            flat[(i + 1) * sp - 16 : (i + 1) * sp] = jnp.zeros((16, width), BF16)
            flat[i * sp : i * sp + seq] = cotangent[i]
        for k in range(4):
            placed[4 + k] = mm(hot_rows(slot_rows[4 + k], cap), flat[...]).astype(BF16)
            cots[k].start()
        for copy in far:
            copy.wait_recv()
        for copy in onward + spread[1:]:
            copy.start()
        for k in range(4):
            placed[k] = mm(hot_rows(slot_rows[k], cap), flat[...]).astype(BF16)
            kept[k].start()
        for copy in near + onward:
            copy.wait_recv()
        for copy in far + near + onward:
            copy.wait_send()
        vec[...] = jnp.concatenate([smalls[i] for i in range(4)], axis=1).astype(F32)
        router[...] = jnp.zeros_like(router)
        router[0:8] = vec[8:16].astype(BF16)
        vec_o[...] = vec[...]
        router_o[...] = router[...]
        for copy in saved:
            copy.start()

    @pl.when(step == last - 3)
    def _():
        spread[0].wait_recv()
        spread[3].wait_send()
        ahead.start()

    forward_kernel(
        images, qkv, out, vec, router, joint_o, weights_o, mixed_o, attended_o, routed_o,
        probs_o, rows,
    )

    sp = rows.shape[0]
    band = pl.ds(pl.multiple_of(step * sp, sp), sp)
    flat[band] = routed_o[0]

    @pl.when(step == last)
    def _():
        for copy in kept + saved:
            copy.wait()
        for k in range(4):
            placed[k] = mm(hot_rows(slot_rows[4 + k], cap), flat[...]).astype(BF16)
            sent[k].start()
        for copy in sent:
            copy.wait()
        for copy in cots + [spread[1], spread[2], ahead]:
            copy.wait()
        spread[3].wait_recv()
        spread[0].wait_send()


def gather_forward(images, cotangent, slot_rows, w_qkv, w_out, small, e_in, e_out, e_bias, sp, cap):
    n, seq, width = images.shape
    piece = 2 * width + 16
    blocks = [
        jax.ShapeDtypeStruct((n, sp, 3 * width), BF16),
        jax.ShapeDtypeStruct((n, HEADS, sp, sp), BF16),
        jax.ShapeDtypeStruct((n, sp, width), BF16),
        jax.ShapeDtypeStruct((n, sp, width), F32),
        jax.ShapeDtypeStruct((n, sp, width), BF16),
        jax.ShapeDtypeStruct((n, sp, 128), F32),
    ]
    far = [
        jax.ShapeDtypeStruct((4, 2 * cap, width), BF16),
        jax.ShapeDtypeStruct((6, piece, width), BF16),
        jax.ShapeDtypeStruct((width, 3 * width), BF16),
        jax.ShapeDtypeStruct((width, width), BF16),
        jax.ShapeDtypeStruct((4, cap, width), BF16),
    ]
    small_shapes = [
        jax.ShapeDtypeStruct((16, width), F32),
        jax.ShapeDtypeStruct((128, width), BF16),
    ]
    return pl.pallas_call(
        gather_kernel,
        grid=(n,),
        in_specs=[part((seq, width))]
        + [
            whole(a.shape)
            for a in (cotangent, slot_rows, w_qkv, w_out, small, e_in, e_out, e_bias)
        ],
        out_specs=[part(s.shape[1:]) for s in blocks]
        + [any_space()] * 5
        + [whole(s.shape) for s in small_shapes],
        out_shape=blocks + far + small_shapes,
        scratch_shapes=[
            pltpu.VMEM((sp, width), F32),
            pltpu.VMEM((n * sp, width), BF16),
            pltpu.VMEM((8, cap, width), BF16),
            pltpu.VMEM((piece, width), BF16),
            pltpu.VMEM((width, 3 * width), BF16),
            pltpu.VMEM((width, width), BF16),
            pltpu.VMEM((4, 16, width // 4), BF16),
            pltpu.VMEM((16, width), F32),
            pltpu.VMEM((128, width), BF16),
            pltpu.SemaphoreType.DMA((18,)),
            pltpu.SemaphoreType.DMA((18,)),
            pltpu.SemaphoreType.DMA((11,)),
        ],
        compiler_params=pltpu.CompilerParams(
            dimension_semantics=("arbitrary",),
            vmem_limit_bytes=VMEM_LIMIT,
            collective_id=0,
            has_side_effects=True,
        ),
        cost_estimate=cost(2 * n * seq * width * width * 20, 40e6),
        name="gather_forward",
    )(images, cotangent, slot_rows, w_qkv, w_out, small, e_in, e_out, e_bias)


def add16(a, b):
    return (a.astype(F32) + b.astype(F32)).astype(BF16)


def once(shape):
    return pl.BlockSpec(shape, lambda *_: (0,) * len(shape), pipeline_mode=pl.Buffered(1))


def experts_kernel(
    slot_rows, routed, router, cots, pieces, rows_s,
    grows_o, ggs_o, answers_o, sent_o, own_o, far_o, far_in,
    weights, rows, grad, core_in, ans_s, grow_s, ans_b, grow_b, gg_b,
    send, recv, local,
):
    k = pl.program_id(0)
    w = lax.axis_index("wshard")
    to = partners()
    cap = rows.shape[1] // 2
    width = rows.shape[2]
    near, away = pl.ds(0, cap), pl.ds(cap, cap)

    def link(slot, device, src, dst):
        return sender(send, recv, slot, to[device], src, dst)

    first, rest = pl.ds(0, HALF), pl.ds(HALF, pieces.shape[1] - HALF)
    shared = [None, None, pl.ds(0, CUT), rest]
    other = [None, None, pl.ds(CUT, pieces.shape[1] - CUT), first]
    loads = [
        pltpu.make_async_copy(src, dst, local.at[j])
        for j, (src, dst) in enumerate(
            (
                (pieces.at[0], weights.at[0, 0]),
                (pieces.at[1], weights.at[0, 1]),
                (pieces.at[2], weights.at[0, 2]),
                (pieces.at[4], weights.at[1, 0]),
                (pieces.at[5, first], weights.at[2, 0, first]),
            )
        )
    ]
    ring = [
        link(0, "z", pieces.at[4, rest], weights.at[2, 0, rest]),
        link(1, "z", pieces.at[5, first], weights.at[3, 0, first]),
        link(2, "z", weights.at[2, 0, rest], weights.at[3, 0, rest]),
    ]
    ride = [None, None] + [
        link(3, "z", weights.at[1, 2, shared[2]], weights.at[2, 2, shared[2]]),
        link(4, "z", weights.at[2, 2, shared[3]], weights.at[3, 2, shared[3]]),
    ]
    held = [None, pieces.at[4], weights.at[2, 0], weights.at[3, 0]]
    beside = [None] + [link(37 + i, "core", held[i], weights.at[i, 1]) for i in (1, 2, 3)]
    across = [None, link(5, "y", held[1], weights.at[1, 2])] + [
        link(4 + i, "y", held[i].at[other[i]], weights.at[i, 2, other[i]]) for i in (2, 3)
    ]
    onward = [link(8, "core", pieces.at[2], weights.at[0, 3])] + [
        link(8 + i, "core", weights.at[i, 2], weights.at[i, 3]) for i in (1, 2, 3)
    ]
    rows_out = [link(12 + i, "x", rows_s.at[i], rows.at[i, away]) for i in range(4)]
    slot = lax.rem(k, 2)
    grow_out = link(20 + k, "x", grow_b.at[k, away], grows_o.at[4 + k])
    gg_out = link(24, "x", gg_b.at[away], ggs_o.at[1])
    gg_own = pltpu.make_async_copy(gg_b.at[near], ggs_o.at[0], local.at[28])
    core_out = [
        link(28 + 2 * k + i, "core", grad.at[1 + 2 * i], core_in.at[slot, i]) for i in range(2)
    ]
    far_out = link(36, "y", far_o.at[1], far_in)

    def results(j):
        return [
            pltpu.make_async_copy(src, dst, local.at[5 + 5 * j + i])
            for i, (src, dst) in enumerate(
                (
                    (grow_b.at[j, near], grows_o.at[j]),
                    (ans_b.at[j, near], answers_o.at[j]),
                    (ans_b.at[j, away], sent_o.at[j]),
                    (grad.at[0], own_o.at[j]),
                    (grad.at[2], far_o.at[j]),
                )
            )
        ]

    @pl.when(k == 0)
    def _():
        for copy in loads:
            copy.start()
        gg_b[...] = jnp.zeros_like(gg_b)
        meet(list(to.values()))
        for copy in (ring[0], across[1], beside[1], onward[0]):
            copy.start()
        rows_out[0].start()
        for r in range(4):
            rows[r, 0:cap] = mm(hot_rows(slot_rows[r], cap), routed[...]).astype(BF16)
        rows_out[0].wait_send()
        rows_out[1].start()
        for copy in loads:
            copy.wait()
        onward[0].wait_recv()

    for i in (1, 2, 3):

        @pl.when(k == i)
        def _(i=i):
            beside[i].wait_recv()

    for i in range(4):

        @pl.when(k == i)
        def _(i=i):
            rows_out[i].wait_recv()

    x = rows[k]
    cot = cots[k].astype(F32)
    lane = lax.broadcasted_iota(jnp.int32, gg_b.shape, 1)
    gate = jnp.sum(jnp.where(lane == k, route_probs(x, router), 0.0), axis=1, keepdims=True)
    scaled = (cot * gate).astype(BF16)
    g_bias_out = jnp.sum(scaled.astype(F32), axis=0, keepdims=True)
    for turn, q in enumerate((1, 0, 3, 2)):
        if turn == 2:
            for i in (1, 2, 3):

                @pl.when(k == i)
                def _(i=i):
                    onward[i].wait_recv()

        w_in = weights[k, q, 0:width]
        w_out = weights[k, q, width : 2 * width]
        before = mm(x, w_in) + weights[k, q, 2 * width : 2 * width + 16].astype(F32)[0:1]
        square = before * before
        inner = before * (ROOT + ROOT * CUBE * square)
        curve = jnp.tanh(inner)
        half = 0.5 * curve + 0.5
        active = (before * half).astype(BF16)
        slope = half + (0.5 * before) * (1.0 - curve * curve) * (ROOT + 3.0 * ROOT * CUBE * square)
        grad_active = mm(scaled, w_out, NT)
        grad_before = (grad_active * slope).astype(BF16)
        if turn == 0:
            ans_s[...] = mm(active, w_out)
            grow_s[...] = mm(grad_before, w_in, NT)
        else:
            ans_s[...] += mm(active, w_out)
            grow_s[...] += mm(grad_before, w_in, NT)
        g_bias_in = jnp.sum(grad_before.astype(F32), axis=0, keepdims=True)
        tail = lax.broadcasted_iota(jnp.int32, (16, width), 0)

        @pl.when(k > 0)
        def _(q=q):
            if q % 2:
                link(28 + 2 * (k - 1) + q // 2, "core", grad.at[q], core_in.at[1 - slot, q // 2]).wait_send()
            elif q == 0:
                results(k - 1)[3].wait()

        if q == 2:

            @pl.when(k == 3)
            def _():
                results(2)[4].wait()

        grad[q, 0:width] = mm(x, grad_before, TN).astype(BF16)
        grad[q, width : 2 * width] = mm(active, scaled, TN).astype(BF16)
        grad[q, 2 * width : 2 * width + 16] = jnp.where(
            tail == 0, g_bias_in, jnp.where(tail == 1, g_bias_out, 0.0)
        ).astype(BF16)
        if q % 2:
            core_out[q // 2].start()
        if turn == 0:

            @pl.when(k == 0)
            def _():
                ring[0].wait_recv()
                for copy in (ring[1], beside[2]):
                    copy.start()

            @pl.when(k == 1)
            def _():
                results(0)[4].wait()

            @pl.when(k == 2)
            def _():
                results(1)[4].wait()
                ride[2].wait_recv()
                across[2].wait_recv()
                ring[1].wait_recv()
                for copy in (onward[2], across[3], ride[3]):
                    copy.start()

            @pl.when(k == 3)
            def _():
                ride[3].wait_recv()
                across[3].wait_recv()
                onward[3].start()

        if turn == 1:

            @pl.when(k == 2)
            def _():
                ring[2].wait_recv()
                beside[3].start()

        if turn == 2:

            @pl.when(k == 0)
            def _():
                rows_out[1].wait_send()
                rows_out[2].start()

            @pl.when(k == 1)
            def _():
                rows_out[2].wait_send()
                rows_out[3].start()

        if turn == 3:

            @pl.when(k == 0)
            def _():
                across[1].wait_recv()
                for copy in (onward[1], across[2], ride[2], ring[2]):
                    copy.start()

            @pl.when(k == 2)
            def _():
                far_out.start()

    bias = []
    for j in range(4):
        q = lax.rem(j + w, 2) + 2 * lax.rem(j // 2 + w // 2, 2)
        bias.append(weights[k, q, 2 * width : 2 * width + 16, 0:128].astype(F32)[1:2])
    bias_out = jnp.concatenate(bias, axis=1)
    answer = (ans_s[...] + bias_out).astype(BF16).astype(F32)
    gg = jnp.sum(answer * cot, axis=1, keepdims=True)
    row = lax.broadcasted_iota(jnp.int32, gg_b.shape, 0)
    own_lane = k + jnp.where(row >= cap, 4, 0)
    gg_b[...] = jnp.where(lane == own_lane, gg, gg_b[...].astype(F32)).astype(BF16)
    grow_b[k] = grow_s[...].astype(BF16)
    grow_out.start()
    ans_b[k] = (answer * gate).astype(BF16)
    for copy in core_out:
        copy.wait_recv()
    grad[0] = add16(grad[0], core_in[slot, 0])
    grad[2] = add16(grad[2], core_in[slot, 1])
    done = results(k)
    for copy in done:
        copy.start()

    @pl.when(k == 3)
    def _():
        gg_out.start()
        gg_own.start()
        for copy in core_out:
            copy.wait_send()
        done[3].wait()
        done[4].wait()
        for j in range(4):
            for copy in results(j)[:3]:
                copy.wait()
            link(20 + j, "x", grow_b.at[j, away], grows_o.at[4 + j]).wait()
        for copy in ring + ride[2:] + beside[1:] + across[1:] + onward:
            copy.wait_send()
        rows_out[3].wait_send()
        gg_out.wait()
        gg_own.wait()
        far_out.wait()


def run_experts(slot_rows, routed, router, cots, pieces, rows_s):
    _, both, width = cots.shape
    cap = both // 2
    piece = pieces.shape[1]
    shapes = [
        jax.ShapeDtypeStruct((8, cap, width), BF16),
        jax.ShapeDtypeStruct((2, cap, 128), BF16),
        jax.ShapeDtypeStruct((4, cap, width), BF16),
        jax.ShapeDtypeStruct((4, cap, width), BF16),
        jax.ShapeDtypeStruct((4, piece, width), BF16),
        jax.ShapeDtypeStruct((4, piece, width), BF16),
        jax.ShapeDtypeStruct((piece, width), BF16),
    ]
    return pl.pallas_call(
        experts_kernel,
        grid=(4,),
        in_specs=[once(a.shape) for a in (slot_rows, routed, router, cots)] + [any_space()] * 2,
        out_specs=[any_space()] * len(shapes),
        out_shape=shapes,
        scratch_shapes=[
            pltpu.VMEM((4, 4, piece, width), BF16),
            pltpu.VMEM((4, both, width), BF16),
            pltpu.VMEM((4, piece, width), BF16),
            pltpu.VMEM((2, 2, piece, width), BF16),
            pltpu.VMEM((both, width), F32),
            pltpu.VMEM((both, width), F32),
            pltpu.VMEM((4, both, width), BF16),
            pltpu.VMEM((4, both, width), BF16),
            pltpu.VMEM((both, 128), BF16),
            pltpu.SemaphoreType.DMA((41,)),
            pltpu.SemaphoreType.DMA((41,)),
            pltpu.SemaphoreType.DMA((29,)),
        ],
        compiler_params=pltpu.CompilerParams(
            dimension_semantics=("arbitrary",),
            vmem_limit_bytes=62 * 1024 * 1024,
            collective_id=1,
            has_side_effects=True,
        ),
        cost_estimate=cost(2 * 2 * cap * width * width * 4 * 6 * 4, 60e6),
        name="run_experts",
    )(slot_rows, routed, router, cots, pieces, rows_s)


SUMS = ((16, 0, 0), (17, 0, 1), (19, 1, 0), (20, 2, 0), (21, 1, 1), (22, 2, 1), (22, 3, 0), (23, 3, 1), (23, 4, 0))


def backward_all_kernel(
    count, images, cotangent, joint, weights, mixed, attended, routed, probs, slots,
    w_qkv, w_out, vec, router, grows, ggs, answers_l, answers_s, own, far, far_in,
    output, g_images, g_qkv_o, g_out_o, g_small_o, e_in_o, e_out_o, e_bias_o,
    rows, cots, g_joints, g_attends, g_mixes, g_near, g_away, g_out, g_vec, g_sum, g_rows,
    answers_r, mine, far_got, ring_got,
    dense_a, core_a, y_a, ours_a, x_a, z_a, all_a, dense_b, core_b, y_b, ours_b, x_b, z_b, all_b,
    send, recv, local,
):
    step = pl.program_id(0)
    n = pl.num_programs(0) // 3
    e, w = lax.axis_index("expert"), lax.axis_index("wshard")
    to = partners()
    zs = [{"expert": lax.rem(e + 2 * d, 8)} for d in range(1, 4)]
    e_x, e_z = lax.rem(e, 2), e // 2
    width = w_out.shape[0]
    quarter = width // 4
    part_rows = quarter // 8
    half = width // 2
    w_core = w + 1 - 2 * lax.rem(w, 2)
    w_far = lax.rem(w + 2, 4)
    w_last = lax.rem(w_core + 2, 4)

    def load(j):
        pairs = [(own.at[i], mine.at[i]) for i in range(4)]
        pairs += [(far_in, far_got.at[1])]
        return pltpu.make_async_copy(*pairs[j], local.at[j])

    def answer(k):
        return sender(send, recv, k, to["x"], answers_s.at[k], answers_r.at[k])

    def beyond(k):
        return sender(send, recv, 4 + k, to["y"], far.at[k], far_got.at[k])

    first, rest = pl.ds(0, HALF), pl.ds(HALF, mine.shape[1] - HALF)

    def ring(k):
        if k == 3:
            return sender(send, recv, 11, to["z"], mine.at[3, first], ring_got.at[3, first])
        return sender(send, recv, 8 + k, to["z"], mine.at[k], ring_got.at[k])

    def ring_rest():
        return sender(send, recv, 8, to["z"], mine.at[3, rest], ring_got.at[3, rest])

    sides = (
        (12, dense_a, core_a, y_a, ours_a, x_a, z_a, all_a),
        (23, dense_b, core_b, y_b, ours_b, x_b, z_b, all_b),
    )

    def core(side, i):
        base, dense, core_got = sides[side][:3]
        return sender(send, recv, base + i, to["core"], dense.at[(w_core, w_last)[i]], core_got.at[i])

    def y_side(side):
        base, dense, _, y_got = sides[side][:4]
        return sender(send, recv, base + 2, to["y"], dense.at[w_far], y_got)

    def x_half(which):
        return pl.ds(pl.multiple_of(which * 4 * part_rows, 4 * part_rows), 4 * part_rows)

    def x_side(side):
        base, ours, x_got = sides[side][0], sides[side][4], sides[side][5]
        return sender(send, recv, base + 3, to["x"], ours.at[x_half(1 - e_x)], x_got)

    def chunk(which):
        return pl.ds(
            pl.multiple_of(e_x * 4 * part_rows + which * part_rows, part_rows), part_rows
        )

    def scatter(side, d):
        base, ours, z_got = sides[side][0], sides[side][4], sides[side][6]
        src = ours.at[chunk(lax.rem(e_z + d, 4))]
        return sender(send, recv, base + 3 + d, zs[d - 1], src, z_got.at[d - 1])

    def share(side, d):
        base, every = sides[side][0], sides[side][7]
        return sender(send, recv, base + 6 + d, zs[d - 1], every.at[e_x, e_z], every.at[e_x, e_z])

    def x_share(side):
        base, every = sides[side][0], sides[side][7]
        return sender(send, recv, base + 10, to["x"], every.at[e_x], every.at[e_x])

    def core_done(side):
        _, dense, core_got, _, ours = sides[side][:5]
        for i in range(2):
            core(side, i).wait()
        dense[w_far] = add16(dense[w_far], core_got[1])
        y_side(side).start()
        ours[...] = add16(dense[w], core_got[0])

    def y_done(side):
        ours, y_got = sides[side][4], sides[side][3]
        y_side(side).wait()
        ours[...] = add16(ours[...], y_got[...])
        x_side(side).start()

    def x_done(side):
        ours, x_got = sides[side][4:6]
        x_side(side).wait()
        ours[x_half(e_x)] = add16(ours[x_half(e_x)], x_got[...])
        for d in range(1, 4):
            scatter(side, d).start()

    def z_done(side):
        ours, _, z_got, every = sides[side][4:8]
        for d in range(1, 4):
            scatter(side, d).wait_recv()
        total = ours[chunk(e_z)].astype(F32)
        for d in range(1, 4):
            total = total + z_got[d - 1].astype(F32)
        every[e_x, e_z] = total.astype(BF16)
        for d in range(1, 4):
            share(side, d).start()

    def share_done(side):
        for d in range(1, 4):
            share(side, d).wait_recv()
        x_share(side).start()

    def at(which):
        return pl.when(step == which)

    @at(0)
    def _():
        g_near[...] = jnp.zeros_like(g_near)
        g_away[...] = jnp.zeros_like(g_away)
        g_out[...] = jnp.zeros_like(g_out)
        g_vec[...] = jnp.zeros_like(g_vec)
        g_sum[...] = jnp.zeros_like(g_sum)
        for j in (1, 4, 0, 2, 3):
            load(j).start()
        meet([to["y"], to["core"], to["x"]] + zs)
        beyond(2).start()
        load(1).wait()
        load(4).wait()
        mine[1] = add16(mine[1], far_got[1])
        ring(1).start()
        for k in range(4):
            answer(k).start()

    for k, when in ((2, 6), (3, 2 * n)):

        @at(when)
        def _(k=k):
            if k == 2:
                for j in (0, 2, 3):
                    load(j).wait()
            beyond(k).wait_recv()
            ring(k - 1).wait_recv()
            total = mine[k].astype(F32) + far_got[k].astype(F32) + ring_got[k - 1].astype(F32)
            mine[k] = total.astype(BF16)
            ring(k).start()
            if k == 2:
                beyond(3).start()

    @pl.when(step < n)
    def _():
        early_kernel(
            step, count, images, cotangent, joint, weights, mixed, attended, routed, probs, slots,
            w_out, vec, router, grows, ggs, g_out, g_vec, rows, cots,
            g_attends.at[step], g_mixes.at[step],
        )
        attention_part(
            0, images, vec, joint, weights, g_mixes.at[step], g_joints.at[step], g_near, g_sum, rows
        )

    @at(n - 1)
    def _():
        for j in range(4):
            band = slice(j * quarter, (j + 1) * quarter)
            dense_a[j, :, 0 : 3 * half] = g_near[band].astype(BF16)
            dense_a[j, :, 3 * half :] = g_out[band].astype(BF16)
        for i in range(2):
            core(0, i).start()

    @pl.when((step >= n) & (step < 2 * n))
    def _():
        attention_part(
            1, images, vec, joint, weights, g_mixes.at[step - n], g_joints.at[step - n], g_away,
            g_sum, rows,
        )

    @at(2 * n - 1)
    def _():
        sums = g_sum[...]
        g_bias = (mm_split(sums, w_qkv[...]))[0:1]
        ones = jnp.ones((16, half), BF16)
        g_gain = jnp.zeros((16, width), F32)
        for third in range(3):
            for part_of, at_col in ((g_near, 0), (g_away, half)):
                col = third * width + at_col
                product = w_qkv[:, col : col + half].astype(F32)
                product = product * part_of[:, third * half : (third + 1) * half]
                high = product.astype(BF16)
                low = (product - high.astype(F32)).astype(BF16)
                g_gain = g_gain + mm(ones, high, NT) + mm(ones, low, NT)
        g_vec[0:1] = (g_gain[0:1] - vec[1:2] * g_bias) / vec[0:1]
        g_vec[1:2] = g_bias
        g_vec[2:3] = sums[0:1, 0:width]
        g_vec[3:4] = sums[0:1, 2 * width :]
        g_rows[0:8] = g_vec[0:8]
        for r in range(8):
            expert = lax.rem(e + 8 - 2 * (r % 4), 8)
            expert = expert if r < 4 else expert + 1 - 2 * lax.rem(expert, 2)
            g_rows[pl.ds(8 + expert, 1)] = g_vec[8 + r : 9 + r]
        dense_b[:, 16:quarter, 3 * half :] = jnp.zeros((4, quarter - 16, quarter), BF16)
        for j in range(4):
            band = slice(j * quarter, (j + 1) * quarter)
            dense_b[j, :, 0 : 3 * half] = g_away[band].astype(BF16)
            dense_b[j, 0:16, 3 * half :] = g_rows[:, band].astype(BF16)
        for i in range(2):
            core(1, i).start()

    @at(2 * n)
    def _():
        for k in range(4):
            answer(k).wait_recv()

    for when, stage, side in SUMS:

        @at(when)
        def _(stage=stage, side=side):
            (core_done, y_done, x_done, z_done, share_done)[stage](side)
            if (stage, side) == (1, 1):
                beyond(0).start()
            if (stage, side) == (3, 1):
                ring_rest().start()

    @pl.when(step >= 2 * n)
    def _():
        i = step - 2 * n
        late_kernel(images, vec, w_qkv, rows, g_joints.at[i], g_attends.at[i], g_images)
        output_kernel(i, count, slots, attended, answers_l, answers_r, output)

    @at(3 * n - 1)
    def _():
        share_done(1)
        for side in range(2):
            x_share(side).wait_recv()
        for i in range(8):
            band = slice(i * part_rows, (i + 1) * part_rows)
            near, away = all_a[i // 4, i % 4].astype(F32), all_b[i // 4, i % 4].astype(F32)
            for third in range(3):
                col = third * width
                cols = slice(third * half, (third + 1) * half)
                g_qkv_o[band, col : col + half] = near[:, cols]
                g_qkv_o[band, col + half : col + width] = away[:, cols]
            g_out_o[band] = near[:, 3 * half :]
            if i == 0:
                g_small_o[...] = away[0:16, 3 * half :]
        ring(3).wait_recv()
        ring_rest().wait_recv()
        beyond(0).wait_recv()
        total = mine[0].astype(F32) + far_got[0].astype(F32) + ring_got[3].astype(F32)
        e_in_o[0] = total[0:width]
        e_out_o[0] = total[width : 2 * width]
        e_bias_o[...] = total[2 * width : 2 * width + 16]
        for side in range(2):
            x_share(side).wait_send()
            for d in range(1, 4):
                scatter(side, d).wait_send()
                share(side, d).wait_send()
        for k in range(4):
            answer(k).wait_send()
        for k in (2, 3, 0):
            beyond(k).wait_send()
        for k in (1, 2, 3):
            ring(k).wait_send()
        ring_rest().wait_send()


def backward_all(
    count, images, cotangent, joint, weights, mixed, attended, routed, probs, slots,
    w_qkv, w_out, vec, router, grows, ggs, answers_l, answers_s, own, far, far_in,
):
    n, seq, width = images.shape
    sp = joint.shape[1]
    cap = grows.shape[1]
    piece = own.shape[1]
    quarter = width // 4
    half = width // 2

    def early(shape):
        return pl.BlockSpec((1,) + shape, lambda i: (jnp.minimum(i, n - 1),) + (0,) * len(shape))

    def image(i):
        return jnp.where(i < n, i, jnp.where(i < 2 * n, i - n, n - 1))

    def twice(shape):
        return pl.BlockSpec((1,) + shape, lambda i: (image(i),) + (0,) * len(shape))

    def halves(shape):
        half_heads = (1, shape[0] // 2) + shape[1:]
        return pl.BlockSpec(half_heads, lambda i: (image(i), jnp.where(i < n, 0, 1), 0, 0))

    def both(shape):
        return pl.BlockSpec((1,) + shape, lambda i: (lax.rem(i, n),) + (0,) * len(shape))

    def late(shape):
        return pl.BlockSpec((1,) + shape, lambda i: (jnp.maximum(i - 2 * n, 0),) + (0,) * len(shape))

    streams = [
        (images, both), (cotangent, early), (joint, twice), (weights, halves), (mixed, early),
        (attended, both), (routed, early), (probs, early), (slots, both),
    ]
    fixed = [w_qkv, w_out, vec, router, grows, ggs, answers_l]
    far_refs = [answers_s, own, far, far_in]
    shapes = [
        jax.ShapeDtypeStruct((n, seq, width), BF16),
        jax.ShapeDtypeStruct((n, seq, width), F32),
        jax.ShapeDtypeStruct((quarter, 3 * width), F32),
        jax.ShapeDtypeStruct((quarter, width), F32),
        jax.ShapeDtypeStruct((16, quarter), F32),
        jax.ShapeDtypeStruct((1, width, width), F32),
        jax.ShapeDtypeStruct((1, width, width), F32),
        jax.ShapeDtypeStruct((16, width), F32),
    ]

    def side(cols):
        return [
            pltpu.VMEM((4, quarter, cols), BF16),
            pltpu.VMEM((2, quarter, cols), BF16),
            pltpu.VMEM((quarter, cols), BF16),
            pltpu.VMEM((quarter, cols), BF16),
            pltpu.VMEM((quarter // 2, cols), BF16),
            pltpu.VMEM((3, quarter // 8, cols), BF16),
            pltpu.VMEM((2, 4, quarter // 8, cols), BF16),
        ]

    return pl.pallas_call(
        backward_all_kernel,
        grid=(3 * n,),
        in_specs=[pl.BlockSpec(memory_space=pltpu.SMEM)]
        + [kind(a.shape[1:]) for a, kind in streams]
        + [once(a.shape) for a in fixed]
        + [any_space()] * len(far_refs),
        out_specs=[late((seq, width)), late((seq, width))] + [whole(s.shape) for s in shapes[2:]],
        out_shape=shapes,
        scratch_shapes=[
            pltpu.VMEM((sp, width), F32),
            pltpu.VMEM((sp, width), F32),
            pltpu.VMEM((n, sp, 3 * width), BF16),
            pltpu.VMEM((n, sp, width), F32),
            pltpu.VMEM((n, sp, width), BF16),
            pltpu.VMEM((width, 3 * half), F32),
            pltpu.VMEM((width, 3 * half), F32),
            pltpu.VMEM((width, width), F32),
            pltpu.VMEM((16, width), F32),
            pltpu.VMEM((16, 3 * width), F32),
            pltpu.VMEM((16, width), F32),
            pltpu.VMEM((4, cap, width), BF16),
            pltpu.VMEM((4, piece, width), BF16),
            pltpu.VMEM((4, piece, width), BF16),
            pltpu.VMEM((4, piece, width), BF16),
        ]
        + side(3 * half + width)
        + side(3 * half + quarter)
        + [
            pltpu.SemaphoreType.DMA((34,)),
            pltpu.SemaphoreType.DMA((34,)),
            pltpu.SemaphoreType.DMA((5,)),
        ],
        compiler_params=pltpu.CompilerParams(
            dimension_semantics=("arbitrary",),
            vmem_limit_bytes=62 * 1024 * 1024,
            collective_id=2,
            has_side_effects=True,
        ),
        cost_estimate=cost(2 * n * seq * width * width * 30, 40e6),
        name="backward_all",
    )(count, *[a for a, _ in streams], *fixed, *far_refs)


def weight_body(
    images, cotangent, image_count, routes, attn_norm_gain, attn_norm_bias, w_qkv, b_query,
    b_value, w_attn_out, b_attn_out, moe_norm_gain, moe_norm_bias, w_router, expert_in,
    expert_in_bias, expert_out, expert_out_bias,
):
    n, seq, width = images.shape
    sp = -(-seq // 16) * 16
    experts = lax.axis_size("expert")
    capacity = (2 * n * seq + experts - 1) // experts
    cap = -(-capacity // 16) * 16
    shard = lax.axis_index("wshard")
    place = lax.axis_index("expert")
    near = jnp.stack([(place - 2 * k) % 8 for k in range(4)])
    order = jnp.concatenate([near, near ^ 1])

    vectors = jnp.stack(
        [attn_norm_gain, attn_norm_bias, b_query, b_value, b_attn_out, moe_norm_gain, moe_norm_bias]
    )
    small = jnp.concatenate([jnp.pad(vectors, ((0, 1), (0, 0))), w_router.T[order]])
    e_bias = jnp.concatenate(
        [
            expert_in_bias,
            jnp.pad(expert_out_bias, ((0, 0), (0, width - expert_out_bias.shape[1]))),
            jnp.zeros((14, width), BF16),
        ]
    )

    live = jnp.arange(n, dtype=jnp.int32) < image_count[0]
    member = (routes[:, :, 0:1] == order) | (routes[:, :, 1:2] == order)
    member = (member & live[:, None, None]).astype(BF16)
    lower = jnp.tril(jnp.ones((seq, seq), BF16), -1)
    earlier = jnp.einsum("ts,ise->ite", lower, member, preferred_element_type=F32)
    counts = jnp.sum(member.astype(F32), axis=1)
    base = jnp.cumsum(counts, axis=0) - counts
    position = (earlier + base[:, None, :]).astype(jnp.int32)
    slots = jnp.where((member > 0) & (position < capacity), position, -1)
    slots = jnp.pad(slots, ((0, 0), (0, sp - seq), (0, 0)), constant_values=-1)
    slot_rows = slots.transpose(2, 0, 1).reshape(8, 1, n * sp)

    (
        joint, weights, mixed, attended, routed, probs,
        cots, pieces, w_qkv_full, w_out_full, rows_s, vec, router,
    ) = gather_forward(
        images, cotangent, slot_rows, w_qkv, w_attn_out, small, expert_in, expert_out, e_bias, sp, cap
    )
    grows, ggs, answers_l, answers_s, g_own, g_far, far_in = run_experts(
        slot_rows, routed.reshape(n * sp, width), router, cots, pieces, rows_s
    )
    output, grad_images, g_qkv, g_out, g_small, e_in, e_out, e_bias = backward_all(
        image_count, images, cotangent, joint, weights, mixed, attended, routed, probs, slots,
        w_qkv_full, w_out_full, vec, router, grows, ggs, answers_l, answers_s, g_own, g_far, far_in,
    )
    quarter = width // 4
    g_bias_out = lax.dynamic_slice_in_dim(e_bias[1:2], shard * quarter, quarter, 1)
    return (
        output,
        grad_images,
        g_small[0],
        g_small[1],
        g_qkv,
        g_small[2],
        g_small[3],
        g_out,
        g_small[4],
        g_small[5],
        g_small[6],
        g_small[8:16].T,
        e_in,
        e_bias[0:1],
        e_out,
        g_bias_out,
    )


def solution(mesh):
    in_specs = (
        P(("expert", "wshard"), None, None),
        P(("expert", "wshard"), None, None),
        P(("expert", "wshard")),
        P(("expert", "wshard"), None, None),
        P("wshard"),
        P("wshard"),
        P("wshard", None),
        P("wshard"),
        P("wshard"),
        P("wshard", None),
        P("wshard"),
        P("wshard"),
        P("wshard"),
        P("wshard", None),
        P("expert", None, "wshard"),
        P("expert", "wshard"),
        P("expert", "wshard", None),
        P("expert", "wshard"),
    )
    out_specs = (
        P(("expert", "wshard"), None, None),
        P(("expert", "wshard"), None, None),
        P("wshard"),
        P("wshard"),
        P("wshard", None),
        P("wshard"),
        P("wshard"),
        P("wshard", None),
        P("wshard"),
        P("wshard"),
        P("wshard"),
        P("wshard", None),
        P("expert", None, "wshard"),
        P("expert", "wshard"),
        P("expert", "wshard", None),
        P("expert", "wshard"),
    )
    small_slice = mesh.shape["expert"] == 8 and mesh.shape["wshard"] == 4
    body = weight_body if small_slice else token_body
    return jax.shard_map(body, mesh=mesh, in_specs=in_specs, out_specs=out_specs, check_vma=False)
```
